32 devices in a mesh: section: 4 (over x, core), seq: 8 (over z, y).
Axes of the slice: x: 2, y: 2, z: 4, core: 2. Of those that a mesh axis runs over, the one named last changes fastest.
Arguments:
- queries: bfloat16 [4, 2560, 1024], P('section', 'seq'), may hold values from -60 to 60
- keys_new: bfloat16 [4, 2560, 1024], P('section', 'seq'), may hold values from -6 to 6
- values_new: bfloat16 [4, 2560, 1024], P('section', 'seq'), may hold values from -6 to 6
- keys_cache: bfloat16 [4, 6144, 1024], P('section', None, 'seq'), may hold values from -6 to 6
- values_cache: bfloat16 [4, 6144, 1024], P('section', None, 'seq'), may hold values from -6 to 6
- window: int32 [4, 8], P('section', 'seq'), may hold values from 1 to 3, as said below
- global_blocks: int32 [4, 2], P('section'), may hold values from 0 to 95
- random_blocks: int32 [4, 40, 3], P('section'), may hold values from 0 to 95
Outputs:
- handed: bfloat16 [4, 2560, 1024], P('section', 'seq')
The draws below stay inside these ranges and needn't reach their ends.
Inputs may be any that keep to these rules, and one draw needn't show every extreme that they name: In every section some head has the window 3.
All inputs are finite; a program needn't handle non-finite values.
Results may differ from the reference program's by a relative error of at most 0.0049.
Values may be sent and summed in bfloat16 or wider, within the bound.
No kernel may reach another device: no remote copies, remote signals or barrier semaphores. Data moves between devices by JAX's collectives and lax.ppermute only.
A program may use at most 128 MiB of HBM per device.

```python
import math
import jax
import jax.numpy as jnp
from jax import lax

HD = 128
HEADS = 8
WIDE = 1024
BLK = 64
WMAX = 3
GLOB = 2
RAND = 3
NK = 8
CTXB = 96
SECTIONS = 4
STRETCH = 2560
QBLK = 40
CTX = 6144


def aligned_pair(key):
    base = jax.random.fold_in(key, 7)
    shape = (SECTIONS, STRETCH, WIDE)
    keys = jnp.clip(jax.random.normal(jax.random.fold_in(base, 1), shape, jnp.float32), -6.0, 6.0)
    queries = jnp.clip(jax.random.normal(jax.random.fold_in(base, 2), shape, jnp.float32), -6.0, 6.0)
    token_at = jnp.arange(STRETCH)[None, :, None]
    column_at = jnp.arange(WIDE)[None, None, :]
    upper_end = (token_at == 0) & (column_at == 0)
    lower_end = (token_at == 1) & (column_at == 0)
    queries = jnp.where(upper_end, 60.0, jnp.where(lower_end, -60.0, queries))
    keys = jnp.where(upper_end, 6.0, jnp.where(lower_end, -6.0, keys))
    return (queries, keys)


def draw_queries(key, part):
    return aligned_pair(key)[0].astype(jnp.bfloat16)


def draw_keys_new(key, part):
    return aligned_pair(key)[1].astype(jnp.bfloat16)


def draw_window(key, part):
    spans = jax.random.randint(jax.random.fold_in(key, 3), (SECTIONS, HEADS), 1, WMAX + 1)
    chosen = jax.random.randint(jax.random.fold_in(key, 4), (SECTIONS, 1), 0, HEADS)
    return jnp.where(jnp.arange(HEADS)[None, :] == chosen, WMAX, spans).astype(jnp.int32)


def place_ends(entries, stream_key, least, high):
    extent = entries.shape
    place = [jax.random.randint(jax.random.fold_in(stream_key, axis), (), 0, extent[axis]) for axis in range(len(extent))]
    entries = entries.at[tuple(place)].set(least)
    longest = extent.index(max(extent))
    place[longest] = (place[longest] + 1) % extent[longest]
    return entries.at[tuple(place)].set(high)


def levels(stream_key, shape, split, smallest, largest):
    gain = 1.0
    for axis_at, parts in split:
        draws = jax.random.uniform(jax.random.fold_in(jax.random.fold_in(stream_key, 6), axis_at), (parts,), jnp.float32, smallest / len(split), largest / len(split))
        gain = gain * jnp.repeat(jnp.exp(draws), shape[axis_at] // parts).reshape((-1,) + (1,) * (len(shape) - 1 - axis_at))
    return gain


def bell_draw(rng, shape, width, reach, cuts=(), held_as=jnp.bfloat16):
    factor_of = levels(rng, shape, cuts, -0.22, 0.18) if cuts else 1.0
    drawn = jax.random.normal(rng, shape, jnp.float32) * width * factor_of
    return jnp.minimum(jnp.maximum(drawn, -reach), reach).astype(held_as)


def setup_inputs(seed: int = 0) -> dict:
    splits = jax.random.split(jax.random.key(seed), 9)
    queries = draw_queries(jax.random.fold_in(splits[8], 71), 0)
    keys_new = draw_keys_new(jax.random.fold_in(splits[8], 71), 0)
    values_new = bell_draw(splits[2], (SECTIONS, STRETCH, WIDE), 1.0, 6.0, ((0, 4), (1, 8)))
    keys_cache = bell_draw(splits[3], (SECTIONS, CTX, WIDE), 1.0, 6.0, ((0, 4), (2, 8)))
    values_cache = bell_draw(splits[4], (SECTIONS, CTX, WIDE), 1.0, 6.0, ((0, 4), (2, 8)))
    window = draw_window(jax.random.fold_in(splits[8], 71), 0)
    global_blocks = place_ends(jax.random.randint(splits[6], (SECTIONS, GLOB), 0, CTXB), jax.random.fold_in(splits[6], 1), 0, CTXB - 1).astype(jnp.int32)
    random_blocks = place_ends(jax.random.randint(splits[7], (SECTIONS, QBLK, RAND), 0, CTXB), jax.random.fold_in(splits[7], 1), 0, CTXB - 1).astype(jnp.int32)
    return dict(queries=queries, keys_new=keys_new, values_new=values_new, keys_cache=keys_cache, values_cache=values_cache, window=window, global_blocks=global_blocks, random_blocks=random_blocks)


masked_score = -1e+30

def block_mask(span_blocks):
    rows = jnp.arange(BLK, dtype=jnp.int32)[:, None]
    column = jnp.arange(NK * BLK, dtype=jnp.int32)[None, :]
    which = column // BLK
    inside = column % BLK
    allowed = jnp.where(which >= WMAX, True, which < span_blocks)
    return allowed & ((which != 0) | (inside <= rows))

def attend_head(query, key_all, value_all, span_blocks, table):
    query_blocks = query.reshape(QBLK, BLK, HD).astype(jnp.float32)
    key_blocks = key_all.reshape(CTXB + QBLK, BLK, HD)
    value_blocks = value_all.reshape(CTXB + QBLK, BLK, HD)
    picked_keys = key_blocks[table].reshape(QBLK, NK * BLK, HD).astype(jnp.float32)
    picked_values = value_blocks[table].reshape(QBLK, NK * BLK, HD).astype(jnp.float32)
    scores = jnp.einsum('qih,qjh->qij', query_blocks, picked_keys) * (1.0 / math.sqrt(HD))
    scores = jnp.where(block_mask(span_blocks)[None], scores, masked_score)
    top = lax.optimization_barrier(jnp.max(scores, axis=-1, keepdims=True))
    expo = jnp.exp(scores - top)
    weights = (expo / lax.optimization_barrier(jnp.sum(expo, axis=-1, keepdims=True))).astype(jnp.bfloat16)
    result = jnp.einsum('qij,qjh->qih', weights.astype(jnp.float32), picked_values)
    return result.astype(jnp.bfloat16).reshape(STRETCH, HD)

def reference(queries, keys_new, values_new, keys_cache, values_cache, window, global_blocks, random_blocks):
    zero = jnp.int32(0)

    def one_item(item):
        section_at = item // HEADS
        head_at = item % HEADS
        column = head_at * HD
        query = lax.dynamic_slice(queries, (section_at, zero, column), (1, STRETCH, HD))[0]
        fresh_keys = lax.dynamic_slice(keys_new, (section_at, zero, column), (1, STRETCH, HD))[0]
        fresh_values = lax.dynamic_slice(values_new, (section_at, zero, column), (1, STRETCH, HD))[0]
        old_keys = lax.dynamic_slice(keys_cache, (section_at, zero, column), (1, CTX, HD))[0]
        old_values = lax.dynamic_slice(values_cache, (section_at, zero, column), (1, CTX, HD))[0]
        key_all = jnp.concatenate([old_keys, fresh_keys], axis=0)
        value_all = jnp.concatenate([old_values, fresh_values], axis=0)
        span_blocks = lax.dynamic_slice(window, (section_at, head_at), (1, 1))[0, 0]
        global_row = lax.dynamic_slice(global_blocks, (section_at, zero), (1, GLOB))[0]
        random_rows = lax.dynamic_slice(random_blocks, (section_at, zero, zero), (1, QBLK, RAND))[0]
        starts = CTXB + jnp.arange(QBLK, dtype=jnp.int32)[:, None] - jnp.arange(WMAX, dtype=jnp.int32)[None, :]
        spread = jnp.broadcast_to(global_row[None, :], (QBLK, GLOB)).astype(jnp.int32)
        table = jnp.concatenate([starts, spread, random_rows.astype(jnp.int32)], axis=1)
        return attend_head(query, key_all, value_all, span_blocks, table)
    outputs = lax.map(one_item, jnp.arange(SECTIONS * HEADS, dtype=jnp.int32))
    outputs = outputs.reshape(SECTIONS, HEADS, STRETCH, HD).transpose(0, 2, 1, 3).reshape(SECTIONS, STRETCH, WIDE)
    return jnp.roll(outputs, 1, axis=0)
```

```python
import functools
import math

import jax
import jax.numpy as jnp
from jax import lax
from jax.experimental import pallas as pl
from jax.experimental.pallas import tpu as pltpu
from jax.sharding import PartitionSpec as P

HD = 128
BLK = 64
WMAX = 3
GLOB = 2
RAND = 3
LANES = 128
STAT_ROWS = 16
MASKED = -1e30
EXPO_SCALE = math.log2(math.e) / math.sqrt(HD)
VMEM_LIMIT = 56 * 1024 * 1024
CHUNKS_PER_CALL = 8

whole_vmem = pl.BlockSpec(memory_space=pltpu.VMEM)
whole_smem = pl.BlockSpec(memory_space=pltpu.SMEM)


def partner(me, step):
    return jnp.bitwise_xor(me, step)


def scores_of(query, keys):
    return lax.dot_general(
        query, keys, (((1,), (1,)), ((), ())), preferred_element_type=jnp.float32
    )


def softmax_part(pieces, values):
    top = functools.reduce(
        jnp.maximum, [jnp.max(piece, axis=1, keepdims=True) for piece in pieces]
    )
    expo = [jnp.exp2((piece - top) * EXPO_SCALE) for piece in pieces]
    total = functools.reduce(jnp.add, [jnp.sum(part, axis=1, keepdims=True) for part in expo])
    mixed = functools.reduce(
        jnp.add,
        [
            jnp.dot(part.astype(jnp.bfloat16), value, preferred_element_type=jnp.float32)
            for part, value in zip(expo, values)
        ],
    )
    return mixed / total, top * EXPO_SCALE + jnp.log2(total)


def as_row(column, offset):
    shape = (column.shape[0], LANES)
    row_at = lax.broadcasted_iota(jnp.int32, shape, 0)
    lane_at = lax.broadcasted_iota(jnp.int32, shape, 1)
    spread = jnp.where(lane_at == row_at + offset, column, 0.0)
    return jnp.sum(spread, axis=0, keepdims=True)


def stat_tile(rows):
    at = lax.broadcasted_iota(jnp.int32, (STAT_ROWS, LANES), 0)
    tile = jnp.zeros((STAT_ROWS, LANES), jnp.float32)
    count = len(rows)
    for index, row in enumerate(rows):
        high = row.astype(jnp.bfloat16).astype(jnp.float32)
        middle = (row - high).astype(jnp.bfloat16).astype(jnp.float32)
        low = row - high - middle
        for part, value in enumerate((high, middle, low)):
            tile = jnp.where(at == part * count + index, value, tile)
    return tile.astype(jnp.bfloat16)


def stat_rows_of(tile, count):
    wide = tile.astype(jnp.float32)
    return [
        wide[index : index + 1]
        + wide[count + index : count + index + 1]
        + wide[2 * count + index : 2 * count + index + 1]
        for index in range(count)
    ]


def stat_count(rows):
    return -(-rows // LANES)


def split_kernel(steps, me_ref, query_ref, key_ref, value_ref, *out_refs):
    me = me_ref[0]
    rows = query_ref.shape[0]
    halo = (WMAX - 1) * BLK
    out_refs[0][0] = key_ref[rows - halo :, :]
    out_refs[0][1] = value_ref[rows - halo :, :]
    for step in range(steps):
        head = pl.multiple_of(partner(me, step) * HD, HD)
        out_refs[1 + step][...] = query_ref[:, pl.ds(head, HD)]


def far_kernel(
    steps, me_ref, span_ref, global_ref, random_ref, key_ref, value_ref, *refs
):
    me = me_ref[0]
    span = span_ref[0]
    count = len(steps)
    query_refs, out_refs = refs[:count], refs[count:]
    last = key_ref.shape[0] // BLK - 1

    def block(ref, at):
        if isinstance(at, int):
            return ref[at * BLK : (at + 1) * BLK, :]
        return ref[pl.ds(pl.multiple_of(at * BLK, BLK), BLK), :]

    glob_keys = [block(key_ref, global_ref[g]) for g in range(GLOB)]
    glob_values = [block(value_ref, global_ref[g]) for g in range(GLOB)]
    for index, step in enumerate(steps):
        chunk = partner(me, step)
        query_ref, out_ref = query_refs[index], out_refs[index]
        rows = query_ref.shape[0]
        blocks = rows // BLK
        first = chunk == 0
        stats = []
        for b in range(blocks):
            query = query_ref[b * BLK : (b + 1) * BLK, :]
            base = (chunk * blocks + b) * RAND
            picks = [random_ref[base + r] for r in range(RAND)]
            keys = glob_keys + [block(key_ref, pick) for pick in picks]
            values = glob_values + [block(value_ref, pick) for pick in picks]
            known = len(keys) * BLK
            spare = [last + 1 + b - w for w in range(b + 1, WMAX)]
            keys = keys + [block(key_ref, at) for at in spare]
            values = values + [block(value_ref, at) for at in spare]
            scores = scores_of(query, jnp.concatenate(keys, axis=0))
            if spare:
                open_slots = jnp.where(first, jnp.clip(span - (b + 1), 0, len(spare)), 0)
                lane_at = lax.broadcasted_iota(jnp.int32, scores.shape, 1)
                scores = jnp.where(lane_at < known + open_slots * BLK, scores, MASKED)
            mixed, lse = softmax_part([scores], [jnp.concatenate(values, axis=0)])
            out_ref[b * BLK : (b + 1) * BLK, :] = mixed.astype(jnp.bfloat16)
            row = as_row(lse, (b * BLK) % LANES)
            if (b * BLK) % LANES:
                stats[-1] = stats[-1] + row
            else:
                stats.append(row)
        out_ref[rows:, :] = stat_tile(stats)


def near_kernel(
    me_ref, spans_ref, query_ref, key_ref, value_ref, halo_ref, out_ref
):
    me = me_ref[0]
    rows = query_ref.shape[0]
    heads = query_ref.shape[1] // HD
    halo = (WMAX - 1) * BLK

    def one_head(head, carry):
        lanes = pl.ds(pl.multiple_of(head * HD, HD), HD)
        span = spans_ref[head]
        stats = []
        for start in range(0, rows, 2 * BLK):
            size = min(2 * BLK, rows - start)
            query = query_ref[start : start + size, lanes]
            if start < halo:
                keys = [halo_ref[0, start:, lanes], key_ref[: start + size, lanes]]
                values = [halo_ref[1, start:, lanes], value_ref[: start + size, lanes]]
                keys, values = jnp.concatenate(keys, axis=0), jnp.concatenate(values, axis=0)
            else:
                keys = key_ref[start - halo : start + size, lanes]
                values = value_ref[start - halo : start + size, lanes]
            scores = scores_of(query, keys)
            row_at = lax.broadcasted_iota(jnp.int32, scores.shape, 0)
            lane_at = lax.broadcasted_iota(jnp.int32, scores.shape, 1)
            allowed = (lane_at <= row_at + halo) & (
                lane_at // BLK - row_at // BLK > WMAX - 1 - span
            )
            if start < halo:
                closed = jnp.where(me == 0, halo - start, 0)
                allowed = allowed & (lane_at >= closed)
            mixed, lse = softmax_part([jnp.where(allowed, scores, MASKED)], [values])
            out_ref[start : start + size, lanes] = mixed.astype(jnp.bfloat16)
            stats.append(as_row(lse, 0))
        out_ref[rows:, lanes] = stat_tile(stats)
        return carry

    lax.fori_loop(0, heads, one_head, 0)


def merge_kernel(steps, me_ref, near_ref, *refs):
    me = me_ref[0]
    far_refs, out_ref = refs[:-1], refs[-1]
    rows = out_ref.shape[0]
    count = stat_count(rows)
    for step in range(steps):
        far_ref = far_refs[step]
        lanes = pl.ds(pl.multiple_of(partner(me, step) * HD, HD), HD)
        far_stats = stat_rows_of(far_ref[rows:, :], count)
        near_stats = stat_rows_of(near_ref[rows:, lanes], count)
        for index in range(count):
            start = index * LANES
            size = min(LANES, rows - start)
            share = 1.0 / (1.0 + jnp.exp2(near_stats[index] - far_stats[index]))
            row_at = lax.broadcasted_iota(jnp.int32, (size, LANES), 0)
            lane_at = lax.broadcasted_iota(jnp.int32, (size, LANES), 1)
            column = jnp.sum(
                jnp.where(row_at == lane_at, share, 0.0), axis=1, keepdims=True
            )
            far = far_ref[start : start + size, :].astype(jnp.float32)
            near = near_ref[start : start + size, lanes].astype(jnp.float32)
            out_ref[start : start + size, lanes] = (
                far * column + near * (1.0 - column)
            ).astype(jnp.bfloat16)


def params():
    return pltpu.CompilerParams(vmem_limit_bytes=VMEM_LIMIT)


def per_device(
    queries, keys_new, values_new, keys_cache, values_cache, window, global_blocks, random_blocks
):
    section_count = lax.axis_size("section")
    seq_count = lax.axis_size("seq")
    rows, wide = queries.shape[1], queries.shape[2]
    halo = (WMAX - 1) * BLK
    heads = wide // HD
    bf16 = jnp.bfloat16
    me = lax.axis_index("seq").astype(jnp.int32)[None]
    spans = lax.all_gather(window[0], "seq", axis=0, tiled=True)

    parts = pl.pallas_call(
        functools.partial(split_kernel, seq_count),
        out_shape=[jax.ShapeDtypeStruct((2, halo, wide), bf16)]
        + [jax.ShapeDtypeStruct((rows, HD), bf16)] * seq_count,
        in_specs=[whole_smem] + [whole_vmem] * 3,
        out_specs=[whole_vmem] * (1 + seq_count),
        compiler_params=params(),
        cost_estimate=pl.CostEstimate(flops=0, bytes_accessed=5 * rows * wide, transcendentals=0),
        name="split",
    )(me, queries[0], keys_new[0], values_new[0])
    mine, sent = parts[0], parts[1:]

    def swapped(shard, step):
        if step == 0:
            return shard
        return lax.ppermute(shard, "seq", [(i, i ^ step) for i in range(seq_count)])

    order = sorted(range(seq_count), reverse=True)
    came = {step: swapped(sent[step], step) for step in order}
    before = lax.ppermute(mine, "seq", [(i, i + 1) for i in range(seq_count - 1)])

    picks = random_blocks[0].reshape(-1)

    def far_call(steps):
        count = len(steps)
        return pl.pallas_call(
            functools.partial(far_kernel, steps),
            out_shape=[jax.ShapeDtypeStruct((rows + STAT_ROWS, HD), bf16)] * count,
            in_specs=[whole_smem] * 4 + [whole_vmem] * (2 + count),
            out_specs=[whole_vmem] * count,
            compiler_params=params(),
            cost_estimate=pl.CostEstimate(
                flops=count * rows * 320 * HD * 4,
                bytes_accessed=2 * 2 * keys_cache.shape[1] * HD + 4 * count * rows * HD,
                transcendentals=count * rows * 320,
            ),
            name="far",
        )(
            me,
            window[0],
            global_blocks[0],
            picks,
            keys_cache[0],
            values_cache[0],
            *[came[step] for step in steps],
        )

    far = {}
    for begin in range(0, seq_count, CHUNKS_PER_CALL):
        steps = order[begin : begin + CHUNKS_PER_CALL]
        far.update(zip(steps, far_call(steps)))

    def onward(shard, step):
        pairs = [
            (s * seq_count + t, ((s + 1) % section_count) * seq_count + (t ^ step))
            for s in range(section_count)
            for t in range(seq_count)
        ]
        return lax.ppermute(shard, ("section", "seq"), pairs)

    handed_far = {step: onward(far[step], step) for step in order}

    near = pl.pallas_call(
        near_kernel,
        out_shape=jax.ShapeDtypeStruct((rows + STAT_ROWS, wide), bf16),
        in_specs=[whole_smem] * 2 + [whole_vmem] * 4,
        out_specs=whole_vmem,
        compiler_params=params(),
        cost_estimate=pl.CostEstimate(
            flops=heads * rows * 256 * HD * 4,
            bytes_accessed=9 * rows * wide,
            transcendentals=heads * rows * 256,
        ),
        name="near",
    )(me, spans, queries[0], keys_new[0], values_new[0], before)
    handed_near = lax.ppermute(
        near, "section", [(s, (s + 1) % section_count) for s in range(section_count)]
    )

    merged = pl.pallas_call(
        functools.partial(merge_kernel, seq_count),
        out_shape=jax.ShapeDtypeStruct((rows, wide), bf16),
        in_specs=[whole_smem] + [whole_vmem] * (1 + seq_count),
        out_specs=whole_vmem,
        compiler_params=params(),
        cost_estimate=pl.CostEstimate(flops=0, bytes_accessed=6 * rows * wide, transcendentals=0),
        name="merge",
    )(me, handed_near, *[handed_far[step] for step in range(seq_count)])
    return merged[None]


def solution(mesh):
    placed = (
        P("section", "seq", None),
        P("section", "seq", None),
        P("section", "seq", None),
        P("section", None, "seq"),
        P("section", None, "seq"),
        P("section", "seq"),
        P("section", None),
        P("section", None, None),
    )
    return jax.shard_map(
        per_device, mesh=mesh, in_specs=placed, out_specs=P("section", "seq", None), check_vma=False
    )
```

```python
import functools
import math

import jax
import jax.numpy as jnp
from jax import lax
from jax.experimental import pallas as pl
from jax.experimental.pallas import tpu as pltpu
from jax.sharding import PartitionSpec as P

HD = 128
BLK = 64
WMAX = 3
GLOB = 2
RAND = 3
LANES = 128
STAT_ROWS = 16
MASKED = -1e30
EXPO_SCALE = math.log2(math.e) / math.sqrt(HD)
VMEM_BASE = 12 * 1024 * 1024

whole_vmem = pl.BlockSpec(memory_space=pltpu.VMEM)
anywhere = pl.BlockSpec(memory_space=pl.ANY)
whole_smem = pl.BlockSpec(memory_space=pltpu.SMEM)


def partner(me, step):
    return jnp.bitwise_xor(me, step)


def scores_of(query, keys):
    return lax.dot_general(
        query, keys, (((1,), (1,)), ((), ())), preferred_element_type=jnp.float32
    )


def softmax_parts(scores, values):
    tops = [jnp.max(score, axis=1, keepdims=True) for score in scores]
    expos = [jnp.exp2((score - top) * EXPO_SCALE) for score, top in zip(scores, tops)]
    totals = [jnp.sum(expo, axis=1, keepdims=True) for expo in expos]
    mixed = [
        jnp.dot(expo.astype(jnp.bfloat16), value, preferred_element_type=jnp.float32)
        for expo, value in zip(expos, values)
    ]
    parts = [(mix * (1.0 / total)).astype(jnp.bfloat16) for mix, total in zip(mixed, totals)]
    lses = [top * EXPO_SCALE + jnp.log2(total) for top, total in zip(tops, totals)]
    return parts, lses


def as_row(column, offset):
    shape = (column.shape[0], LANES)
    row_at = lax.broadcasted_iota(jnp.int32, shape, 0)
    lane_at = lax.broadcasted_iota(jnp.int32, shape, 1)
    spread = jnp.where(lane_at == row_at + offset, column, 0.0)
    return jnp.sum(spread, axis=0, keepdims=True)


def stat_tile(rows):
    at = lax.broadcasted_iota(jnp.int32, (STAT_ROWS, LANES), 0)
    tile = jnp.zeros((STAT_ROWS, LANES), jnp.float32)
    count = len(rows)
    for index, row in enumerate(rows):
        high = row.astype(jnp.bfloat16).astype(jnp.float32)
        middle = (row - high).astype(jnp.bfloat16).astype(jnp.float32)
        low = row - high - middle
        for part, value in enumerate((high, middle, low)):
            tile = jnp.where(at == part * count + index, value, tile)
    return tile.astype(jnp.bfloat16)


def stat_rows_of(tile, count):
    wide = tile.astype(jnp.float32)
    return [
        wide[index : index + 1]
        + wide[count + index : count + index + 1]
        + wide[2 * count + index : 2 * count + index + 1]
        for index in range(count)
    ]


def stat_count(rows):
    return -(-rows // LANES)


def split_kernel(steps, me_ref, query_ref, key_ref, value_ref, *out_refs):
    me = me_ref[0]
    rows = query_ref.shape[0]
    halo = (WMAX - 1) * BLK
    out_refs[0][0] = key_ref[rows - halo :, :]
    out_refs[0][1] = value_ref[rows - halo :, :]
    for step in range(steps):
        head = pl.multiple_of(partner(me, step) * HD, HD)
        out_refs[1 + step][...] = query_ref[:, pl.ds(head, HD)]


def far_kernel(
    steps, me_ref, span_ref, global_ref, random_ref, key_ref, value_ref, *refs
):
    me = me_ref[0]
    span = span_ref[0]
    count = len(steps)
    query_refs, out_refs = refs[:count], refs[-count:]
    last = key_ref.shape[0] // BLK - 1

    def block(ref, at):
        if isinstance(at, int):
            return ref[at * BLK : (at + 1) * BLK, :]
        return ref[pl.ds(pl.multiple_of(at * BLK, BLK), BLK), :]

    glob_keys = [block(key_ref, global_ref[g]) for g in range(GLOB)]
    glob_values = [block(value_ref, global_ref[g]) for g in range(GLOB)]
    for index, step in enumerate(steps):
        chunk = partner(me, step)
        query_ref, out_ref = query_refs[index], out_refs[index]
        if step == 0:
            near_ref = refs[count]
            wide = near_ref.shape[1]
            out_ref[:, :wide] = near_ref[...]
        else:
            wide = 0
        rows = query_ref.shape[0]
        blocks = rows // BLK
        first = chunk == 0
        all_scores, all_values = [], []
        for b in range(blocks):
            query = query_ref[b * BLK : (b + 1) * BLK, :]
            base = (chunk * blocks + b) * RAND
            picks = [random_ref[base + r] for r in range(RAND)]
            keys = glob_keys + [block(key_ref, pick) for pick in picks]
            values = glob_values + [block(value_ref, pick) for pick in picks]
            known = len(keys) * BLK
            spare = [last + 1 + b - w for w in range(b + 1, WMAX)]
            keys = keys + [block(key_ref, at) for at in spare]
            values = values + [block(value_ref, at) for at in spare]
            scores = scores_of(query, jnp.concatenate(keys, axis=0))
            if spare:
                open_slots = jnp.where(first, jnp.clip(span - (b + 1), 0, len(spare)), 0)
                lane_at = lax.broadcasted_iota(jnp.int32, scores.shape, 1)
                scores = jnp.where(lane_at < known + open_slots * BLK, scores, MASKED)
            all_scores.append(scores)
            all_values.append(jnp.concatenate(values, axis=0))
        parts, lses = softmax_parts(all_scores, all_values)
        stats = []
        for b in range(blocks):
            row = as_row(lses[b], (b * BLK) % LANES)
            if (b * BLK) % LANES:
                stats[-1] = stats[-1] + row
            else:
                stats.append(row)
        tile = stat_tile(stats)
        for b in range(blocks):
            out_ref[b * BLK : (b + 1) * BLK, wide:] = parts[b]
        out_ref[rows:, wide:] = tile


def near_kernel(
    me_ref, spans_ref, query_ref, key_ref, value_ref, halo_ref, out_ref
):
    me = me_ref[0]
    rows = query_ref.shape[0]
    heads = query_ref.shape[1] // HD
    halo = (WMAX - 1) * BLK

    def one_head(head, carry):
        lanes = pl.ds(pl.multiple_of(head * HD, HD), HD)
        span = spans_ref[head, 0]
        all_scores, all_values = [], []
        starts = list(range(0, rows, 2 * BLK))
        sizes = [min(2 * BLK, rows - start) for start in starts]
        for start, size in zip(starts, sizes):
            query = query_ref[start : start + size, lanes]
            if start < halo:
                keys = [halo_ref[0, start:, lanes], key_ref[: start + size, lanes]]
                values = [halo_ref[1, start:, lanes], value_ref[: start + size, lanes]]
                keys, values = jnp.concatenate(keys, axis=0), jnp.concatenate(values, axis=0)
            else:
                keys = key_ref[start - halo : start + size, lanes]
                values = value_ref[start - halo : start + size, lanes]
            scores = scores_of(query, keys)
            row_at = lax.broadcasted_iota(jnp.int32, scores.shape, 0)
            lane_at = lax.broadcasted_iota(jnp.int32, scores.shape, 1)
            allowed = (lane_at <= row_at + halo) & (
                lane_at // BLK - row_at // BLK > WMAX - 1 - span
            )
            if start < halo:
                closed = jnp.where(me == 0, halo - start, 0)
                allowed = allowed & (lane_at >= closed)
            all_scores.append(jnp.where(allowed, scores, MASKED))
            all_values.append(values)
        parts, lses = softmax_parts(all_scores, all_values)
        tile = stat_tile([as_row(lse, 0) for lse in lses])
        for start, size, part in zip(starts, sizes, parts):
            out_ref[start : start + size, lanes] = part
        out_ref[rows:, lanes] = tile
        return carry

    lax.fori_loop(0, heads, one_head, 0)


def merge_kernel(steps, me_ref, *refs):
    me = me_ref[0]
    far_refs, out_ref = refs[:-1], refs[-1]
    near_ref = far_refs[steps.index(0)]
    rows, wide = out_ref.shape
    count = stat_count(rows)
    for step, far_ref in zip(steps, far_refs):
        part = slice(wide, None) if step == 0 else slice(None)
        lanes = pl.ds(pl.multiple_of(partner(me, step) * HD, HD), HD)
        far_stats = stat_rows_of(far_ref[rows:, part], count)
        near_stats = stat_rows_of(near_ref[rows:, lanes], count)
        for index in range(count):
            start = index * LANES
            size = min(LANES, rows - start)
            share = 1.0 / (1.0 + jnp.exp2(near_stats[index] - far_stats[index]))
            row_at = lax.broadcasted_iota(jnp.int32, (size, LANES), 0)
            lane_at = lax.broadcasted_iota(jnp.int32, (size, LANES), 1)
            column = jnp.sum(
                jnp.where(row_at == lane_at, share, 0.0), axis=1, keepdims=True
            )
            far = far_ref[start : start + size, part].astype(jnp.float32)
            near = near_ref[start : start + size, lanes].astype(jnp.float32)
            out_ref[start : start + size, lanes] = (
                far * column + near * (1.0 - column)
            ).astype(jnp.bfloat16)


def params(shard):
    return pltpu.CompilerParams(vmem_limit_bytes=VMEM_BASE + 14 * 2 * math.prod(shard.shape))


def per_device(
    queries, keys_new, values_new, keys_cache, values_cache, window, global_blocks, random_blocks
):
    section_count = lax.axis_size("section")
    seq_count = lax.axis_size("seq")
    rows, wide = queries.shape[1], queries.shape[2]
    halo = (WMAX - 1) * BLK
    heads = wide // HD
    bf16 = jnp.bfloat16
    me = lax.axis_index("seq").astype(jnp.int32)[None]
    spans = lax.all_gather(
        lax.optimization_barrier(jnp.broadcast_to(window, (8, LANES))), "seq", axis=0, tiled=True
    )

    parts = pl.pallas_call(
        functools.partial(split_kernel, seq_count),
        out_shape=[jax.ShapeDtypeStruct((2, halo, wide), bf16)]
        + [jax.ShapeDtypeStruct((rows, HD), bf16)] * seq_count,
        in_specs=[whole_smem] + [whole_vmem] * 3,
        out_specs=[whole_vmem] * (1 + seq_count),
        compiler_params=params(queries),
        cost_estimate=pl.CostEstimate(flops=0, bytes_accessed=5 * rows * wide, transcendentals=0),
        name="split",
    )(me, queries[0], keys_new[0], values_new[0])
    mine, sent = parts[0], parts[1:]

    def swapped(shard, step):
        if step == 0:
            return shard
        return lax.ppermute(shard, "seq", [(i, i ^ step) for i in range(seq_count)])

    half = max(seq_count // 2, 1)
    order = list(range(seq_count - 1, half - 1, -1)) + list(range(half))
    came = {step: swapped(sent[step], step) for step in order}
    before = lax.ppermute(mine, "seq", [(i, i + 1) for i in range(seq_count - 1)])

    near = pl.pallas_call(
        near_kernel,
        out_shape=jax.ShapeDtypeStruct((rows + STAT_ROWS, wide), bf16),
        in_specs=[whole_smem] * 2 + [whole_vmem] * 4,
        out_specs=whole_vmem,
        compiler_params=params(queries),
        cost_estimate=pl.CostEstimate(
            flops=heads * rows * 256 * HD * 4,
            bytes_accessed=9 * rows * wide,
            transcendentals=heads * rows * 256,
        ),
        name="near",
    )(me, spans[::8], queries[0], keys_new[0], values_new[0], before)
    picks = random_blocks[0].reshape(-1)

    def far_call(steps):
        count = len(steps)
        out_rows = rows + STAT_ROWS
        widths = [HD] * count
        widths[steps.index(0)] += wide
        return pl.pallas_call(
            functools.partial(far_kernel, steps),
            out_shape=[jax.ShapeDtypeStruct((out_rows, width), bf16) for width in widths],
            in_specs=[whole_smem] * 4 + [whole_vmem] * (2 + count + 1),
            out_specs=[whole_vmem] * count,
            compiler_params=params(queries),
            cost_estimate=pl.CostEstimate(
                flops=count * rows * 320 * HD * 4,
                bytes_accessed=2 * 2 * keys_cache.shape[1] * HD + 4 * count * rows * HD,
                transcendentals=count * rows * 320,
            ),
            name="far",
        )(
            me,
            window[0],
            global_blocks[0],
            picks,
            keys_cache[0],
            values_cache[0],
            *[came[step] for step in steps],
            near,
        )

    far = dict(zip(order, far_call(order)))

    def onward(shard, step):
        pairs = [
            (s * seq_count + t, ((s + 1) % section_count) * seq_count + (t ^ step))
            for s in range(section_count)
            for t in range(seq_count)
        ]
        return lax.ppermute(shard, ("section", "seq"), pairs)

    handed = {step: onward(far[step], step) for step in order}

    merged = pl.pallas_call(
        functools.partial(merge_kernel, order),
        out_shape=jax.ShapeDtypeStruct((rows, wide), bf16),
        in_specs=[whole_smem] + [whole_vmem] * seq_count,
        out_specs=whole_vmem,
        compiler_params=params(queries),
        cost_estimate=pl.CostEstimate(flops=0, bytes_accessed=6 * rows * wide, transcendentals=0),
        name="merge",
    )(me, *[handed[step] for step in order])
    return merged[None]


def solution(mesh):
    placed = (
        P("section", "seq", None),
        P("section", "seq", None),
        P("section", "seq", None),
        P("section", None, "seq"),
        P("section", None, "seq"),
        P("section", "seq"),
        P("section", None),
        P("section", None, None),
    )
    return jax.shard_map(
        per_device, mesh=mesh, in_specs=placed, out_specs=P("section", "seq", None), check_vma=False
    )
```

```python
import functools
import math

import jax
import jax.numpy as jnp
from jax import lax
from jax.experimental import pallas as pl
from jax.experimental.pallas import tpu as pltpu
from jax.sharding import PartitionSpec as P

HD = 128
BLK = 64
WMAX = 3
GLOB = 2
RAND = 3
LANES = 128
STAT_ROWS = 16
MASKED = -1e30
EXPO_SCALE = math.log2(math.e) / math.sqrt(HD)
VMEM_BASE = 12 * 1024 * 1024

whole_vmem = pl.BlockSpec(memory_space=pltpu.VMEM)
anywhere = pl.BlockSpec(memory_space=pl.ANY)
whole_smem = pl.BlockSpec(memory_space=pltpu.SMEM)


def partner(me, step):
    return jnp.bitwise_xor(me, step)


def scores_of(query, keys):
    return lax.dot_general(
        query, keys, (((1,), (1,)), ((), ())), preferred_element_type=jnp.float32
    )


def softmax_parts(scores, values):
    tops = [jnp.max(score, axis=1, keepdims=True) for score in scores]
    expos = [jnp.exp2((score - top) * EXPO_SCALE) for score, top in zip(scores, tops)]
    totals = [jnp.sum(expo, axis=1, keepdims=True) for expo in expos]
    mixed = [
        jnp.dot(expo.astype(jnp.bfloat16), value, preferred_element_type=jnp.float32)
        for expo, value in zip(expos, values)
    ]
    parts = [(mix * (1.0 / total)).astype(jnp.bfloat16) for mix, total in zip(mixed, totals)]
    lses = [top * EXPO_SCALE + jnp.log2(total) for top, total in zip(tops, totals)]
    return parts, lses


def as_row(column, offset):
    shape = (column.shape[0], LANES)
    row_at = lax.broadcasted_iota(jnp.int32, shape, 0)
    lane_at = lax.broadcasted_iota(jnp.int32, shape, 1)
    spread = jnp.where(lane_at == row_at + offset, column, 0.0)
    return jnp.sum(spread, axis=0, keepdims=True)


def stat_tile(rows):
    at = lax.broadcasted_iota(jnp.int32, (STAT_ROWS, LANES), 0)
    tile = jnp.zeros((STAT_ROWS, LANES), jnp.float32)
    count = len(rows)
    for index, row in enumerate(rows):
        high = row.astype(jnp.bfloat16).astype(jnp.float32)
        middle = (row - high).astype(jnp.bfloat16).astype(jnp.float32)
        low = row - high - middle
        for part, value in enumerate((high, middle, low)):
            tile = jnp.where(at == part * count + index, value, tile)
    return tile.astype(jnp.bfloat16)


def stat_rows_of(tile, count):
    wide = tile.astype(jnp.float32)
    return [
        wide[index : index + 1]
        + wide[count + index : count + index + 1]
        + wide[2 * count + index : 2 * count + index + 1]
        for index in range(count)
    ]


def stat_count(rows):
    return -(-rows // LANES)


def split_kernel(
    steps, me_ref, span_ref, query_ref, key_ref, value_ref, *refs
):
    halo_ref, out_refs, arrived = refs[0], refs[1:-1], refs[-1]
    me = me_ref[0]
    rows = query_ref.shape[0]
    halo = halo_ref.shape[1]
    copies = []
    for step, out_ref in zip(steps, out_refs):
        head = pl.multiple_of(partner(me, step) * HD, HD)
        copies.append((query_ref.at[:, pl.ds(head, HD)], out_ref.at[:rows]))
    copies.append((key_ref.at[rows - halo :], halo_ref.at[0]))
    copies.append((value_ref.at[rows - halo :], halo_ref.at[1]))
    copies = [
        pltpu.make_async_copy(source, target, arrived.at[index])
        for index, (source, target) in enumerate(copies)
    ]
    for copy in copies:
        copy.start()
    width = jnp.full((STAT_ROWS, HD), span_ref[0].astype(jnp.float32)).astype(jnp.bfloat16)
    for out_ref in out_refs:
        out_ref[rows:, :] = width
    for copy in copies:
        copy.wait()


def far_kernel(
    steps, me_ref, span_ref, global_ref, random_ref, key_ref, value_ref, *refs
):
    me = me_ref[0]
    span = span_ref[0]
    count = len(steps)
    query_refs, out_refs = refs[:count], refs[count:]
    last = key_ref.shape[0] // BLK - 1

    def block(ref, at):
        if isinstance(at, int):
            return ref[at * BLK : (at + 1) * BLK, :]
        return ref[pl.ds(pl.multiple_of(at * BLK, BLK), BLK), :]

    glob_keys = [block(key_ref, global_ref[g]) for g in range(GLOB)]
    glob_values = [block(value_ref, global_ref[g]) for g in range(GLOB)]
    for index, step in enumerate(steps):
        chunk = partner(me, step)
        query_ref, out_ref = query_refs[index], out_refs[index]
        rows = query_ref.shape[0] - STAT_ROWS
        blocks = rows // BLK
        first = chunk == 0
        all_scores, all_values = [], []
        for b in range(blocks):
            query = query_ref[b * BLK : (b + 1) * BLK, :]
            base = (chunk * blocks + b) * RAND
            picks = [random_ref[base + r] for r in range(RAND)]
            keys = glob_keys + [block(key_ref, pick) for pick in picks]
            values = glob_values + [block(value_ref, pick) for pick in picks]
            known = len(keys) * BLK
            spare = [last + 1 + b - w for w in range(b + 1, WMAX)]
            keys = keys + [block(key_ref, at) for at in spare]
            values = values + [block(value_ref, at) for at in spare]
            scores = scores_of(query, jnp.concatenate(keys, axis=0))
            if spare:
                open_slots = jnp.where(first, jnp.clip(span - (b + 1), 0, len(spare)), 0)
                lane_at = lax.broadcasted_iota(jnp.int32, scores.shape, 1)
                scores = jnp.where(lane_at < known + open_slots * BLK, scores, MASKED)
            all_scores.append(scores)
            all_values.append(jnp.concatenate(values, axis=0))
        parts, lses = softmax_parts(all_scores, all_values)
        stats = []
        for b in range(blocks):
            row = as_row(lses[b], (b * BLK) % LANES)
            if (b * BLK) % LANES:
                stats[-1] = stats[-1] + row
            else:
                stats.append(row)
        tile = stat_tile(stats)
        for b in range(blocks):
            out_ref[b * BLK : (b + 1) * BLK, :] = parts[b]
        out_ref[rows:, :] = tile


def near_kernel(
    steps, me_ref, query_ref, key_ref, value_ref, halo_ref, own_ref, *refs
):
    came_refs, out_ref = refs[:-1], refs[-1]
    me = me_ref[0]
    rows, wide = query_ref.shape
    halo = (WMAX - 1) * BLK
    starts = list(range(0, rows, 2 * BLK))
    sizes = [min(2 * BLK, rows - start) for start in starts]
    out_ref[:, wide:] = own_ref[...]
    for step, came_ref in zip(steps, came_refs):
        lanes = pl.ds(pl.multiple_of(partner(me, step) * HD, HD), HD)
        width = came_ref[rows:, :].astype(jnp.float32)[:1]
        width = jnp.concatenate([width] * ((2 * BLK + halo) // LANES), axis=1)
        all_scores, all_values = [], []
        for start, size in zip(starts, sizes):
            query = query_ref[start : start + size, lanes]
            if start < halo:
                keys = [halo_ref[0, start:, lanes], key_ref[: start + size, lanes]]
                values = [halo_ref[1, start:, lanes], value_ref[: start + size, lanes]]
                keys, values = jnp.concatenate(keys, axis=0), jnp.concatenate(values, axis=0)
            else:
                keys = key_ref[start - halo : start + size, lanes]
                values = value_ref[start - halo : start + size, lanes]
            scores = scores_of(query, keys)
            row_at = lax.broadcasted_iota(jnp.int32, scores.shape, 0)
            lane_at = lax.broadcasted_iota(jnp.int32, scores.shape, 1)
            slot = (lane_at // BLK - row_at // BLK).astype(jnp.float32)
            allowed = (lane_at <= row_at + halo) & (slot + width[:, : size + halo] >= WMAX)
            if start < halo:
                closed = jnp.where(me == 0, halo - start, 0)
                allowed = allowed & (lane_at >= closed)
            all_scores.append(jnp.where(allowed, scores, MASKED))
            all_values.append(values)
        parts, lses = softmax_parts(all_scores, all_values)
        tile = stat_tile([as_row(lse, 0) for lse in lses])
        for start, size, part in zip(starts, sizes, parts):
            out_ref[start : start + size, lanes] = part
        out_ref[rows:, lanes] = tile


def merge_kernel(steps, me_ref, *refs):
    me = me_ref[0]
    far_refs, out_ref = refs[:-1], refs[-1]
    near_ref = far_refs[steps.index(0)]
    rows, wide = out_ref.shape
    count = stat_count(rows)
    for step, far_ref in zip(steps, far_refs):
        part = slice(wide, None) if step == 0 else slice(None)
        lanes = pl.ds(pl.multiple_of(partner(me, step) * HD, HD), HD)
        far_stats = stat_rows_of(far_ref[rows:, part], count)
        near_stats = stat_rows_of(near_ref[rows:, lanes], count)
        for index in range(count):
            start = index * LANES
            size = min(LANES, rows - start)
            share = 1.0 / (1.0 + jnp.exp2(near_stats[index] - far_stats[index]))
            row_at = lax.broadcasted_iota(jnp.int32, (size, LANES), 0)
            lane_at = lax.broadcasted_iota(jnp.int32, (size, LANES), 1)
            column = jnp.sum(
                jnp.where(row_at == lane_at, share, 0.0), axis=1, keepdims=True
            )
            far = far_ref[start : start + size, part].astype(jnp.float32)
            near = near_ref[start : start + size, lanes].astype(jnp.float32)
            out_ref[start : start + size, lanes] = (
                far * column + near * (1.0 - column)
            ).astype(jnp.bfloat16)


def params(shard):
    return pltpu.CompilerParams(vmem_limit_bytes=VMEM_BASE + 14 * 2 * math.prod(shard.shape))


def per_device(
    queries, keys_new, values_new, keys_cache, values_cache, window, global_blocks, random_blocks
):
    section_count = lax.axis_size("section")
    seq_count = lax.axis_size("seq")
    rows, wide = queries.shape[1], queries.shape[2]
    halo = (WMAX - 1) * BLK
    heads = wide // HD
    bf16 = jnp.bfloat16
    me = lax.axis_index("seq").astype(jnp.int32)[None]
    half = max(seq_count // 2, 1)
    order = list(range(seq_count - 1, half - 1, -1)) + list(range(half))

    parts = pl.pallas_call(
        functools.partial(split_kernel, order),
        out_shape=[jax.ShapeDtypeStruct((2, halo, wide), bf16)]
        + [jax.ShapeDtypeStruct((rows + STAT_ROWS, HD), bf16)] * seq_count,
        in_specs=[whole_smem] * 2 + [anywhere] * 3,
        out_specs=[whole_vmem] * (1 + seq_count),
        scratch_shapes=[pltpu.SemaphoreType.DMA((seq_count + 2,))],
        compiler_params=params(queries),
        cost_estimate=pl.CostEstimate(flops=0, bytes_accessed=5 * rows * wide, transcendentals=0),
        name="split",
    )(me, window[0], queries[0], keys_new[0], values_new[0])
    mine, sent = parts[0], dict(zip(order, parts[1:]))

    def swapped(shard, step):
        if step == 0:
            return shard
        return lax.ppermute(shard, "seq", [(i, i ^ step) for i in range(seq_count)])

    came = {step: swapped(sent[step], step) for step in order}
    before = lax.ppermute(mine, "seq", [(i, i + 1) for i in range(seq_count - 1)])

    picks = random_blocks[0].reshape(-1)

    def far_call(steps):
        count = len(steps)
        out_rows = rows + STAT_ROWS
        return pl.pallas_call(
            functools.partial(far_kernel, steps),
            out_shape=[jax.ShapeDtypeStruct((out_rows, HD), bf16)] * count,
            in_specs=[whole_smem] * 4 + [whole_vmem] * (2 + count),
            out_specs=[whole_vmem] * count,
            compiler_params=params(queries),
            cost_estimate=pl.CostEstimate(
                flops=count * rows * 320 * HD * 4,
                bytes_accessed=2 * 2 * keys_cache.shape[1] * HD + 4 * count * rows * HD,
                transcendentals=count * rows * 320,
            ),
            name="far",
        )(
            me,
            window[0],
            global_blocks[0],
            picks,
            keys_cache[0],
            values_cache[0],
            *[came[step] for step in steps],
        )

    far = dict(zip(order, far_call(order)))
    far[0] = pl.pallas_call(
        functools.partial(near_kernel, order),
        out_shape=jax.ShapeDtypeStruct((rows + STAT_ROWS, wide + HD), bf16),
        in_specs=[whole_smem] + [whole_vmem] * (5 + seq_count),
        out_specs=whole_vmem,
        compiler_params=params(queries),
        cost_estimate=pl.CostEstimate(
            flops=heads * rows * 256 * HD * 4,
            bytes_accessed=9 * rows * wide,
            transcendentals=heads * rows * 256,
        ),
        name="near",
    )(
        me,
        queries[0],
        keys_new[0],
        values_new[0],
        before,
        far[0],
        *[came[step] for step in order],
    )

    def onward(shard, step):
        pairs = [
            (s * seq_count + t, ((s + 1) % section_count) * seq_count + (t ^ step))
            for s in range(section_count)
            for t in range(seq_count)
        ]
        return lax.ppermute(shard, ("section", "seq"), pairs)

    handed = {step: onward(far[step], step) for step in order}

    merged = pl.pallas_call(
        functools.partial(merge_kernel, order),
        out_shape=jax.ShapeDtypeStruct((rows, wide), bf16),
        in_specs=[whole_smem] + [whole_vmem] * seq_count,
        out_specs=whole_vmem,
        compiler_params=params(queries),
        cost_estimate=pl.CostEstimate(flops=0, bytes_accessed=6 * rows * wide, transcendentals=0),
        name="merge",
    )(me, *[handed[step] for step in order])
    return merged[None]


def solution(mesh):
    placed = (
        P("section", "seq", None),
        P("section", "seq", None),
        P("section", "seq", None),
        P("section", None, "seq"),
        P("section", None, "seq"),
        P("section", "seq"),
        P("section", None),
        P("section", None, None),
    )
    return jax.shard_map(
        per_device, mesh=mesh, in_specs=placed, out_specs=P("section", "seq", None), check_vma=False
    )
```

```python
import functools
import math

import jax
import jax.numpy as jnp
from jax import lax
from jax.experimental import pallas as pl
from jax.experimental.pallas import tpu as pltpu
from jax.sharding import PartitionSpec as P

HD = 128
BLK = 64
WMAX = 3
GLOB = 2
RAND = 3
LANES = 128
STAT_ROWS = 16
MASKED = -1e30
EXPO_SCALE = math.log2(math.e) / math.sqrt(HD)
VMEM_BASE = 12 * 1024 * 1024

whole_vmem = pl.BlockSpec(memory_space=pltpu.VMEM)
in_hbm = pl.BlockSpec(memory_space=pltpu.HBM)
whole_smem = pl.BlockSpec(memory_space=pltpu.SMEM)


def partner(me, step):
    return jnp.bitwise_xor(me, step)


def scores_of(query, keys):
    return lax.dot_general(
        query, keys, (((1,), (1,)), ((), ())), preferred_element_type=jnp.float32
    )


def softmax_parts(scores, values):
    tops = [jnp.max(score, axis=1, keepdims=True) for score in scores]
    expos = [jnp.exp2((score - top) * EXPO_SCALE) for score, top in zip(scores, tops)]
    totals = [jnp.sum(expo, axis=1, keepdims=True) for expo in expos]
    mixed = [
        jnp.dot(expo.astype(jnp.bfloat16), value, preferred_element_type=jnp.float32)
        for expo, value in zip(expos, values)
    ]
    parts = [(mix * (1.0 / total)).astype(jnp.bfloat16) for mix, total in zip(mixed, totals)]
    lses = [top * EXPO_SCALE + jnp.log2(total) for top, total in zip(tops, totals)]
    return parts, lses


def as_row(column, offset):
    shape = (column.shape[0], LANES)
    row_at = lax.broadcasted_iota(jnp.int32, shape, 0)
    lane_at = lax.broadcasted_iota(jnp.int32, shape, 1)
    spread = jnp.where(lane_at == row_at + offset, column, 0.0)
    return jnp.sum(spread, axis=0, keepdims=True)


def stat_tile(rows):
    at = lax.broadcasted_iota(jnp.int32, (STAT_ROWS, LANES), 0)
    tile = jnp.zeros((STAT_ROWS, LANES), jnp.float32)
    count = len(rows)
    for index, row in enumerate(rows):
        high = row.astype(jnp.bfloat16).astype(jnp.float32)
        middle = (row - high).astype(jnp.bfloat16).astype(jnp.float32)
        low = row - high - middle
        for part, value in enumerate((high, middle, low)):
            tile = jnp.where(at == part * count + index, value, tile)
    return tile.astype(jnp.bfloat16)


def stat_rows_of(tile, count):
    wide = tile.astype(jnp.float32)
    return [
        wide[index : index + 1]
        + wide[count + index : count + index + 1]
        + wide[2 * count + index : 2 * count + index + 1]
        for index in range(count)
    ]


def stat_count(rows):
    return -(-rows // LANES)


def split_kernel(
    steps, me_ref, span_ref, query_ref, key_ref, value_ref, *refs
):
    halo_ref, out_refs, arrived = refs[0], refs[1:-1], refs[-1]
    me = me_ref[0]
    rows = query_ref.shape[0]
    halo = halo_ref.shape[1]
    copies = []
    for step, out_ref in zip(steps, out_refs):
        head = pl.multiple_of(partner(me, step) * HD, HD)
        copies.append((query_ref.at[:, pl.ds(head, HD)], out_ref.at[:rows]))
    copies.append((key_ref.at[rows - halo :], halo_ref.at[0]))
    copies.append((value_ref.at[rows - halo :], halo_ref.at[1]))
    copies = [
        pltpu.make_async_copy(source, target, arrived.at[index])
        for index, (source, target) in enumerate(copies)
    ]
    for copy in copies:
        copy.start()
    width = jnp.full((STAT_ROWS, HD), span_ref[0].astype(jnp.float32)).astype(jnp.bfloat16)
    for out_ref in out_refs:
        out_ref[rows:, :] = width
    for copy in copies:
        copy.wait()


def far_kernel(
    steps, me_ref, span_ref, global_ref, random_ref, key_ref, value_ref, *refs
):
    count = len(steps)
    query_refs, out_refs = refs[:count], refs[count : 2 * count]
    value_held, arrived = refs[2 * count :]
    value_copy = pltpu.make_async_copy(value_ref, value_held, arrived)
    value_copy.start()
    me = me_ref[0]
    span = span_ref[0]
    last = key_ref.shape[0] // BLK - 1

    def block(ref, at):
        if isinstance(at, int):
            return ref[at * BLK : (at + 1) * BLK, :]
        return ref[pl.ds(pl.multiple_of(at * BLK, BLK), BLK), :]

    glob_keys = [block(key_ref, global_ref[g]) for g in range(GLOB)]
    for index, step in enumerate(steps):
        chunk = partner(me, step)
        query_ref, out_ref = query_refs[index], out_refs[index]
        rows = query_ref.shape[0] - STAT_ROWS
        blocks = rows // BLK
        first = chunk == 0
        all_scores, all_picks = [], []
        for b in range(blocks):
            query = query_ref[b * BLK : (b + 1) * BLK, :]
            base = (chunk * blocks + b) * RAND
            picks = [random_ref[base + r] for r in range(RAND)]
            keys = glob_keys + [block(key_ref, pick) for pick in picks]
            known = len(keys) * BLK
            spare = [last + 1 + b - w for w in range(b + 1, WMAX)]
            keys = keys + [block(key_ref, at) for at in spare]
            scores = scores_of(query, jnp.concatenate(keys, axis=0))
            if spare:
                open_slots = jnp.where(first, jnp.clip(span - (b + 1), 0, len(spare)), 0)
                lane_at = lax.broadcasted_iota(jnp.int32, scores.shape, 1)
                scores = jnp.where(lane_at < known + open_slots * BLK, scores, MASKED)
            all_scores.append(scores)
            all_picks.append(picks + spare)
        if index == 0:
            value_copy.wait()
            glob_values = [block(value_held, global_ref[g]) for g in range(GLOB)]
        all_values = [
            jnp.concatenate(glob_values + [block(value_held, at) for at in picks], axis=0)
            for picks in all_picks
        ]
        parts, lses = softmax_parts(all_scores, all_values)
        stats = []
        for b in range(blocks):
            row = as_row(lses[b], (b * BLK) % LANES)
            if (b * BLK) % LANES:
                stats[-1] = stats[-1] + row
            else:
                stats.append(row)
        tile = stat_tile(stats)
        for b in range(blocks):
            out_ref[b * BLK : (b + 1) * BLK, :] = parts[b]
        out_ref[rows:, :] = tile


def near_kernel(
    steps, me_ref, query_ref, key_ref, value_ref, halo_ref, own_ref, *refs
):
    came_refs, out_ref = refs[:-1], refs[-1]
    me = me_ref[0]
    rows, wide = query_ref.shape
    halo = (WMAX - 1) * BLK
    starts = list(range(0, rows, 2 * BLK))
    sizes = [min(2 * BLK, rows - start) for start in starts]
    out_ref[:, wide:] = own_ref[...]
    for step, came_ref in zip(steps, came_refs):
        lanes = pl.ds(pl.multiple_of(partner(me, step) * HD, HD), HD)
        width = came_ref[rows:, :].astype(jnp.float32)[:1]
        width = jnp.concatenate([width] * ((2 * BLK + halo) // LANES), axis=1)
        all_scores, all_values = [], []
        for start, size in zip(starts, sizes):
            query = query_ref[start : start + size, lanes]
            if start < halo:
                keys = [halo_ref[0, start:, lanes], key_ref[: start + size, lanes]]
                values = [halo_ref[1, start:, lanes], value_ref[: start + size, lanes]]
                keys, values = jnp.concatenate(keys, axis=0), jnp.concatenate(values, axis=0)
            else:
                keys = key_ref[start - halo : start + size, lanes]
                values = value_ref[start - halo : start + size, lanes]
            scores = scores_of(query, keys)
            row_at = lax.broadcasted_iota(jnp.int32, scores.shape, 0)
            lane_at = lax.broadcasted_iota(jnp.int32, scores.shape, 1)
            slot = (lane_at // BLK - row_at // BLK).astype(jnp.float32)
            allowed = (lane_at <= row_at + halo) & (slot + width[:, : size + halo] >= WMAX)
            if start < halo:
                closed = jnp.where(me == 0, halo - start, 0)
                allowed = allowed & (lane_at >= closed)
            all_scores.append(jnp.where(allowed, scores, MASKED))
            all_values.append(values)
        parts, lses = softmax_parts(all_scores, all_values)
        tile = stat_tile([as_row(lse, 0) for lse in lses])
        for start, size, part in zip(starts, sizes, parts):
            out_ref[start : start + size, lanes] = part
        out_ref[rows:, lanes] = tile


def merge_kernel(steps, me_ref, *refs):
    me = me_ref[0]
    far_refs, out_ref = refs[:-1], refs[-1]
    near_ref = far_refs[steps.index(0)]
    rows, wide = out_ref.shape
    count = stat_count(rows)
    for step, far_ref in zip(steps, far_refs):
        part = slice(wide, None) if step == 0 else slice(None)
        lanes = pl.ds(pl.multiple_of(partner(me, step) * HD, HD), HD)
        far_stats = stat_rows_of(far_ref[rows:, part], count)
        near_stats = stat_rows_of(near_ref[rows:, lanes], count)
        for index in range(count):
            start = index * LANES
            size = min(LANES, rows - start)
            share = 1.0 / (1.0 + jnp.exp2(near_stats[index] - far_stats[index]))
            row_at = lax.broadcasted_iota(jnp.int32, (size, LANES), 0)
            lane_at = lax.broadcasted_iota(jnp.int32, (size, LANES), 1)
            column = jnp.sum(
                jnp.where(row_at == lane_at, share, 0.0), axis=1, keepdims=True
            )
            far = far_ref[start : start + size, part].astype(jnp.float32)
            near = near_ref[start : start + size, lanes].astype(jnp.float32)
            out_ref[start : start + size, lanes] = (
                far * column + near * (1.0 - column)
            ).astype(jnp.bfloat16)


def params(shard):
    return pltpu.CompilerParams(vmem_limit_bytes=VMEM_BASE + 14 * 2 * math.prod(shard.shape))


def per_device(
    queries, keys_new, values_new, keys_cache, values_cache, window, global_blocks, random_blocks
):
    section_count = lax.axis_size("section")
    seq_count = lax.axis_size("seq")
    rows, wide = queries.shape[1], queries.shape[2]
    halo = (WMAX - 1) * BLK
    heads = wide // HD
    bf16 = jnp.bfloat16
    me = lax.axis_index("seq").astype(jnp.int32)[None]
    half = max(seq_count // 2, 1)
    order = list(range(1, half)) + list(range(seq_count - 1, half - 1, -1)) + [0]

    parts = pl.pallas_call(
        functools.partial(split_kernel, order),
        out_shape=[jax.ShapeDtypeStruct((2, halo, wide), bf16)]
        + [jax.ShapeDtypeStruct((rows + STAT_ROWS, HD), bf16)] * seq_count,
        in_specs=[whole_smem] * 2 + [in_hbm] * 3,
        out_specs=[whole_vmem] * (1 + seq_count),
        scratch_shapes=[pltpu.SemaphoreType.DMA((seq_count + 2,))],
        compiler_params=params(queries),
        cost_estimate=pl.CostEstimate(flops=0, bytes_accessed=5 * rows * wide, transcendentals=0),
        name="split",
    )(me, window[0], queries[0], keys_new[0], values_new[0])
    mine, sent = parts[0], dict(zip(order, parts[1:]))

    def swapped(shard, step):
        if step == 0:
            return shard
        return lax.ppermute(shard, "seq", [(i, i ^ step) for i in range(seq_count)])

    came = {step: swapped(sent[step], step) for step in order}
    before = lax.ppermute(mine, "seq", [(i, i + 1) for i in range(seq_count - 1)])

    picks = random_blocks[0].reshape(-1)

    def far_call(steps):
        count = len(steps)
        out_rows = rows + STAT_ROWS
        return pl.pallas_call(
            functools.partial(far_kernel, steps),
            out_shape=[jax.ShapeDtypeStruct((out_rows, HD), bf16)] * count,
            in_specs=[whole_smem] * 4 + [whole_vmem, in_hbm] + [whole_vmem] * count,
            out_specs=[whole_vmem] * count,
            scratch_shapes=[
                pltpu.VMEM(values_cache.shape[1:], bf16),
                pltpu.SemaphoreType.DMA,
            ],
            compiler_params=params(queries),
            cost_estimate=pl.CostEstimate(
                flops=count * rows * 320 * HD * 4,
                bytes_accessed=2 * 2 * keys_cache.shape[1] * HD + 4 * count * rows * HD,
                transcendentals=count * rows * 320,
            ),
            name="far",
        )(
            me,
            window[0],
            global_blocks[0],
            picks,
            keys_cache[0],
            values_cache[0],
            *[came[step] for step in steps],
        )

    far = dict(zip(order, far_call(order)))
    far[0] = pl.pallas_call(
        functools.partial(near_kernel, order),
        out_shape=jax.ShapeDtypeStruct((rows + STAT_ROWS, wide + HD), bf16),
        in_specs=[whole_smem] + [whole_vmem] * (5 + seq_count),
        out_specs=whole_vmem,
        compiler_params=params(queries),
        cost_estimate=pl.CostEstimate(
            flops=heads * rows * 256 * HD * 4,
            bytes_accessed=9 * rows * wide,
            transcendentals=heads * rows * 256,
        ),
        name="near",
    )(
        me,
        queries[0],
        keys_new[0],
        values_new[0],
        before,
        far[0],
        *[came[step] for step in order],
    )

    def onward(shard, step):
        pairs = [
            (s * seq_count + t, ((s + 1) % section_count) * seq_count + (t ^ step))
            for s in range(section_count)
            for t in range(seq_count)
        ]
        return lax.ppermute(shard, ("section", "seq"), pairs)

    handed = {step: onward(far[step], step) for step in order}

    merged = pl.pallas_call(
        functools.partial(merge_kernel, order),
        out_shape=jax.ShapeDtypeStruct((rows, wide), bf16),
        in_specs=[whole_smem] + [whole_vmem] * seq_count,
        out_specs=whole_vmem,
        compiler_params=params(queries),
        cost_estimate=pl.CostEstimate(flops=0, bytes_accessed=6 * rows * wide, transcendentals=0),
        name="merge",
    )(me, *[handed[step] for step in order])
    return merged[None]


def solution(mesh):
    placed = (
        P("section", "seq", None),
        P("section", "seq", None),
        P("section", "seq", None),
        P("section", None, "seq"),
        P("section", None, "seq"),
        P("section", "seq"),
        P("section", None),
        P("section", None, None),
    )
    return jax.shard_map(
        per_device, mesh=mesh, in_specs=placed, out_specs=P("section", "seq", None), check_vma=False
    )
```

```python
import functools
import math

import jax
import jax.numpy as jnp
from jax import lax
from jax.experimental import pallas as pl
from jax.experimental.pallas import tpu as pltpu
from jax.sharding import PartitionSpec as P

HD = 128
BLK = 64
WMAX = 3
GLOB = 2
RAND = 3
LANES = 128
STAT_ROWS = 16
MASKED = -1e30
EXPO_SCALE = math.log2(math.e) / math.sqrt(HD)
VMEM_BASE = 12 * 1024 * 1024

whole_vmem = pl.BlockSpec(memory_space=pltpu.VMEM)
in_hbm = pl.BlockSpec(memory_space=pltpu.HBM)
whole_smem = pl.BlockSpec(memory_space=pltpu.SMEM)


def peers_of(there, by):
    count = lax.axis_size("section")
    other = lax.rem(lax.axis_index("section") + (by + count), count)
    odd = lax.rem(other, 2) == 1
    me = lax.axis_index("seq")
    return [
        jnp.bitwise_xor(me, jnp.where(odd, odd_step, even_step))
        for even_step, odd_step in zip(*there)
    ]


def scores_of(query, keys):
    return lax.dot_general(
        query, keys, (((1,), (1,)), ((), ())), preferred_element_type=jnp.float32
    )


def softmax_parts(scores, values):
    tops = [jnp.max(score, axis=1, keepdims=True) for score in scores]
    expos = [jnp.exp2((score - top) * EXPO_SCALE) for score, top in zip(scores, tops)]
    totals = [jnp.sum(expo, axis=1, keepdims=True) for expo in expos]
    mixed = [
        jnp.dot(expo.astype(jnp.bfloat16), value, preferred_element_type=jnp.float32)
        for expo, value in zip(expos, values)
    ]
    parts = [(mix * (1.0 / total)).astype(jnp.bfloat16) for mix, total in zip(mixed, totals)]
    lses = [top * EXPO_SCALE + jnp.log2(total) for top, total in zip(tops, totals)]
    return parts, lses


def as_row(column, offset):
    shape = (column.shape[0], LANES)
    row_at = lax.broadcasted_iota(jnp.int32, shape, 0)
    lane_at = lax.broadcasted_iota(jnp.int32, shape, 1)
    spread = jnp.where(lane_at == row_at + offset, column, 0.0)
    return jnp.sum(spread, axis=0, keepdims=True)


def stat_tile(rows):
    at = lax.broadcasted_iota(jnp.int32, (STAT_ROWS, LANES), 0)
    tile = jnp.zeros((STAT_ROWS, LANES), jnp.float32)
    count = len(rows)
    for index, row in enumerate(rows):
        high = row.astype(jnp.bfloat16).astype(jnp.float32)
        middle = (row - high).astype(jnp.bfloat16).astype(jnp.float32)
        low = row - high - middle
        for part, value in enumerate((high, middle, low)):
            tile = jnp.where(at == part * count + index, value, tile)
    return tile.astype(jnp.bfloat16)


def stat_rows_of(tile, count):
    wide = tile.astype(jnp.float32)
    return [
        wide[index : index + 1]
        + wide[count + index : count + index + 1]
        + wide[2 * count + index : 2 * count + index + 1]
        for index in range(count)
    ]


def stat_count(rows):
    return -(-rows // LANES)


def split_kernel(there, span_ref, query_ref, *refs):
    out_refs, arrived = refs[:-1], refs[-1]
    rows = query_ref.shape[0]
    copies = []
    for peer, out_ref in zip(peers_of(there, 0), out_refs):
        head = pl.multiple_of(peer * HD, HD)
        copies.append((query_ref.at[:, pl.ds(head, HD)], out_ref.at[:rows]))
    copies = [
        pltpu.make_async_copy(source, target, arrived.at[index])
        for index, (source, target) in enumerate(copies)
    ]
    for copy in copies:
        copy.start()
    width = jnp.full((STAT_ROWS, HD), span_ref[0].astype(jnp.float32)).astype(jnp.bfloat16)
    for out_ref in out_refs:
        out_ref[rows:, :] = width
    for copy in copies:
        copy.wait()


def fetch_kernel(key_ref, value_ref, old_key_ref, old_value_ref, *refs):
    halo_ref, held_key_ref, held_value_ref, arrived = refs
    halo = halo_ref.shape[1]
    rows = key_ref.shape[0]
    copies = [
        (key_ref.at[rows - halo :], halo_ref.at[0]),
        (value_ref.at[rows - halo :], halo_ref.at[1]),
        (old_key_ref, held_key_ref),
        (old_value_ref, held_value_ref),
    ]
    copies = [
        pltpu.make_async_copy(source, target, arrived.at[index])
        for index, (source, target) in enumerate(copies)
    ]
    for copy in copies:
        copy.start()
    for copy in copies:
        copy.wait()


def far_kernel(
    there, span_ref, global_ref, random_ref, key_ref, value_ref, *refs
):
    peers = peers_of(there, 0)
    count = len(peers)
    query_refs, out_refs = refs[:count], refs[count:]
    span = span_ref[0]
    last = key_ref.shape[0] // BLK - 1

    def block(ref, at):
        if isinstance(at, int):
            return ref[at * BLK : (at + 1) * BLK, :]
        return ref[pl.ds(pl.multiple_of(at * BLK, BLK), BLK), :]

    glob_keys = [block(key_ref, global_ref[g]) for g in range(GLOB)]
    glob_values = [block(value_ref, global_ref[g]) for g in range(GLOB)]
    for index, chunk in enumerate(peers):
        query_ref, out_ref = query_refs[index], out_refs[index]
        rows = query_ref.shape[0] - STAT_ROWS
        blocks = rows // BLK
        first = chunk == 0
        all_scores, all_picks = [], []
        for b in range(blocks):
            query = query_ref[b * BLK : (b + 1) * BLK, :]
            base = (chunk * blocks + b) * RAND
            picks = [random_ref[base + r] for r in range(RAND)]
            keys = glob_keys + [block(key_ref, pick) for pick in picks]
            known = len(keys) * BLK
            spare = [last + 1 + b - w for w in range(b + 1, WMAX)]
            keys = keys + [block(key_ref, at) for at in spare]
            scores = scores_of(query, jnp.concatenate(keys, axis=0))
            if spare:
                open_slots = jnp.where(first, jnp.clip(span - (b + 1), 0, len(spare)), 0)
                lane_at = lax.broadcasted_iota(jnp.int32, scores.shape, 1)
                scores = jnp.where(lane_at < known + open_slots * BLK, scores, MASKED)
            all_scores.append(scores)
            all_picks.append(picks + spare)
        all_values = [
            jnp.concatenate(glob_values + [block(value_ref, at) for at in picks], axis=0)
            for picks in all_picks
        ]
        parts, lses = softmax_parts(all_scores, all_values)
        stats = []
        for b in range(blocks):
            row = as_row(lses[b], (b * BLK) % LANES)
            if (b * BLK) % LANES:
                stats[-1] = stats[-1] + row
            else:
                stats.append(row)
        tile = stat_tile(stats)
        for b in range(blocks):
            out_ref[b * BLK : (b + 1) * BLK, :] = parts[b]
        out_ref[rows:, :] = tile


def near_kernel(
    there, query_ref, key_ref, value_ref, halo_ref, own_ref, *refs
):
    came_refs, out_ref = refs[:-1], refs[-1]
    me = lax.axis_index("seq")
    rows, wide = query_ref.shape
    halo = (WMAX - 1) * BLK
    starts = list(range(0, rows, 2 * BLK))
    sizes = [min(2 * BLK, rows - start) for start in starts]
    out_ref[:, wide:] = own_ref[...]
    for peer, came_ref in zip(peers_of(there, 0), came_refs):
        lanes = pl.ds(pl.multiple_of(peer * HD, HD), HD)
        width = came_ref[rows:, :].astype(jnp.float32)[:1]
        width = jnp.concatenate([width] * ((2 * BLK + halo) // LANES), axis=1)
        all_scores, all_values = [], []
        for start, size in zip(starts, sizes):
            query = query_ref[start : start + size, lanes]
            if start < halo:
                keys = [halo_ref[0, start:, lanes], key_ref[: start + size, lanes]]
                values = [halo_ref[1, start:, lanes], value_ref[: start + size, lanes]]
                keys, values = jnp.concatenate(keys, axis=0), jnp.concatenate(values, axis=0)
            else:
                keys = key_ref[start - halo : start + size, lanes]
                values = value_ref[start - halo : start + size, lanes]
            scores = scores_of(query, keys)
            row_at = lax.broadcasted_iota(jnp.int32, scores.shape, 0)
            lane_at = lax.broadcasted_iota(jnp.int32, scores.shape, 1)
            slot = (lane_at // BLK - row_at // BLK).astype(jnp.float32)
            allowed = (lane_at <= row_at + halo) & (slot + width[:, : size + halo] >= WMAX)
            if start < halo:
                closed = jnp.where(me == 0, halo - start, 0)
                allowed = allowed & (lane_at >= closed)
            all_scores.append(jnp.where(allowed, scores, MASKED))
            all_values.append(values)
        parts, lses = softmax_parts(all_scores, all_values)
        tile = stat_tile([as_row(lse, 0) for lse in lses])
        for start, size, part in zip(starts, sizes, parts):
            out_ref[start : start + size, lanes] = part
        out_ref[rows:, lanes] = tile


def merge_kernel(there, *refs):
    far_refs, out_ref = refs[:-1], refs[-1]
    own = len(far_refs) - 1
    near_ref = far_refs[own]
    rows, wide = out_ref.shape
    count = stat_count(rows)
    for index, (peer, far_ref) in enumerate(zip(peers_of(there, -1), far_refs)):
        part = slice(wide, None) if index == own else slice(None)
        lanes = pl.ds(pl.multiple_of(peer * HD, HD), HD)
        far_stats = stat_rows_of(far_ref[rows:, part], count)
        near_stats = stat_rows_of(near_ref[rows:, lanes], count)
        for group in range(count):
            start = group * LANES
            size = min(LANES, rows - start)
            share = 1.0 / (1.0 + jnp.exp2(near_stats[group] - far_stats[group]))
            row_at = lax.broadcasted_iota(jnp.int32, (size, LANES), 0)
            lane_at = lax.broadcasted_iota(jnp.int32, (size, LANES), 1)
            column = jnp.sum(
                jnp.where(row_at == lane_at, share, 0.0), axis=1, keepdims=True
            )
            far = far_ref[start : start + size, part].astype(jnp.float32)
            near = near_ref[start : start + size, lanes].astype(jnp.float32)
            out_ref[start : start + size, lanes] = (
                far * column + near * (1.0 - column)
            ).astype(jnp.bfloat16)


def params(shard):
    return pltpu.CompilerParams(vmem_limit_bytes=VMEM_BASE + 14 * 2 * math.prod(shard.shape))


def per_device(
    queries, keys_new, values_new, keys_cache, values_cache, window, global_blocks, random_blocks
):
    section_count = lax.axis_size("section")
    seq_count = lax.axis_size("seq")
    rows, wide = queries.shape[1], queries.shape[2]
    halo = (WMAX - 1) * BLK
    heads = wide // HD
    bf16 = jnp.bfloat16
    half = max(seq_count // 2, 1)
    inner, outer = list(range(1, half)), list(range(seq_count - 1, half - 1, -1))
    there = [outer + inner + [0], inner + outer + [0]]

    sent = pl.pallas_call(
        functools.partial(split_kernel, there),
        out_shape=[jax.ShapeDtypeStruct((rows + STAT_ROWS, HD), bf16)] * seq_count,
        in_specs=[whole_smem, in_hbm],
        out_specs=[whole_vmem] * seq_count,
        scratch_shapes=[pltpu.SemaphoreType.DMA((seq_count,))],
        compiler_params=params(queries),
        cost_estimate=pl.CostEstimate(flops=0, bytes_accessed=5 * rows * wide, transcendentals=0),
        name="split",
    )(window[0], queries[0])

    def linked(shard, by, steps):
        pairs = [
            (
                s * seq_count + t,
                (s + by) % section_count * seq_count + (t ^ steps[s % 2]),
            )
            for s in range(section_count)
            for t in range(seq_count)
        ]
        return lax.ppermute(shard, ("section", "seq"), pairs)

    came = [linked(shard, 0, steps) for shard, steps in zip(sent[:-1], zip(*there))]
    came.append(sent[-1])
    mine, held_keys, held_values = pl.pallas_call(
        fetch_kernel,
        out_shape=[
            jax.ShapeDtypeStruct((2, halo, wide), bf16),
            jax.ShapeDtypeStruct(keys_cache.shape[1:], bf16),
            jax.ShapeDtypeStruct(values_cache.shape[1:], bf16),
        ],
        in_specs=[in_hbm] * 4,
        out_specs=[whole_vmem] * 3,
        scratch_shapes=[pltpu.SemaphoreType.DMA((4,))],
        compiler_params=params(queries),
        cost_estimate=pl.CostEstimate(
            flops=0, bytes_accessed=8 * keys_cache.shape[1] * HD, transcendentals=0
        ),
        name="fetch",
    )(keys_new[0], values_new[0], keys_cache[0], values_cache[0])
    before = lax.ppermute(mine, "seq", [(i, i + 1) for i in range(seq_count - 1)])

    picks = random_blocks[0].reshape(-1)

    def far_call():
        count = seq_count
        out_rows = rows + STAT_ROWS
        return pl.pallas_call(
            functools.partial(far_kernel, there),
            out_shape=[jax.ShapeDtypeStruct((out_rows, HD), bf16)] * count,
            in_specs=[whole_smem] * 3 + [whole_vmem] * (2 + count),
            out_specs=[whole_vmem] * count,
            compiler_params=params(queries),
            cost_estimate=pl.CostEstimate(
                flops=40 * count * rows * 320 * HD * 4,
                bytes_accessed=2 * 2 * keys_cache.shape[1] * HD + 4 * count * rows * HD,
                transcendentals=count * rows * 320,
            ),
            name="far",
        )(
            window[0],
            global_blocks[0],
            picks,
            held_keys,
            held_values,
            *came,
        )

    far = far_call()
    both = pl.pallas_call(
        functools.partial(near_kernel, there),
        out_shape=jax.ShapeDtypeStruct((rows + STAT_ROWS, wide + HD), bf16),
        in_specs=[whole_vmem] * (5 + seq_count),
        out_specs=whole_vmem,
        compiler_params=params(queries),
        cost_estimate=pl.CostEstimate(
            flops=40 * heads * rows * 256 * HD * 4,
            bytes_accessed=9 * rows * wide,
            transcendentals=heads * rows * 256,
        ),
        name="near",
    )(
        queries[0],
        keys_new[0],
        values_new[0],
        before,
        far[-1],
        *came,
    )

    returned = [*far[:-1], both]
    handed = [linked(shard, 1, steps) for shard, steps in zip(returned, zip(*there))]

    merged = pl.pallas_call(
        functools.partial(merge_kernel, there),
        out_shape=jax.ShapeDtypeStruct((rows, wide), bf16),
        in_specs=[whole_vmem] * seq_count,
        out_specs=whole_vmem,
        compiler_params=params(queries),
        cost_estimate=pl.CostEstimate(flops=0, bytes_accessed=6 * rows * wide, transcendentals=0),
        name="merge",
    )(*handed)
    return merged[None]


def solution(mesh):
    placed = (
        P("section", "seq", None),
        P("section", "seq", None),
        P("section", "seq", None),
        P("section", None, "seq"),
        P("section", None, "seq"),
        P("section", "seq"),
        P("section", None),
        P("section", None, None),
    )
    return jax.shard_map(
        per_device, mesh=mesh, in_specs=placed, out_specs=P("section", "seq", None), check_vma=False
    )
```

```python
import functools
import math

import jax
import jax.numpy as jnp
from jax import lax
from jax.experimental import pallas as pl
from jax.experimental.pallas import tpu as pltpu
from jax.sharding import PartitionSpec as P

HD = 128
BLK = 64
WMAX = 3
GLOB = 2
RAND = 3
LANES = 128
STAT_ROWS = 16
MASKED = -1e30
EXPO_SCALE = math.log2(math.e) / math.sqrt(HD)
VMEM_BASE = 12 * 1024 * 1024

whole_vmem = pl.BlockSpec(memory_space=pltpu.VMEM)
anywhere = pl.BlockSpec(memory_space=pl.ANY)
in_hbm = pl.BlockSpec(memory_space=pltpu.HBM)
whole_smem = pl.BlockSpec(memory_space=pltpu.SMEM)


def peers_of(there, by):
    count = lax.axis_size("section")
    other = lax.rem(lax.axis_index("section") + (by + count), count)
    odd = lax.rem(other, 2) == 1
    me = lax.axis_index("seq")
    return [
        jnp.bitwise_xor(me, jnp.where(odd, odd_step, even_step))
        for even_step, odd_step in zip(*there)
    ]


def scores_of(query, keys):
    return lax.dot_general(
        query, keys, (((1,), (1,)), ((), ())), preferred_element_type=jnp.float32
    )


def softmax_parts(scores, values):
    tops = [jnp.max(score, axis=1, keepdims=True) for score in scores]
    expos = [jnp.exp2((score - top) * EXPO_SCALE) for score, top in zip(scores, tops)]
    totals = [jnp.sum(expo, axis=1, keepdims=True) for expo in expos]
    mixed = [
        jnp.dot(expo.astype(jnp.bfloat16), value, preferred_element_type=jnp.float32)
        for expo, value in zip(expos, values)
    ]
    parts = [(mix * (1.0 / total)).astype(jnp.bfloat16) for mix, total in zip(mixed, totals)]
    lses = [top * EXPO_SCALE + jnp.log2(total) for top, total in zip(tops, totals)]
    return parts, lses


def as_row(column, offset):
    shape = (column.shape[0], LANES)
    row_at = lax.broadcasted_iota(jnp.int32, shape, 0)
    lane_at = lax.broadcasted_iota(jnp.int32, shape, 1)
    spread = jnp.where(lane_at == row_at + offset, column, 0.0)
    return jnp.sum(spread, axis=0, keepdims=True)


def stat_tile(rows):
    at = lax.broadcasted_iota(jnp.int32, (STAT_ROWS, LANES), 0)
    tile = jnp.zeros((STAT_ROWS, LANES), jnp.float32)
    count = len(rows)
    for index, row in enumerate(rows):
        high = row.astype(jnp.bfloat16).astype(jnp.float32)
        middle = (row - high).astype(jnp.bfloat16).astype(jnp.float32)
        low = row - high - middle
        for part, value in enumerate((high, middle, low)):
            tile = jnp.where(at == part * count + index, value, tile)
    return tile.astype(jnp.bfloat16)


def stat_rows_of(tile, count):
    wide = tile.astype(jnp.float32)
    return [
        wide[index : index + 1]
        + wide[count + index : count + index + 1]
        + wide[2 * count + index : 2 * count + index + 1]
        for index in range(count)
    ]


def stat_count(rows):
    return -(-rows // LANES)


def split_kernel(there, span_ref, query_ref, *refs):
    out_refs, arrived = refs[:-1], refs[-1]
    rows = query_ref.shape[0]
    copies = []
    for peer, out_ref in zip(peers_of(there, 0), out_refs):
        head = pl.multiple_of(peer * HD, HD)
        copies.append((query_ref.at[:, pl.ds(head, HD)], out_ref.at[:rows]))
    copies = [
        pltpu.make_async_copy(source, target, arrived.at[index])
        for index, (source, target) in enumerate(copies)
    ]
    for copy in copies:
        copy.start()
    width = jnp.full((STAT_ROWS, HD), span_ref[0].astype(jnp.float32)).astype(jnp.bfloat16)
    for out_ref in out_refs:
        out_ref[rows:, :] = width
    for copy in copies:
        copy.wait()


def far_kernel(
    there, span_ref, global_ref, random_ref, key_ref, value_ref, *refs
):
    peers = peers_of(there, 0)
    count = len(peers)
    query_refs, out_refs = refs[:count], refs[count:]
    span = span_ref[0]
    last = key_ref.shape[0] // BLK - 1

    def block(ref, at):
        if isinstance(at, int):
            return ref[at * BLK : (at + 1) * BLK, :]
        return ref[pl.ds(pl.multiple_of(at * BLK, BLK), BLK), :]

    glob_keys = [block(key_ref, global_ref[g]) for g in range(GLOB)]
    glob_values = [block(value_ref, global_ref[g]) for g in range(GLOB)]
    for index, chunk in enumerate(peers):
        query_ref, out_ref = query_refs[index], out_refs[index]
        rows = query_ref.shape[0] - STAT_ROWS
        blocks = rows // BLK
        first = chunk == 0
        all_scores, all_picks = [], []
        for b in range(blocks):
            query = query_ref[b * BLK : (b + 1) * BLK, :]
            base = (chunk * blocks + b) * RAND
            picks = [random_ref[base + r] for r in range(RAND)]
            keys = glob_keys + [block(key_ref, pick) for pick in picks]
            known = len(keys) * BLK
            spare = [last + 1 + b - w for w in range(b + 1, WMAX)]
            keys = keys + [block(key_ref, at) for at in spare]
            scores = scores_of(query, jnp.concatenate(keys, axis=0))
            if spare:
                open_slots = jnp.where(first, jnp.clip(span - (b + 1), 0, len(spare)), 0)
                lane_at = lax.broadcasted_iota(jnp.int32, scores.shape, 1)
                scores = jnp.where(lane_at < known + open_slots * BLK, scores, MASKED)
            all_scores.append(scores)
            all_picks.append(picks + spare)
        all_values = [
            jnp.concatenate(glob_values + [block(value_ref, at) for at in picks], axis=0)
            for picks in all_picks
        ]
        parts, lses = softmax_parts(all_scores, all_values)
        stats = []
        for b in range(blocks):
            row = as_row(lses[b], (b * BLK) % LANES)
            if (b * BLK) % LANES:
                stats[-1] = stats[-1] + row
            else:
                stats.append(row)
        tile = stat_tile(stats)
        for b in range(blocks):
            out_ref[b * BLK : (b + 1) * BLK, :] = parts[b]
        out_ref[rows:, :] = tile


def near_kernel(
    there, query_ref, key_ref, value_ref, halo_ref, own_ref, *refs
):
    came_refs, out_ref = refs[: len(there[0])], refs[-1]
    me = lax.axis_index("seq")
    rows, wide = query_ref.shape
    halo = (WMAX - 1) * BLK
    starts = list(range(0, rows, 2 * BLK))
    sizes = [min(2 * BLK, rows - start) for start in starts]
    out_ref[:, wide:] = own_ref[...]
    for peer, came_ref in zip(peers_of(there, 0), came_refs):
        lanes = pl.ds(pl.multiple_of(peer * HD, HD), HD)
        width = came_ref[rows:, :].astype(jnp.float32)[:1]
        width = jnp.concatenate([width] * ((2 * BLK + halo) // LANES), axis=1)
        all_scores, all_values = [], []
        for start, size in zip(starts, sizes):
            query = query_ref[start : start + size, lanes]
            if start < halo:
                keys = [halo_ref[0, start:, lanes], key_ref[: start + size, lanes]]
                values = [halo_ref[1, start:, lanes], value_ref[: start + size, lanes]]
                keys, values = jnp.concatenate(keys, axis=0), jnp.concatenate(values, axis=0)
            else:
                keys = key_ref[start - halo : start + size, lanes]
                values = value_ref[start - halo : start + size, lanes]
            scores = scores_of(query, keys)
            row_at = lax.broadcasted_iota(jnp.int32, scores.shape, 0)
            lane_at = lax.broadcasted_iota(jnp.int32, scores.shape, 1)
            slot = (lane_at // BLK - row_at // BLK).astype(jnp.float32)
            allowed = (lane_at <= row_at + halo) & (slot + width[:, : size + halo] >= WMAX)
            if start < halo:
                closed = jnp.where(me == 0, halo - start, 0)
                allowed = allowed & (lane_at >= closed)
            all_scores.append(jnp.where(allowed, scores, MASKED))
            all_values.append(values)
        parts, lses = softmax_parts(all_scores, all_values)
        tile = stat_tile([as_row(lse, 0) for lse in lses])
        for start, size, part in zip(starts, sizes, parts):
            out_ref[start : start + size, lanes] = part
        out_ref[rows:, lanes] = tile


def merge_kernel(there, *refs):
    far_refs, out_ref = refs[:-1], refs[-1]
    own = len(far_refs) - 1
    near_ref = far_refs[own]
    rows, wide = out_ref.shape
    count = stat_count(rows)
    for index, (peer, far_ref) in enumerate(zip(peers_of(there, -1), far_refs)):
        part = slice(wide, None) if index == own else slice(None)
        lanes = pl.ds(pl.multiple_of(peer * HD, HD), HD)
        far_stats = stat_rows_of(far_ref[rows:, part], count)
        near_stats = stat_rows_of(near_ref[rows:, lanes], count)
        for group in range(count):
            start = group * LANES
            size = min(LANES, rows - start)
            share = 1.0 / (1.0 + jnp.exp2(near_stats[group] - far_stats[group]))
            row_at = lax.broadcasted_iota(jnp.int32, (size, LANES), 0)
            lane_at = lax.broadcasted_iota(jnp.int32, (size, LANES), 1)
            column = jnp.sum(
                jnp.where(row_at == lane_at, share, 0.0), axis=1, keepdims=True
            )
            far = far_ref[start : start + size, part].astype(jnp.float32)
            near = near_ref[start : start + size, lanes].astype(jnp.float32)
            out_ref[start : start + size, lanes] = (
                far * column + near * (1.0 - column)
            ).astype(jnp.bfloat16)


def params(shard):
    return pltpu.CompilerParams(vmem_limit_bytes=VMEM_BASE + 14 * 2 * math.prod(shard.shape))


def per_device(
    queries, keys_new, values_new, keys_cache, values_cache, window, global_blocks, random_blocks
):
    section_count = lax.axis_size("section")
    seq_count = lax.axis_size("seq")
    rows, wide = queries.shape[1], queries.shape[2]
    halo = (WMAX - 1) * BLK
    heads = wide // HD
    bf16 = jnp.bfloat16
    half = max(seq_count // 2, 1)
    inner, outer = list(range(1, half)), list(range(seq_count - 1, half - 1, -1))
    there = [outer + inner + [0], inner + outer + [0]]

    sent = pl.pallas_call(
        functools.partial(split_kernel, there),
        out_shape=[jax.ShapeDtypeStruct((rows + STAT_ROWS, HD), bf16)] * seq_count,
        in_specs=[whole_smem, in_hbm],
        out_specs=[whole_vmem] * seq_count,
        scratch_shapes=[pltpu.SemaphoreType.DMA((seq_count,))],
        compiler_params=params(queries),
        cost_estimate=pl.CostEstimate(flops=0, bytes_accessed=5 * rows * wide, transcendentals=0),
        name="split",
    )(window[0], queries[0])

    def linked(shard, by, steps):
        pairs = [
            (
                s * seq_count + t,
                (s + by) % section_count * seq_count + (t ^ steps[s % 2]),
            )
            for s in range(section_count)
            for t in range(seq_count)
        ]
        return lax.ppermute(shard, ("section", "seq"), pairs)

    came = [linked(shard, 0, steps) for shard, steps in zip(sent[:-1], zip(*there))]
    came.append(sent[-1])
    mine = jnp.stack([keys_new[0, rows - halo :], values_new[0, rows - halo :]])
    before = lax.ppermute(mine, "seq", [(i, i + 1) for i in range(seq_count - 1)])

    picks = random_blocks[0].reshape(-1)

    def far_call():
        count = seq_count
        out_rows = rows + STAT_ROWS
        return pl.pallas_call(
            functools.partial(far_kernel, there),
            out_shape=[jax.ShapeDtypeStruct((out_rows, HD), bf16)] * count,
            in_specs=[whole_smem] * 3 + [whole_vmem] * (2 + count),
            out_specs=[whole_vmem] * count,
            compiler_params=params(queries),
            cost_estimate=pl.CostEstimate(
                flops=40 * count * rows * 320 * HD * 4,
                bytes_accessed=2 * 2 * keys_cache.shape[1] * HD + 4 * count * rows * HD,
                transcendentals=count * rows * 320,
            ),
            name="far",
        )(
            window[0],
            global_blocks[0],
            picks,
            keys_cache[0],
            values_cache[0],
            *came,
        )

    far = far_call()
    ahead = min(3, seq_count - 1)
    handed = [linked(shard, 1, steps) for shard, steps in zip(far[:-1], zip(*there))]
    both = pl.pallas_call(
        functools.partial(near_kernel, there),
        out_shape=jax.ShapeDtypeStruct((rows + STAT_ROWS, wide + HD), bf16),
        in_specs=[whole_vmem] * (5 + seq_count) + [anywhere] * ahead,
        out_specs=whole_vmem,
        compiler_params=params(queries),
        cost_estimate=pl.CostEstimate(
            flops=40 * heads * rows * 256 * HD * 4,
            bytes_accessed=9 * rows * wide,
            transcendentals=heads * rows * 256,
        ),
        name="near",
    )(
        queries[0],
        keys_new[0],
        values_new[0],
        before,
        far[-1],
        *came,
        *handed[:ahead],
    )

    handed.append(linked(both, 1, [0, 0]))

    merged = pl.pallas_call(
        functools.partial(merge_kernel, there),
        out_shape=jax.ShapeDtypeStruct((rows, wide), bf16),
        in_specs=[whole_vmem] * seq_count,
        out_specs=whole_vmem,
        compiler_params=params(queries),
        cost_estimate=pl.CostEstimate(flops=0, bytes_accessed=6 * rows * wide, transcendentals=0),
        name="merge",
    )(*handed)
    return merged[None]


def solution(mesh):
    placed = (
        P("section", "seq", None),
        P("section", "seq", None),
        P("section", "seq", None),
        P("section", None, "seq"),
        P("section", None, "seq"),
        P("section", "seq"),
        P("section", None),
        P("section", None, None),
    )
    return jax.shard_map(
        per_device, mesh=mesh, in_specs=placed, out_specs=P("section", "seq", None), check_vma=False
    )
```

```python
import functools
import math

import jax
import jax.numpy as jnp
from jax import lax
from jax.experimental import pallas as pl
from jax.experimental.pallas import tpu as pltpu
from jax.sharding import PartitionSpec as P

HD = 128
BLK = 64
WMAX = 3
GLOB = 2
RAND = 3
LANES = 128
STAT_ROWS = 16
MASKED = -1e30
EXPO_SCALE = math.log2(math.e) / math.sqrt(HD)
VMEM_BASE = 12 * 1024 * 1024

whole_vmem = pl.BlockSpec(memory_space=pltpu.VMEM)
anywhere = pl.BlockSpec(memory_space=pl.ANY)
in_hbm = pl.BlockSpec(memory_space=pltpu.HBM)
whole_smem = pl.BlockSpec(memory_space=pltpu.SMEM)


def peers_of(there, by):
    count = lax.axis_size("section")
    other = lax.rem(lax.axis_index("section") + (by + count), count)
    odd = lax.rem(other, 2) == 1
    me = lax.axis_index("seq")
    return [
        jnp.bitwise_xor(me, jnp.where(odd, odd_step, even_step))
        for even_step, odd_step in zip(*there)
    ]


def scores_of(query, keys):
    return lax.dot_general(
        query, keys, (((1,), (1,)), ((), ())), preferred_element_type=jnp.float32
    )


def softmax_parts(scores, values):
    tops = [jnp.max(score, axis=1, keepdims=True) for score in scores]
    expos = [jnp.exp2((score - top) * EXPO_SCALE) for score, top in zip(scores, tops)]
    totals = [jnp.sum(expo, axis=1, keepdims=True) for expo in expos]
    mixed = [
        jnp.dot(expo.astype(jnp.bfloat16), value, preferred_element_type=jnp.float32)
        for expo, value in zip(expos, values)
    ]
    parts = [(mix * (1.0 / total)).astype(jnp.bfloat16) for mix, total in zip(mixed, totals)]
    lses = [top * EXPO_SCALE + jnp.log2(total) for top, total in zip(tops, totals)]
    return parts, lses


def as_row(column, offset):
    shape = (column.shape[0], LANES)
    row_at = lax.broadcasted_iota(jnp.int32, shape, 0)
    lane_at = lax.broadcasted_iota(jnp.int32, shape, 1)
    spread = jnp.where(lane_at == row_at + offset, column, 0.0)
    return jnp.sum(spread, axis=0, keepdims=True)


def stat_tile(rows):
    at = lax.broadcasted_iota(jnp.int32, (STAT_ROWS, LANES), 0)
    tile = jnp.zeros((STAT_ROWS, LANES), jnp.float32)
    count = len(rows)
    for index, row in enumerate(rows):
        high = row.astype(jnp.bfloat16).astype(jnp.float32)
        middle = (row - high).astype(jnp.bfloat16).astype(jnp.float32)
        low = row - high - middle
        for part, value in enumerate((high, middle, low)):
            tile = jnp.where(at == part * count + index, value, tile)
    return tile.astype(jnp.bfloat16)


def stat_rows_of(tile, count):
    wide = tile.astype(jnp.float32)
    return [
        wide[index : index + 1]
        + wide[count + index : count + index + 1]
        + wide[2 * count + index : 2 * count + index + 1]
        for index in range(count)
    ]


def stat_count(rows):
    return -(-rows // LANES)


def split_kernel(there, span_ref, query_ref, *refs):
    out_refs, arrived = refs[:-1], refs[-1]
    rows = query_ref.shape[0]
    copies = []
    for peer, out_ref in zip(peers_of(there, 0), out_refs):
        head = pl.multiple_of(peer * HD, HD)
        copies.append((query_ref.at[:, pl.ds(head, HD)], out_ref.at[:rows]))
    copies = [
        pltpu.make_async_copy(source, target, arrived.at[index])
        for index, (source, target) in enumerate(copies)
    ]
    for copy in copies:
        copy.start()
    width = jnp.full((STAT_ROWS, HD), span_ref[0].astype(jnp.float32)).astype(jnp.bfloat16)
    for out_ref in out_refs:
        out_ref[rows:, :] = width
    for copy in copies:
        copy.wait()


def far_kernel(
    there, span_ref, global_ref, random_ref, key_ref, value_ref, *refs
):
    span = span_ref[0]
    last = key_ref.shape[0] // BLK - 1

    def block(ref, at):
        if isinstance(at, int):
            return ref[at * BLK : (at + 1) * BLK, :]
        return ref[pl.ds(pl.multiple_of(at * BLK, BLK), BLK), :]

    glob_keys = [block(key_ref, global_ref[g]) for g in range(GLOB)]
    glob_values = [block(value_ref, global_ref[g]) for g in range(GLOB)]
    peers = peers_of(there, 0)
    query_refs, out_refs = refs[: len(peers)], refs[len(peers) :]
    rows = query_refs[0].shape[0] - STAT_ROWS
    for chunk, query_ref, out_ref in zip(peers, query_refs, out_refs):
        blocks = rows // BLK
        first = chunk == 0
        all_scores, all_picks = [], []
        for b in range(blocks):
            query = query_ref[b * BLK : (b + 1) * BLK, :]
            base = (chunk * blocks + b) * RAND
            picks = [random_ref[base + r] for r in range(RAND)]
            keys = glob_keys + [block(key_ref, pick) for pick in picks]
            known = len(keys) * BLK
            spare = [last + 1 + b - w for w in range(b + 1, WMAX)]
            keys = keys + [block(key_ref, at) for at in spare]
            scores = scores_of(query, jnp.concatenate(keys, axis=0))
            if spare:
                open_slots = jnp.where(first, jnp.clip(span - (b + 1), 0, len(spare)), 0)
                lane_at = lax.broadcasted_iota(jnp.int32, scores.shape, 1)
                scores = jnp.where(lane_at < known + open_slots * BLK, scores, MASKED)
            all_scores.append(scores)
            all_picks.append(picks + spare)
        all_values = [
            jnp.concatenate(glob_values + [block(value_ref, at) for at in picks], axis=0)
            for picks in all_picks
        ]
        parts, lses = softmax_parts(all_scores, all_values)
        stats = []
        for b in range(blocks):
            row = as_row(lses[b], (b * BLK) % LANES)
            if (b * BLK) % LANES:
                stats[-1] = stats[-1] + row
            else:
                stats.append(row)
        tile = stat_tile(stats)
        for b in range(blocks):
            out_ref[b * BLK : (b + 1) * BLK, :] = parts[b]
        out_ref[rows:, :] = tile


def near_rows(
    there, first, last, query_ref, key_ref, value_ref, halo_ref, came_refs, out_ref
):
    rows = query_ref.shape[0]
    halo = (WMAX - 1) * BLK
    starts = list(range(first, last, 2 * BLK))
    sizes = [min(2 * BLK, last - start) for start in starts]
    for peer, came_ref in zip(peers_of(there, 0), came_refs):
        lanes = pl.ds(pl.multiple_of(peer * HD, HD), HD)
        width = came_ref[rows:, :].astype(jnp.float32)[:1]
        width = jnp.concatenate([width] * ((2 * BLK + halo) // LANES), axis=1)
        all_scores, all_values = [], []
        for start, size in zip(starts, sizes):
            query = query_ref[start : start + size, lanes]
            if start < halo:
                keys = [halo_ref[0, start:, lanes], key_ref[: start + size, lanes]]
                values = [halo_ref[1, start:, lanes], value_ref[: start + size, lanes]]
                keys, values = jnp.concatenate(keys, axis=0), jnp.concatenate(values, axis=0)
            else:
                keys = key_ref[start - halo : start + size, lanes]
                values = value_ref[start - halo : start + size, lanes]
            scores = scores_of(query, keys)
            row_at = lax.broadcasted_iota(jnp.int32, scores.shape, 0)
            lane_at = lax.broadcasted_iota(jnp.int32, scores.shape, 1)
            slot = (lane_at // BLK - row_at // BLK).astype(jnp.float32)
            allowed = (lane_at <= row_at + halo) & (slot + width[:, : size + halo] >= WMAX)
            if start < halo:
                closed = jnp.where(lax.axis_index("seq") == 0, halo - start, 0)
                allowed = allowed & (lane_at >= closed)
            all_scores.append(jnp.where(allowed, scores, MASKED))
            all_values.append(values)
        parts, lses = softmax_parts(all_scores, all_values)
        tile = stat_tile([as_row(lse, 0) for lse in lses])
        for start, size, part in zip(starts, sizes, parts):
            out_ref[start - first : start - first + size, lanes] = part
        out_ref[last - first : last - first + STAT_ROWS, lanes] = tile


def packed_at(index, first, wide):
    across = wide // HD
    row, lane = first + index // across * STAT_ROWS, index % across * HD
    return slice(row, row + STAT_ROWS), slice(lane, lane + HD)


def near_inner_kernel(there, query_ref, key_ref, value_ref, own_ref, *refs):
    rows, wide = query_ref.shape
    halo = (WMAX - 1) * BLK
    came_refs, out_ref = refs[:-1], refs[-1]
    near_rows(there, halo, rows, query_ref, key_ref, value_ref, None, came_refs, out_ref)
    for index in range(own_ref.shape[0] // STAT_ROWS):
        at = packed_at(index, rows - halo + STAT_ROWS, wide)
        out_ref[at] = own_ref[index * STAT_ROWS : (index + 1) * STAT_ROWS, :]


def near_edge_kernel(there, query_ref, key_ref, value_ref, halo_ref, *refs):
    halo = (WMAX - 1) * BLK
    came_refs, out_ref = refs[: len(there[0])], refs[-1]
    near_rows(there, 0, halo, query_ref, key_ref, value_ref, halo_ref, came_refs, out_ref)


def merge_kernel(there, edge_ref, inner_ref, *refs):
    far_refs, out_ref, own_ref = refs[:-2], refs[-2], refs[-1]
    rows, wide = out_ref.shape
    halo = (WMAX - 1) * BLK
    for index in range(own_ref.shape[0] // STAT_ROWS):
        at = packed_at(index, rows - halo + STAT_ROWS, wide)
        own_ref[index * STAT_ROWS : (index + 1) * STAT_ROWS, :] = inner_ref[at]
    count = stat_count(rows)
    for peer, far_ref in zip(peers_of(there, -1), (*far_refs, own_ref)):
        lanes = pl.ds(pl.multiple_of(peer * HD, HD), HD)
        far_stats = stat_rows_of(far_ref[rows:, :], count)
        near_stats = stat_rows_of(edge_ref[halo:, lanes], 1) + stat_rows_of(
            inner_ref[rows - halo : rows - halo + STAT_ROWS, lanes], count - 1
        )
        for group in range(count):
            start = group * LANES
            size = min(LANES, rows - start)
            share = 1.0 / (1.0 + jnp.exp2(near_stats[group] - far_stats[group]))
            row_at = lax.broadcasted_iota(jnp.int32, (size, LANES), 0)
            lane_at = lax.broadcasted_iota(jnp.int32, (size, LANES), 1)
            column = jnp.sum(
                jnp.where(row_at == lane_at, share, 0.0), axis=1, keepdims=True
            )
            far = far_ref[start : start + size, :].astype(jnp.float32)
            if start < halo:
                near = edge_ref[start : start + size, lanes].astype(jnp.float32)
            else:
                near = inner_ref[start - halo : start - halo + size, lanes].astype(jnp.float32)
            out_ref[start : start + size, lanes] = (
                far * column + near * (1.0 - column)
            ).astype(jnp.bfloat16)


def params(shard):
    return pltpu.CompilerParams(vmem_limit_bytes=VMEM_BASE + 14 * 2 * math.prod(shard.shape))


def per_device(
    queries, keys_new, values_new, keys_cache, values_cache, window, global_blocks, random_blocks
):
    section_count = lax.axis_size("section")
    seq_count = lax.axis_size("seq")
    rows, wide = queries.shape[1], queries.shape[2]
    halo = (WMAX - 1) * BLK
    heads = wide // HD
    bf16 = jnp.bfloat16
    half = max(seq_count // 2, 1)
    inner, outer = list(range(1, half)), list(range(seq_count - 1, half - 1, -1))
    there = [outer + inner + [0], inner + outer + [0]]

    chunk_shape = jax.ShapeDtypeStruct((rows + STAT_ROWS, HD), bf16)
    chunk_shape = jax.ShapeDtypeStruct((rows + STAT_ROWS, HD), bf16)
    sent = pl.pallas_call(
        functools.partial(split_kernel, there),
        out_shape=[chunk_shape] * seq_count,
        in_specs=[whole_smem, in_hbm],
        out_specs=[whole_vmem] * seq_count,
        scratch_shapes=[pltpu.SemaphoreType.DMA((seq_count,))],
        compiler_params=params(queries),
        cost_estimate=pl.CostEstimate(flops=0, bytes_accessed=5 * rows * wide, transcendentals=0),
        name="split",
    )(window[0], queries[0])

    def linked(shard, by, steps):
        pairs = [
            (
                s * seq_count + t,
                (s + by) % section_count * seq_count + (t ^ steps[s % 2]),
            )
            for s in range(section_count)
            for t in range(seq_count)
        ]
        return lax.ppermute(shard, ("section", "seq"), pairs)

    came = [linked(shard, 0, steps) for shard, steps in zip(sent[:-1], zip(*there))]
    came.append(sent[-1])
    mine = jnp.stack([keys_new[0, rows - halo :], values_new[0, rows - halo :]])
    before = lax.ppermute(mine, "seq", [(i, i + 1) for i in range(seq_count - 1)])

    picks = random_blocks[0].reshape(-1)

    far = pl.pallas_call(
        functools.partial(far_kernel, there),
        out_shape=[chunk_shape] * seq_count,
        in_specs=[whole_smem] * 3 + [whole_vmem] * (2 + seq_count),
        out_specs=[whole_vmem] * seq_count,
        compiler_params=params(queries),
        cost_estimate=pl.CostEstimate(
            flops=40 * seq_count * rows * 320 * HD * 4,
            bytes_accessed=2 * 2 * keys_cache.shape[1] * HD + 4 * seq_count * rows * HD,
            transcendentals=seq_count * rows * 320,
        ),
        name="far",
    )(window[0], global_blocks[0], picks, keys_cache[0], values_cache[0], *came)
    handed = [linked(shard, 1, steps) for shard, steps in zip(far[:-1], zip(*there))]

    def near_call(kernel, name, near_part, out_rows, *operands):
        return pl.pallas_call(
            functools.partial(kernel, there),
            out_shape=jax.ShapeDtypeStruct((out_rows, wide), bf16),
            in_specs=[
                whole_vmem if index < 4 + seq_count else anywhere
                for index in range(3 + len(operands))
            ],
            out_specs=whole_vmem,
            compiler_params=params(queries),
            cost_estimate=pl.CostEstimate(
                flops=40 * heads * near_part * 256 * HD * 4,
                bytes_accessed=9 * near_part * wide,
                transcendentals=heads * near_part * 256,
            ),
            name=name,
        )(queries[0], keys_new[0], values_new[0], *operands)

    packed_rows = -(-(rows + STAT_ROWS) // (STAT_ROWS * heads)) * STAT_ROWS
    inner_part = near_call(
        near_inner_kernel, "near_inner", rows - halo, rows - halo + STAT_ROWS + packed_rows,
        far[-1], *came,
    )
    edge_part = near_call(
        near_edge_kernel, "near_edge", halo, halo + STAT_ROWS, before, *came, *handed[:2]
    )
    handed_inner = linked(inner_part, 1, [0, 0])
    handed_edge = linked(edge_part, 1, [0, 0])

    merged = pl.pallas_call(
        functools.partial(merge_kernel, there),
        out_shape=jax.ShapeDtypeStruct((rows, wide), bf16),
        in_specs=[whole_vmem] * (1 + seq_count),
        out_specs=whole_vmem,
        scratch_shapes=[pltpu.VMEM(chunk_shape.shape, bf16)],
        compiler_params=params(queries),
        cost_estimate=pl.CostEstimate(flops=0, bytes_accessed=6 * rows * wide, transcendentals=0),
        name="merge",
    )(handed_edge, handed_inner, *handed)
    return merged[None]


def solution(mesh):
    placed = (
        P("section", "seq", None),
        P("section", "seq", None),
        P("section", "seq", None),
        P("section", None, "seq"),
        P("section", None, "seq"),
        P("section", "seq"),
        P("section", None),
        P("section", None, None),
    )
    return jax.shard_map(
        per_device, mesh=mesh, in_specs=placed, out_specs=P("section", "seq", None), check_vma=False
    )
```

```python
import functools
import math

import jax
import jax.numpy as jnp
from jax import lax
from jax.experimental import pallas as pl
from jax.experimental.pallas import tpu as pltpu
from jax.sharding import PartitionSpec as P

HD = 128
BLK = 64
WMAX = 3
GLOB = 2
RAND = 3
LANES = 128
STAT_ROWS = 16
MASKED = -1e30
EXPO_SCALE = math.log2(math.e) / math.sqrt(HD)
VMEM_BASE = 12 * 1024 * 1024

whole_vmem = pl.BlockSpec(memory_space=pltpu.VMEM)
anywhere = pl.BlockSpec(memory_space=pl.ANY)
in_hbm = pl.BlockSpec(memory_space=pltpu.HBM)
whole_smem = pl.BlockSpec(memory_space=pltpu.SMEM)


def peers_of(there, by):
    count = lax.axis_size("section")
    other = lax.rem(lax.axis_index("section") + (by + count), count)
    odd = lax.rem(other, 2) == 1
    me = lax.axis_index("seq")
    return [
        jnp.bitwise_xor(me, jnp.where(odd, odd_step, even_step))
        for even_step, odd_step in zip(*there)
    ]


def scores_of(query, keys):
    return lax.dot_general(
        query, keys, (((1,), (1,)), ((), ())), preferred_element_type=jnp.float32
    )


def softmax_parts(scores, values):
    tops = [jnp.max(score, axis=1, keepdims=True) for score in scores]
    expos = [jnp.exp2((score - top) * EXPO_SCALE) for score, top in zip(scores, tops)]
    totals = [jnp.sum(expo, axis=1, keepdims=True) for expo in expos]
    mixed = [
        jnp.dot(expo.astype(jnp.bfloat16), value, preferred_element_type=jnp.float32)
        for expo, value in zip(expos, values)
    ]
    parts = [(mix * (1.0 / total)).astype(jnp.bfloat16) for mix, total in zip(mixed, totals)]
    lses = [top * EXPO_SCALE + jnp.log2(total) for top, total in zip(tops, totals)]
    return parts, lses


def as_row(column, offset):
    shape = (column.shape[0], LANES)
    row_at = lax.broadcasted_iota(jnp.int32, shape, 0)
    lane_at = lax.broadcasted_iota(jnp.int32, shape, 1)
    spread = jnp.where(lane_at == row_at + offset, column, 0.0)
    return jnp.sum(spread, axis=0, keepdims=True)


def stat_tile(rows):
    at = lax.broadcasted_iota(jnp.int32, (STAT_ROWS, LANES), 0)
    tile = jnp.zeros((STAT_ROWS, LANES), jnp.float32)
    count = len(rows)
    for index, row in enumerate(rows):
        high = row.astype(jnp.bfloat16).astype(jnp.float32)
        middle = (row - high).astype(jnp.bfloat16).astype(jnp.float32)
        low = row - high - middle
        for part, value in enumerate((high, middle, low)):
            tile = jnp.where(at == part * count + index, value, tile)
    return tile.astype(jnp.bfloat16)


def stat_rows_of(tile, count):
    wide = tile.astype(jnp.float32)
    return [
        wide[index : index + 1]
        + wide[count + index : count + index + 1]
        + wide[2 * count + index : 2 * count + index + 1]
        for index in range(count)
    ]


def stat_count(rows):
    return -(-rows // LANES)


def split_kernel(there, span_ref, query_ref, *refs):
    out_refs, arrived = refs[:-1], refs[-1]
    rows = query_ref.shape[0]
    copies = []
    for peer, out_ref in zip(peers_of(there, 0), out_refs):
        head = pl.multiple_of(peer * HD, HD)
        copies.append((query_ref.at[:, pl.ds(head, HD)], out_ref.at[:rows]))
    copies = [
        pltpu.make_async_copy(source, target, arrived.at[index])
        for index, (source, target) in enumerate(copies)
    ]
    for copy in copies:
        copy.start()
    width = jnp.full((STAT_ROWS, HD), span_ref[0].astype(jnp.float32)).astype(jnp.bfloat16)
    for out_ref in out_refs:
        out_ref[rows:, :] = width
    for copy in copies:
        copy.wait()


def halo_kernel(rows_ref, _, out_ref):
    out_ref[...] = rows_ref[...]


def far_kernel(
    there, chosen, span_ref, global_ref, random_ref, key_ref, value_ref, *refs
):
    span = span_ref[0]
    last = key_ref.shape[0] // BLK - 1

    def block(ref, at):
        if isinstance(at, int):
            return ref[at * BLK : (at + 1) * BLK, :]
        return ref[pl.ds(pl.multiple_of(at * BLK, BLK), BLK), :]

    glob_keys = [block(key_ref, global_ref[g]) for g in range(GLOB)]
    glob_values = [block(value_ref, global_ref[g]) for g in range(GLOB)]
    peers = [peers_of(there, 0)[at] for at in chosen]
    query_refs, out_refs = refs[: len(peers)], refs[len(peers) :]
    rows = query_refs[0].shape[0] - STAT_ROWS
    for chunk, query_ref, out_ref in zip(peers, query_refs, out_refs):
        blocks = rows // BLK
        first = chunk == 0
        all_scores, all_picks = [], []
        for b in range(blocks):
            query = query_ref[b * BLK : (b + 1) * BLK, :]
            base = (chunk * blocks + b) * RAND
            picks = [random_ref[base + r] for r in range(RAND)]
            keys = glob_keys + [block(key_ref, pick) for pick in picks]
            known = len(keys) * BLK
            spare = [last + 1 + b - w for w in range(b + 1, WMAX)]
            keys = keys + [block(key_ref, at) for at in spare]
            scores = scores_of(query, jnp.concatenate(keys, axis=0))
            if spare:
                open_slots = jnp.where(first, jnp.clip(span - (b + 1), 0, len(spare)), 0)
                lane_at = lax.broadcasted_iota(jnp.int32, scores.shape, 1)
                scores = jnp.where(lane_at < known + open_slots * BLK, scores, MASKED)
            all_scores.append(scores)
            all_picks.append(picks + spare)
        all_values = [
            jnp.concatenate(glob_values + [block(value_ref, at) for at in picks], axis=0)
            for picks in all_picks
        ]
        parts, lses = softmax_parts(all_scores, all_values)
        stats = []
        for b in range(blocks):
            row = as_row(lses[b], (b * BLK) % LANES)
            if (b * BLK) % LANES:
                stats[-1] = stats[-1] + row
            else:
                stats.append(row)
        tile = stat_tile(stats)
        for b in range(blocks):
            out_ref[b * BLK : (b + 1) * BLK, :] = parts[b]
        out_ref[rows:, :] = tile


def near_rows(
    there, first, last, query_ref, key_ref, value_ref, halo_ref, came_refs, out_ref
):
    rows = query_ref.shape[0]
    halo = (WMAX - 1) * BLK
    starts = list(range(first, last, 2 * BLK))
    sizes = [min(2 * BLK, last - start) for start in starts]
    leads = [
        halo if start < halo else min(-(-(size + halo) // LANES) * LANES - size, start)
        for start, size in zip(starts, sizes)
    ]
    peers = peers_of(there, 0)
    for begin in range(0, len(peers), 2):
        pair = range(begin, min(begin + 2, len(peers)))
        all_lanes = [pl.ds(pl.multiple_of(peers[at] * HD, HD), HD) for at in pair]
        all_scores, all_values = [], []
        for at, lanes in zip(pair, all_lanes):
            width = came_refs[at][rows:, :].astype(jnp.float32)[:1]
            width = jnp.concatenate([width] * ((2 * BLK + halo) // LANES), axis=1)
            for start, size, lead in zip(starts, sizes, leads):
                query = query_ref[start : start + size, lanes]
                if start < lead:
                    keys = [halo_ref[0, start:, lanes], key_ref[: start + size, lanes]]
                    values = [halo_ref[1, start:, lanes], value_ref[: start + size, lanes]]
                    keys, values = jnp.concatenate(keys, axis=0), jnp.concatenate(values, axis=0)
                else:
                    keys = key_ref[start - lead : start + size, lanes]
                    values = value_ref[start - lead : start + size, lanes]
                scores = scores_of(query, keys)
                row_at = lax.broadcasted_iota(jnp.int32, scores.shape, 0)
                lane_at = lax.broadcasted_iota(jnp.int32, scores.shape, 1)
                slot = (lane_at // BLK - row_at // BLK - lead // BLK).astype(jnp.float32)
                allowed = (lane_at <= row_at + lead) & (slot + width[:, : size + lead] >= 1.0)
                if start < lead:
                    closed = jnp.where(lax.axis_index("seq") == 0, lead - start, 0)
                    allowed = allowed & (lane_at >= closed)
                all_scores.append(jnp.where(allowed, scores, MASKED))
                all_values.append(values)
        parts, lses = softmax_parts(all_scores, all_values)
        for index, lanes in enumerate(all_lanes):
            own = slice(index * len(starts), (index + 1) * len(starts))
            tile = stat_tile([as_row(lse, 0) for lse in lses[own]])
            for start, size, part in zip(starts, sizes, parts[own]):
                out_ref[start - first : start - first + size, lanes] = part
            out_ref[last - first : last - first + STAT_ROWS, lanes] = tile


def packed_at(index, first, wide):
    across = wide // HD
    row, lane = first + index // across * STAT_ROWS, index % across * HD
    return slice(row, row + STAT_ROWS), slice(lane, lane + HD)


def near_inner_kernel(there, query_ref, key_ref, value_ref, own_ref, *refs):
    rows, wide = query_ref.shape
    halo = (WMAX - 1) * BLK
    came_refs, out_ref = refs[:-1], refs[-1]
    near_rows(there, halo, rows, query_ref, key_ref, value_ref, None, came_refs, out_ref)
    for index in range(own_ref.shape[0] // STAT_ROWS):
        at = packed_at(index, rows - halo + STAT_ROWS, wide)
        out_ref[at] = own_ref[index * STAT_ROWS : (index + 1) * STAT_ROWS, :]


def near_edge_kernel(there, query_ref, key_ref, value_ref, halo_ref, *refs):
    halo = (WMAX - 1) * BLK
    came_refs, out_ref = refs[: len(there[0])], refs[-1]
    near_rows(there, 0, halo, query_ref, key_ref, value_ref, halo_ref, came_refs, out_ref)


def merge_kernel(there, edge_ref, inner_ref, *refs):
    far_refs, out_ref, own_ref = refs[:-2], refs[-2], refs[-1]
    rows, wide = out_ref.shape
    halo = (WMAX - 1) * BLK
    for index in range(own_ref.shape[0] // STAT_ROWS):
        at = packed_at(index, rows - halo + STAT_ROWS, wide)
        own_ref[index * STAT_ROWS : (index + 1) * STAT_ROWS, :] = inner_ref[at]
    count = stat_count(rows)
    for peer, far_ref in zip(peers_of(there, -1), (*far_refs, own_ref)):
        lanes = pl.ds(pl.multiple_of(peer * HD, HD), HD)
        far_stats = stat_rows_of(far_ref[rows:, :], count)
        near_stats = stat_rows_of(edge_ref[halo:, lanes], 1) + stat_rows_of(
            inner_ref[rows - halo : rows - halo + STAT_ROWS, lanes], count - 1
        )
        for group in range(count):
            start = group * LANES
            size = min(LANES, rows - start)
            share = 1.0 / (1.0 + jnp.exp2(near_stats[group] - far_stats[group]))
            row_at = lax.broadcasted_iota(jnp.int32, (size, LANES), 0)
            lane_at = lax.broadcasted_iota(jnp.int32, (size, LANES), 1)
            column = jnp.sum(
                jnp.where(row_at == lane_at, share, 0.0), axis=1, keepdims=True
            )
            far = far_ref[start : start + size, :].astype(jnp.float32)
            if start < halo:
                near = edge_ref[start : start + size, lanes].astype(jnp.float32)
            else:
                near = inner_ref[start - halo : start - halo + size, lanes].astype(jnp.float32)
            out_ref[start : start + size, lanes] = (
                far * column + near * (1.0 - column)
            ).astype(jnp.bfloat16)


def params(shard):
    return pltpu.CompilerParams(vmem_limit_bytes=VMEM_BASE + 14 * 2 * math.prod(shard.shape))


def per_device(
    queries, keys_new, values_new, keys_cache, values_cache, window, global_blocks, random_blocks
):
    section_count = lax.axis_size("section")
    seq_count = lax.axis_size("seq")
    rows, wide = queries.shape[1], queries.shape[2]
    halo = (WMAX - 1) * BLK
    heads = wide // HD
    bf16 = jnp.bfloat16
    half = max(seq_count // 2, 1)
    inner, outer = list(range(1, half)), list(range(seq_count - 1, half - 1, -1))
    there = [outer + inner + [0], inner + outer + [0]]

    chunk_shape = jax.ShapeDtypeStruct((rows + STAT_ROWS, HD), bf16)
    chunk_shape = jax.ShapeDtypeStruct((rows + STAT_ROWS, HD), bf16)
    sent = pl.pallas_call(
        functools.partial(split_kernel, there),
        out_shape=[chunk_shape] * seq_count,
        in_specs=[whole_smem, in_hbm],
        out_specs=[whole_vmem] * seq_count,
        scratch_shapes=[pltpu.SemaphoreType.DMA((seq_count,))],
        compiler_params=params(queries),
        cost_estimate=pl.CostEstimate(flops=0, bytes_accessed=5 * rows * wide, transcendentals=0),
        name="split",
    )(window[0], queries[0])

    def linked(shard, by, steps):
        pairs = [
            (
                s * seq_count + t,
                (s + by) % section_count * seq_count + (t ^ steps[s % 2]),
            )
            for s in range(section_count)
            for t in range(seq_count)
        ]
        return lax.ppermute(shard, ("section", "seq"), pairs)

    came = [linked(shard, 0, steps) for shard, steps in zip(sent[:-1], zip(*there))]
    came.append(sent[-1])
    def linked(shard, by, steps):
        pairs = [
            (
                s * seq_count + t,
                (s + by) % section_count * seq_count + (t ^ steps[s % 2]),
            )
            for s in range(section_count)
            for t in range(seq_count)
        ]
        return lax.ppermute(shard, ("section", "seq"), pairs)

    came = [linked(shard, 0, steps) for shard, steps in zip(sent[:-1], zip(*there))]
    came.append(sent[-1])
    mine = pl.pallas_call(
        halo_kernel,
        out_shape=jax.ShapeDtypeStruct((2, halo, wide), bf16),
        in_specs=[whole_vmem, anywhere],
        out_specs=whole_vmem,
        compiler_params=params(queries),
        name="halo",
    )(jnp.stack([keys_new[0, rows - halo :], values_new[0, rows - halo :]]), came[0])
    before = lax.ppermute(mine, "seq", [(i, i + 1) for i in range(seq_count - 1)])

    picks = random_blocks[0].reshape(-1)

    def far_call(chosen):
        count = len(chosen)
        return pl.pallas_call(
            functools.partial(far_kernel, there, chosen),
            out_shape=[chunk_shape] * count,
            in_specs=[whole_smem] * 3 + [whole_vmem] * (2 + count),
            out_specs=[whole_vmem] * count,
            compiler_params=params(queries),
            cost_estimate=pl.CostEstimate(
                flops=40 * count * rows * 320 * HD * 4,
                bytes_accessed=2 * 2 * keys_cache.shape[1] * HD + 4 * count * rows * HD,
                transcendentals=count * rows * 320,
            ),
            name="far",
        )(
            window[0],
            global_blocks[0],
            picks,
            keys_cache[0],
            values_cache[0],
            *[came[at] for at in chosen],
        )

    late = list(range(seq_count - 1 - seq_count // 4, seq_count - 1))
    early = [at for at in range(seq_count) if at not in late]
    far = dict(zip(early, far_call(early)))
    if late:
        far.update(zip(late, far_call(late)))
    far = [far[at] for at in range(seq_count)]
    handed = [linked(shard, 1, steps) for shard, steps in zip(far[:-1], zip(*there))]

    def near_call(kernel, name, near_part, out_rows, *operands):
        return pl.pallas_call(
            functools.partial(kernel, there),
            out_shape=jax.ShapeDtypeStruct((out_rows, wide), bf16),
            in_specs=[
                whole_vmem if index < 4 + seq_count else anywhere
                for index in range(3 + len(operands))
            ],
            out_specs=whole_vmem,
            compiler_params=params(queries),
            cost_estimate=pl.CostEstimate(
                flops=40 * heads * near_part * 256 * HD * 4,
                bytes_accessed=9 * near_part * wide,
                transcendentals=heads * near_part * 256,
            ),
            name=name,
        )(queries[0], keys_new[0], values_new[0], *operands)

    packed_rows = -(-(rows + STAT_ROWS) // (STAT_ROWS * heads)) * STAT_ROWS
    inner_part = near_call(
        near_inner_kernel, "near_inner", rows - halo, rows - halo + STAT_ROWS + packed_rows,
        far[-1], *came,
    )
    edge_part = near_call(
        near_edge_kernel, "near_edge", halo, halo + STAT_ROWS, before, *came, *handed[:2]
    )
    handed_inner = linked(inner_part, 1, [0, 0])
    handed_edge = linked(edge_part, 1, [0, 0])

    merged = pl.pallas_call(
        functools.partial(merge_kernel, there),
        out_shape=jax.ShapeDtypeStruct((rows, wide), bf16),
        in_specs=[whole_vmem] * (1 + seq_count),
        out_specs=whole_vmem,
        scratch_shapes=[pltpu.VMEM(chunk_shape.shape, bf16)],
        compiler_params=params(queries),
        cost_estimate=pl.CostEstimate(flops=0, bytes_accessed=6 * rows * wide, transcendentals=0),
        name="merge",
    )(handed_edge, handed_inner, *handed)
    return merged[None]


def solution(mesh):
    placed = (
        P("section", "seq", None),
        P("section", "seq", None),
        P("section", "seq", None),
        P("section", None, "seq"),
        P("section", None, "seq"),
        P("section", "seq"),
        P("section", None),
        P("section", None, None),
    )
    return jax.shard_map(
        per_device, mesh=mesh, in_specs=placed, out_specs=P("section", "seq", None), check_vma=False
    )
```

```python
import functools
import math

import jax
import jax.numpy as jnp
from jax import lax
from jax.experimental import pallas as pl
from jax.experimental.pallas import tpu as pltpu
from jax.sharding import PartitionSpec as P

HD = 128
BLK = 64
WMAX = 3
GLOB = 2
RAND = 3
LANES = 128
STAT_ROWS = 16
MASKED = -1e30
EXPO_SCALE = math.log2(math.e) / math.sqrt(HD)
VMEM_BASE = 12 * 1024 * 1024

whole_vmem = pl.BlockSpec(memory_space=pltpu.VMEM)
anywhere = pl.BlockSpec(memory_space=pl.ANY)
in_hbm = pl.BlockSpec(memory_space=pltpu.HBM)
whole_smem = pl.BlockSpec(memory_space=pltpu.SMEM)


def peers_of(there, by):
    count = lax.axis_size("section")
    other = lax.rem(lax.axis_index("section") + (by + count), count)
    odd = lax.rem(other, 2) == 1
    me = lax.axis_index("seq")
    return [
        jnp.bitwise_xor(me, jnp.where(odd, odd_step, even_step))
        for even_step, odd_step in zip(*there)
    ]


def scores_of(query, keys):
    return lax.dot_general(
        query, keys, (((1,), (1,)), ((), ())), preferred_element_type=jnp.float32
    )


def softmax_parts(scores, values):
    tops = [jnp.max(score, axis=1, keepdims=True) for score in scores]
    expos = [jnp.exp2((score - top) * EXPO_SCALE) for score, top in zip(scores, tops)]
    totals = [jnp.sum(expo, axis=1, keepdims=True) for expo in expos]
    mixed = [
        jnp.dot(expo.astype(jnp.bfloat16), value, preferred_element_type=jnp.float32)
        for expo, value in zip(expos, values)
    ]
    parts = [(mix * (1.0 / total)).astype(jnp.bfloat16) for mix, total in zip(mixed, totals)]
    lses = [top * EXPO_SCALE + jnp.log2(total) for top, total in zip(tops, totals)]
    return parts, lses


def as_row(column, offset):
    shape = (column.shape[0], LANES)
    row_at = lax.broadcasted_iota(jnp.int32, shape, 0)
    lane_at = lax.broadcasted_iota(jnp.int32, shape, 1)
    spread = jnp.where(lane_at == row_at + offset, column, 0.0)
    return jnp.sum(spread, axis=0, keepdims=True)


def stat_tile(rows):
    at = lax.broadcasted_iota(jnp.int32, (STAT_ROWS, LANES), 0)
    tile = jnp.zeros((STAT_ROWS, LANES), jnp.float32)
    count = len(rows)
    for index, row in enumerate(rows):
        high = row.astype(jnp.bfloat16).astype(jnp.float32)
        middle = (row - high).astype(jnp.bfloat16).astype(jnp.float32)
        low = row - high - middle
        for part, value in enumerate((high, middle, low)):
            tile = jnp.where(at == part * count + index, value, tile)
    return tile.astype(jnp.bfloat16)


def stat_rows_of(tile, count):
    wide = tile.astype(jnp.float32)
    return [
        wide[index : index + 1]
        + wide[count + index : count + index + 1]
        + wide[2 * count + index : 2 * count + index + 1]
        for index in range(count)
    ]


def stat_count(rows):
    return -(-rows // LANES)


def split_kernel(there, span_ref, query_ref, *refs):
    out_refs, arrived = refs[:-1], refs[-1]
    rows = query_ref.shape[0]
    copies = []
    for peer, out_ref in zip(peers_of(there, 0), out_refs):
        head = pl.multiple_of(peer * HD, HD)
        copies.append((query_ref.at[:, pl.ds(head, HD)], out_ref.at[:rows]))
    copies = [
        pltpu.make_async_copy(source, target, arrived.at[index])
        for index, (source, target) in enumerate(copies)
    ]
    for copy in copies:
        copy.start()
    width = jnp.full((STAT_ROWS, HD), span_ref[0].astype(jnp.float32)).astype(jnp.bfloat16)
    for out_ref in out_refs:
        out_ref[rows:, :] = width
    for copy in copies:
        copy.wait()


def halo_kernel(rows_ref, _, out_ref):
    out_ref[...] = rows_ref[...]


def far_kernel(
    there, chosen, span_ref, global_ref, random_ref, key_ref, value_ref, *refs
):
    span = span_ref[0]
    last = key_ref.shape[0] // BLK - 1

    def block(ref, at):
        if isinstance(at, int):
            return ref[at * BLK : (at + 1) * BLK, :]
        return ref[pl.ds(pl.multiple_of(at * BLK, BLK), BLK), :]

    glob_keys = [block(key_ref, global_ref[g]) for g in range(GLOB)]
    glob_values = [block(value_ref, global_ref[g]) for g in range(GLOB)]
    peers = [peers_of(there, 0)[at] for at in chosen]
    query_refs, out_refs = refs[: len(peers)], refs[len(peers) :]
    rows = query_refs[0].shape[0] - STAT_ROWS
    for chunk, query_ref, out_ref in zip(peers, query_refs, out_refs):
        blocks = rows // BLK
        first = chunk == 0
        all_scores, all_picks = [], []
        for b in range(blocks):
            query = query_ref[b * BLK : (b + 1) * BLK, :]
            base = (chunk * blocks + b) * RAND
            picks = [random_ref[base + r] for r in range(RAND)]
            keys = glob_keys + [block(key_ref, pick) for pick in picks]
            known = len(keys) * BLK
            spare = [last + 1 + b - w for w in range(b + 1, WMAX)]
            keys = keys + [block(key_ref, at) for at in spare]
            scores = scores_of(query, jnp.concatenate(keys, axis=0))
            if spare:
                open_slots = jnp.where(first, jnp.clip(span - (b + 1), 0, len(spare)), 0)
                lane_at = lax.broadcasted_iota(jnp.int32, scores.shape, 1)
                scores = jnp.where(lane_at < known + open_slots * BLK, scores, MASKED)
            all_scores.append(scores)
            all_picks.append(picks + spare)
        all_values = [
            jnp.concatenate(glob_values + [block(value_ref, at) for at in picks], axis=0)
            for picks in all_picks
        ]
        parts, lses = softmax_parts(all_scores, all_values)
        stats = []
        for b in range(blocks):
            row = as_row(lses[b], (b * BLK) % LANES)
            if (b * BLK) % LANES:
                stats[-1] = stats[-1] + row
            else:
                stats.append(row)
        tile = stat_tile(stats)
        for b in range(blocks):
            out_ref[b * BLK : (b + 1) * BLK, :] = parts[b]
        out_ref[rows:, :] = tile


def near_rows(
    there, first, last, query_ref, key_ref, value_ref, halo_ref, came_refs, out_ref
):
    rows = query_ref.shape[0]
    halo = (WMAX - 1) * BLK
    starts = list(range(first, last, 2 * BLK))
    sizes = [min(2 * BLK, last - start) for start in starts]
    leads = [
        halo if start < halo else min(-(-(size + halo) // LANES) * LANES - size, start)
        for start, size in zip(starts, sizes)
    ]
    peers = peers_of(there, 0)
    for begin in range(0, len(peers), 2):
        pair = range(begin, min(begin + 2, len(peers)))
        all_lanes = [pl.ds(pl.multiple_of(peers[at] * HD, HD), HD) for at in pair]
        all_scores, all_values = [], []
        for at, lanes in zip(pair, all_lanes):
            width = came_refs[at][rows:, :].astype(jnp.float32)[:1]
            width = jnp.concatenate([width] * ((2 * BLK + halo) // LANES), axis=1)
            for start, size, lead in zip(starts, sizes, leads):
                query = query_ref[start : start + size, lanes]
                if start < lead:
                    keys = [halo_ref[0, start:, lanes], key_ref[: start + size, lanes]]
                    values = [halo_ref[1, start:, lanes], value_ref[: start + size, lanes]]
                    keys, values = jnp.concatenate(keys, axis=0), jnp.concatenate(values, axis=0)
                else:
                    keys = key_ref[start - lead : start + size, lanes]
                    values = value_ref[start - lead : start + size, lanes]
                scores = scores_of(query, keys)
                row_at = lax.broadcasted_iota(jnp.int32, scores.shape, 0)
                lane_at = lax.broadcasted_iota(jnp.int32, scores.shape, 1)
                slot = (lane_at // BLK - row_at // BLK - lead // BLK).astype(jnp.float32)
                allowed = (lane_at <= row_at + lead) & (slot + width[:, : size + lead] >= 1.0)
                if start < lead:
                    closed = jnp.where(lax.axis_index("seq") == 0, lead - start, 0)
                    allowed = allowed & (lane_at >= closed)
                all_scores.append(jnp.where(allowed, scores, MASKED))
                all_values.append(values)
        parts, lses = softmax_parts(all_scores, all_values)
        for index, lanes in enumerate(all_lanes):
            own = slice(index * len(starts), (index + 1) * len(starts))
            tile = stat_tile([as_row(lse, 0) for lse in lses[own]])
            for start, size, part in zip(starts, sizes, parts[own]):
                out_ref[start - first : start - first + size, lanes] = part
            out_ref[last - first : last - first + STAT_ROWS, lanes] = tile


def packed_at(index, first, wide):
    across = wide // HD
    row, lane = first + index // across * STAT_ROWS, index % across * HD
    return slice(row, row + STAT_ROWS), slice(lane, lane + HD)


def near_inner_kernel(there, query_ref, key_ref, value_ref, own_ref, *refs):
    rows, wide = query_ref.shape
    halo = (WMAX - 1) * BLK
    came_refs, out_ref = refs[:-1], refs[-1]
    near_rows(there, halo, rows, query_ref, key_ref, value_ref, None, came_refs, out_ref)
    for index in range(own_ref.shape[0] // STAT_ROWS):
        at = packed_at(index, rows - halo + STAT_ROWS, wide)
        out_ref[at] = own_ref[index * STAT_ROWS : (index + 1) * STAT_ROWS, :]


def near_edge_kernel(there, query_ref, key_ref, value_ref, odd_ref, even_ref, *refs):
    halo = (WMAX - 1) * BLK
    came_refs, out_ref, halo_ref = refs[: len(there[0])], refs[-2], refs[-1]
    halo_ref[...] = odd_ref[...] + even_ref[...]
    near_rows(there, 0, halo, query_ref, key_ref, value_ref, halo_ref, came_refs, out_ref)


def merge_kernel(there, edge_ref, inner_ref, *refs):
    far_refs, out_ref, own_ref = refs[:-2], refs[-2], refs[-1]
    rows, wide = out_ref.shape
    halo = (WMAX - 1) * BLK
    for index in range(own_ref.shape[0] // STAT_ROWS):
        at = packed_at(index, rows - halo + STAT_ROWS, wide)
        own_ref[index * STAT_ROWS : (index + 1) * STAT_ROWS, :] = inner_ref[at]
    count = stat_count(rows)
    for peer, far_ref in zip(peers_of(there, -1), (*far_refs, own_ref)):
        lanes = pl.ds(pl.multiple_of(peer * HD, HD), HD)
        far_stats = stat_rows_of(far_ref[rows:, :], count)
        near_stats = stat_rows_of(edge_ref[halo:, lanes], 1) + stat_rows_of(
            inner_ref[rows - halo : rows - halo + STAT_ROWS, lanes], count - 1
        )
        for group in range(count):
            start = group * LANES
            size = min(LANES, rows - start)
            share = 1.0 / (1.0 + jnp.exp2(near_stats[group] - far_stats[group]))
            row_at = lax.broadcasted_iota(jnp.int32, (size, LANES), 0)
            lane_at = lax.broadcasted_iota(jnp.int32, (size, LANES), 1)
            column = jnp.sum(
                jnp.where(row_at == lane_at, share, 0.0), axis=1, keepdims=True
            )
            far = far_ref[start : start + size, :].astype(jnp.float32)
            if start < halo:
                near = edge_ref[start : start + size, lanes].astype(jnp.float32)
            else:
                near = inner_ref[start - halo : start - halo + size, lanes].astype(jnp.float32)
            out_ref[start : start + size, lanes] = (
                far * column + near * (1.0 - column)
            ).astype(jnp.bfloat16)


def params(shard):
    return pltpu.CompilerParams(vmem_limit_bytes=VMEM_BASE + 14 * 2 * math.prod(shard.shape))


def per_device(
    queries, keys_new, values_new, keys_cache, values_cache, window, global_blocks, random_blocks
):
    section_count = lax.axis_size("section")
    seq_count = lax.axis_size("seq")
    rows, wide = queries.shape[1], queries.shape[2]
    halo = (WMAX - 1) * BLK
    heads = wide // HD
    bf16 = jnp.bfloat16
    half = max(seq_count // 2, 1)
    inner, outer = list(range(1, half)), list(range(seq_count - 1, half - 1, -1))
    there = [outer + inner + [0], inner + outer + [0]]

    chunk_shape = jax.ShapeDtypeStruct((rows + STAT_ROWS, HD), bf16)
    chunk_shape = jax.ShapeDtypeStruct((rows + STAT_ROWS, HD), bf16)
    sent = pl.pallas_call(
        functools.partial(split_kernel, there),
        out_shape=[chunk_shape] * seq_count,
        in_specs=[whole_smem, in_hbm],
        out_specs=[whole_vmem] * seq_count,
        scratch_shapes=[pltpu.SemaphoreType.DMA((seq_count,))],
        compiler_params=params(queries),
        cost_estimate=pl.CostEstimate(flops=0, bytes_accessed=5 * rows * wide, transcendentals=0),
        name="split",
    )(window[0], queries[0])

    def linked(shard, by, steps):
        pairs = [
            (
                s * seq_count + t,
                (s + by) % section_count * seq_count + (t ^ steps[s % 2]),
            )
            for s in range(section_count)
            for t in range(seq_count)
        ]
        return lax.ppermute(shard, ("section", "seq"), pairs)

    came = [linked(shard, 0, steps) for shard, steps in zip(sent[:-1], zip(*there))]
    came.append(sent[-1])
    def linked(shard, by, steps):
        pairs = [
            (
                s * seq_count + t,
                (s + by) % section_count * seq_count + (t ^ steps[s % 2]),
            )
            for s in range(section_count)
            for t in range(seq_count)
        ]
        return lax.ppermute(shard, ("section", "seq"), pairs)

    came = [linked(shard, 0, steps) for shard, steps in zip(sent[:-1], zip(*there))]
    came.append(sent[-1])
    tails = jnp.stack([keys_new[0, rows - halo :], values_new[0, rows - halo :]])

    def halo_from(parity, after):
        mine = tails if after is None else pl.pallas_call(
            halo_kernel,
            out_shape=jax.ShapeDtypeStruct(tails.shape, bf16),
            in_specs=[whole_vmem, anywhere],
            out_specs=whole_vmem,
            compiler_params=params(queries),
            name="halo",
        )(tails, after)
        pairs = [
            (s * seq_count + t, s * seq_count + t + 1)
            for s in range(parity, section_count, 2)
            for t in range(seq_count - 1)
        ]
        return lax.ppermute(mine, ("section", "seq"), pairs)

    halos = [halo_from(1, None), halo_from(0, came[0])]
    picks = random_blocks[0].reshape(-1)

    def far_call(chosen):
        count = len(chosen)
        return pl.pallas_call(
            functools.partial(far_kernel, there, chosen),
            out_shape=[chunk_shape] * count,
            in_specs=[whole_smem] * 3 + [whole_vmem] * (2 + count),
            out_specs=[whole_vmem] * count,
            compiler_params=params(queries),
            cost_estimate=pl.CostEstimate(
                flops=40 * count * rows * 320 * HD * 4,
                bytes_accessed=2 * 2 * keys_cache.shape[1] * HD + 4 * count * rows * HD,
                transcendentals=count * rows * 320,
            ),
            name="far",
        )(
            window[0],
            global_blocks[0],
            picks,
            keys_cache[0],
            values_cache[0],
            *[came[at] for at in chosen],
        )

    late = list(range(seq_count - 1 - seq_count // 4, seq_count - 1))
    early = [at for at in range(seq_count) if at not in late]
    far = dict(zip(early, far_call(early)))
    if late:
        far.update(zip(late, far_call(late)))
    far = [far[at] for at in range(seq_count)]
    handed = [linked(shard, 1, steps) for shard, steps in zip(far[:-1], zip(*there))]

    def near_call(kernel, name, near_part, out_rows, vmem_count, scratch, *operands):
        return pl.pallas_call(
            functools.partial(kernel, there),
            out_shape=jax.ShapeDtypeStruct((out_rows, wide), bf16),
            in_specs=[
                whole_vmem if index < 3 + vmem_count else anywhere
                for index in range(3 + len(operands))
            ],
            out_specs=whole_vmem,
            scratch_shapes=scratch,
            compiler_params=params(queries),
            cost_estimate=pl.CostEstimate(
                flops=40 * heads * near_part * 256 * HD * 4,
                bytes_accessed=9 * near_part * wide,
                transcendentals=heads * near_part * 256,
            ),
            name=name,
        )(queries[0], keys_new[0], values_new[0], *operands)

    packed_rows = -(-(rows + STAT_ROWS) // (STAT_ROWS * heads)) * STAT_ROWS
    inner_part = near_call(
        near_inner_kernel, "near_inner", rows - halo, rows - halo + STAT_ROWS + packed_rows,
        1 + seq_count, [], far[-1], *came,
    )
    edge_part = near_call(
        near_edge_kernel, "near_edge", halo, halo + STAT_ROWS,
        2 + seq_count, [pltpu.VMEM(tails.shape, bf16)], *halos, *came, *handed[:2],
    )
    handed_inner = linked(inner_part, 1, [0, 0])
    handed_edge = linked(edge_part, 1, [0, 0])

    merged = pl.pallas_call(
        functools.partial(merge_kernel, there),
        out_shape=jax.ShapeDtypeStruct((rows, wide), bf16),
        in_specs=[whole_vmem] * (1 + seq_count),
        out_specs=whole_vmem,
        scratch_shapes=[pltpu.VMEM(chunk_shape.shape, bf16)],
        compiler_params=params(queries),
        cost_estimate=pl.CostEstimate(flops=0, bytes_accessed=6 * rows * wide, transcendentals=0),
        name="merge",
    )(handed_edge, handed_inner, *handed)
    return merged[None]


def solution(mesh):
    placed = (
        P("section", "seq", None),
        P("section", "seq", None),
        P("section", "seq", None),
        P("section", None, "seq"),
        P("section", None, "seq"),
        P("section", "seq"),
        P("section", None),
        P("section", None, None),
    )
    return jax.shard_map(
        per_device, mesh=mesh, in_specs=placed, out_specs=P("section", "seq", None), check_vma=False
    )
```

```python
import functools
import math

import jax
import jax.numpy as jnp
from jax import lax
from jax.experimental import pallas as pl
from jax.experimental.pallas import tpu as pltpu
from jax.sharding import PartitionSpec as P

HD = 128
BLK = 64
WMAX = 3
GLOB = 2
RAND = 3
LANES = 128
STAT_ROWS = 16
MASKED = -1e30
EXPO_SCALE = math.log2(math.e) / math.sqrt(HD)
SPLIT_VMEM = 60 * 1024 * 1024
VMEM_BASE = 12 * 1024 * 1024

whole_vmem = pl.BlockSpec(memory_space=pltpu.VMEM)
anywhere = pl.BlockSpec(memory_space=pl.ANY)
in_hbm = pl.BlockSpec(memory_space=pltpu.HBM)
whole_smem = pl.BlockSpec(memory_space=pltpu.SMEM)


def peers_of(there, by):
    count = lax.axis_size("section")
    other = lax.rem(lax.axis_index("section") + (by + count), count)
    odd = lax.rem(other, 2) == 1
    me = lax.axis_index("seq")
    return [
        jnp.bitwise_xor(me, jnp.where(odd, odd_step, even_step))
        for even_step, odd_step in zip(*there)
    ]


def scores_of(query, keys):
    return lax.dot_general(
        query, keys, (((1,), (1,)), ((), ())), preferred_element_type=jnp.float32
    )


def softmax_parts(scores, values):
    tops = [jnp.max(score, axis=1, keepdims=True) for score in scores]
    expos = [jnp.exp2((score - top) * EXPO_SCALE) for score, top in zip(scores, tops)]
    totals = [jnp.sum(expo, axis=1, keepdims=True) for expo in expos]
    mixed = [
        jnp.dot(expo.astype(jnp.bfloat16), value, preferred_element_type=jnp.float32)
        for expo, value in zip(expos, values)
    ]
    parts = [(mix * (1.0 / total)).astype(jnp.bfloat16) for mix, total in zip(mixed, totals)]
    lses = [top * EXPO_SCALE + jnp.log2(total) for top, total in zip(tops, totals)]
    return parts, lses


def as_row(column, offset):
    shape = (column.shape[0], LANES)
    row_at = lax.broadcasted_iota(jnp.int32, shape, 0)
    lane_at = lax.broadcasted_iota(jnp.int32, shape, 1)
    spread = jnp.where(lane_at == row_at + offset, column, 0.0)
    return jnp.sum(spread, axis=0, keepdims=True)


def stat_tile(rows):
    at = lax.broadcasted_iota(jnp.int32, (STAT_ROWS, LANES), 0)
    tile = jnp.zeros((STAT_ROWS, LANES), jnp.float32)
    count = len(rows)
    for index, row in enumerate(rows):
        high = row.astype(jnp.bfloat16).astype(jnp.float32)
        middle = (row - high).astype(jnp.bfloat16).astype(jnp.float32)
        low = row - high - middle
        for part, value in enumerate((high, middle, low)):
            tile = jnp.where(at == part * count + index, value, tile)
    return tile.astype(jnp.bfloat16)


def stat_rows_of(tile, count):
    wide = tile.astype(jnp.float32)
    return [
        wide[index : index + 1]
        + wide[count + index : count + index + 1]
        + wide[2 * count + index : 2 * count + index + 1]
        for index in range(count)
    ]


def stat_count(rows):
    return -(-rows // LANES)


def split_kernel(there, span_ref, query_ref, *refs):
    out_refs, width_ref, arrived = refs[:-2], refs[-2], refs[-1]
    rows = query_ref.shape[0]
    width_ref[...] = jnp.full(width_ref.shape, span_ref[0].astype(jnp.float32)).astype(
        width_ref.dtype
    )
    copies = []
    for peer, out_ref in zip(peers_of(there, 0), out_refs):
        head = pl.multiple_of(peer * HD, HD)
        copies.append((query_ref.at[:, pl.ds(head, HD)], out_ref.at[:rows]))
        copies.append((width_ref, out_ref.at[rows:]))
    copies = [
        pltpu.make_async_copy(source, target, arrived.at[index])
        for index, (source, target) in enumerate(copies)
    ]
    for copy in copies:
        copy.start()
    for copy in copies:
        copy.wait()


def halo_kernel(rows_ref, _, out_ref):
    out_ref[...] = rows_ref[...]


def far_kernel(
    there, chosen, span_ref, global_ref, random_ref, key_ref, value_ref, *refs
):
    span = span_ref[0]
    last = key_ref.shape[0] // BLK - 1

    def block(ref, at):
        if isinstance(at, int):
            return ref[at * BLK : (at + 1) * BLK, :]
        return ref[pl.ds(pl.multiple_of(at * BLK, BLK), BLK), :]

    glob_keys = [block(key_ref, global_ref[g]) for g in range(GLOB)]
    glob_values = [block(value_ref, global_ref[g]) for g in range(GLOB)]
    peers = [peers_of(there, 0)[at] for at in chosen]
    query_refs, out_refs = refs[: len(peers)], refs[len(peers) :]
    rows = query_refs[0].shape[0] - STAT_ROWS
    for chunk, query_ref, out_ref in zip(peers, query_refs, out_refs):
        blocks = rows // BLK
        first = chunk == 0
        all_scores, all_picks = [], []
        for b in range(blocks):
            query = query_ref[b * BLK : (b + 1) * BLK, :]
            base = (chunk * blocks + b) * RAND
            picks = [random_ref[base + r] for r in range(RAND)]
            keys = glob_keys + [block(key_ref, pick) for pick in picks]
            known = len(keys) * BLK
            spare = [last + 1 + b - w for w in range(b + 1, WMAX)]
            keys = keys + [block(key_ref, at) for at in spare]
            scores = scores_of(query, jnp.concatenate(keys, axis=0))
            if spare:
                open_slots = jnp.where(first, jnp.clip(span - (b + 1), 0, len(spare)), 0)
                lane_at = lax.broadcasted_iota(jnp.int32, scores.shape, 1)
                scores = jnp.where(lane_at < known + open_slots * BLK, scores, MASKED)
            all_scores.append(scores)
            all_picks.append(picks + spare)
        all_values = [
            jnp.concatenate(glob_values + [block(value_ref, at) for at in picks], axis=0)
            for picks in all_picks
        ]
        parts, lses = softmax_parts(all_scores, all_values)
        stats = []
        for b in range(blocks):
            row = as_row(lses[b], (b * BLK) % LANES)
            if (b * BLK) % LANES:
                stats[-1] = stats[-1] + row
            else:
                stats.append(row)
        tile = stat_tile(stats)
        for b in range(blocks):
            out_ref[b * BLK : (b + 1) * BLK, :] = parts[b]
        out_ref[rows:, :] = tile


def near_rows(
    there, first, last, query_ref, key_ref, value_ref, halo_ref, came_refs, out_ref
):
    rows = query_ref.shape[0]
    halo = (WMAX - 1) * BLK
    starts = list(range(first, last, 2 * BLK))
    sizes = [min(2 * BLK, last - start) for start in starts]
    leads = [
        halo if start < halo else min(-(-(size + halo) // LANES) * LANES - size, start)
        for start, size in zip(starts, sizes)
    ]
    peers = peers_of(there, 0)
    for begin in range(0, len(peers), 2):
        pair = range(begin, min(begin + 2, len(peers)))
        all_lanes = [pl.ds(pl.multiple_of(peers[at] * HD, HD), HD) for at in pair]
        all_scores, all_values = [], []
        for at, lanes in zip(pair, all_lanes):
            width = came_refs[at][rows:, :].astype(jnp.float32)[:1]
            width = jnp.concatenate([width] * ((2 * BLK + halo) // LANES), axis=1)
            for start, size, lead in zip(starts, sizes, leads):
                query = query_ref[start : start + size, lanes]
                if start < lead:
                    keys = [halo_ref[0, start:, lanes], key_ref[: start + size, lanes]]
                    values = [halo_ref[1, start:, lanes], value_ref[: start + size, lanes]]
                    keys, values = jnp.concatenate(keys, axis=0), jnp.concatenate(values, axis=0)
                else:
                    keys = key_ref[start - lead : start + size, lanes]
                    values = value_ref[start - lead : start + size, lanes]
                scores = scores_of(query, keys)
                row_at = lax.broadcasted_iota(jnp.int32, scores.shape, 0)
                lane_at = lax.broadcasted_iota(jnp.int32, scores.shape, 1)
                slot = (lane_at // BLK - row_at // BLK - lead // BLK).astype(jnp.float32)
                allowed = (lane_at <= row_at + lead) & (slot + width[:, : size + lead] >= 1.0)
                if start < lead:
                    closed = jnp.where(lax.axis_index("seq") == 0, lead - start, 0)
                    allowed = allowed & (lane_at >= closed)
                all_scores.append(jnp.where(allowed, scores, MASKED))
                all_values.append(values)
        parts, lses = softmax_parts(all_scores, all_values)
        for index, lanes in enumerate(all_lanes):
            own = slice(index * len(starts), (index + 1) * len(starts))
            tile = stat_tile([as_row(lse, 0) for lse in lses[own]])
            for start, size, part in zip(starts, sizes, parts[own]):
                out_ref[start - first : start - first + size, lanes] = part
            out_ref[last - first : last - first + STAT_ROWS, lanes] = tile


def packed_at(index, first, wide):
    across = wide // HD
    row, lane = first + index // across * STAT_ROWS, index % across * HD
    return slice(row, row + STAT_ROWS), slice(lane, lane + HD)


def near_inner_kernel(there, query_ref, key_ref, value_ref, own_ref, *refs):
    rows, wide = query_ref.shape
    halo = (WMAX - 1) * BLK
    came_refs, out_ref = refs[:-1], refs[-1]
    near_rows(there, halo, rows, query_ref, key_ref, value_ref, None, came_refs, out_ref)
    for index in range(own_ref.shape[0] // STAT_ROWS):
        at = packed_at(index, rows - halo + STAT_ROWS, wide)
        out_ref[at] = own_ref[index * STAT_ROWS : (index + 1) * STAT_ROWS, :]


def near_edge_kernel(there, query_ref, key_ref, value_ref, odd_ref, even_ref, *refs):
    halo = (WMAX - 1) * BLK
    came_refs, out_ref, halo_ref = refs[: len(there[0])], refs[-2], refs[-1]
    halo_ref[...] = odd_ref[...] + even_ref[...]
    near_rows(there, 0, halo, query_ref, key_ref, value_ref, halo_ref, came_refs, out_ref)


def merge_kernel(there, edge_ref, inner_ref, *refs):
    far_refs, out_ref, own_ref = refs[:-2], refs[-2], refs[-1]
    rows, wide = out_ref.shape
    halo = (WMAX - 1) * BLK
    for index in range(own_ref.shape[0] // STAT_ROWS):
        at = packed_at(index, rows - halo + STAT_ROWS, wide)
        own_ref[index * STAT_ROWS : (index + 1) * STAT_ROWS, :] = inner_ref[at]
    count = stat_count(rows)
    for peer, far_ref in zip(peers_of(there, -1), (*far_refs, own_ref)):
        lanes = pl.ds(pl.multiple_of(peer * HD, HD), HD)
        far_stats = stat_rows_of(far_ref[rows:, :], count)
        near_stats = stat_rows_of(edge_ref[halo:, lanes], 1) + stat_rows_of(
            inner_ref[rows - halo : rows - halo + STAT_ROWS, lanes], count - 1
        )
        for group in range(count):
            start = group * LANES
            size = min(LANES, rows - start)
            share = 1.0 / (1.0 + jnp.exp2(near_stats[group] - far_stats[group]))
            row_at = lax.broadcasted_iota(jnp.int32, (size, LANES), 0)
            lane_at = lax.broadcasted_iota(jnp.int32, (size, LANES), 1)
            column = jnp.sum(
                jnp.where(row_at == lane_at, share, 0.0), axis=1, keepdims=True
            )
            far = far_ref[start : start + size, :].astype(jnp.float32)
            if start < halo:
                near = edge_ref[start : start + size, lanes].astype(jnp.float32)
            else:
                near = inner_ref[start - halo : start - halo + size, lanes].astype(jnp.float32)
            out_ref[start : start + size, lanes] = (
                far * column + near * (1.0 - column)
            ).astype(jnp.bfloat16)


def params(shard):
    return pltpu.CompilerParams(vmem_limit_bytes=VMEM_BASE + 14 * 2 * math.prod(shard.shape))


def per_device(
    queries, keys_new, values_new, keys_cache, values_cache, window, global_blocks, random_blocks
):
    section_count = lax.axis_size("section")
    seq_count = lax.axis_size("seq")
    rows, wide = queries.shape[1], queries.shape[2]
    halo = (WMAX - 1) * BLK
    heads = wide // HD
    bf16 = jnp.bfloat16
    half = max(seq_count // 2, 1)
    inner, outer = list(range(1, half)), list(range(seq_count - 1, half - 1, -1))
    outer_first = [step for both in zip(outer, inner) for step in both]
    outer_first = outer_first[:-1] + outer[len(inner) :] + outer_first[-1:]
    inner_first = [step for both in zip(inner, outer) for step in both] + outer[len(inner) :]
    there = [outer_first + [0], inner_first + [0]]

    chunk_shape = jax.ShapeDtypeStruct((rows + STAT_ROWS, HD), bf16)
    chunk_shape = jax.ShapeDtypeStruct((rows + STAT_ROWS, HD), bf16)
    sent = pl.pallas_call(
        functools.partial(split_kernel, there),
        out_shape=[chunk_shape] * seq_count,
        in_specs=[whole_smem, anywhere],
        out_specs=[anywhere] * seq_count,
        scratch_shapes=[
            pltpu.VMEM((STAT_ROWS, HD), bf16),
            pltpu.SemaphoreType.DMA((2 * seq_count,)),
        ],
        compiler_params=pltpu.CompilerParams(vmem_limit_bytes=SPLIT_VMEM),
        cost_estimate=pl.CostEstimate(flops=0, bytes_accessed=5 * rows * wide, transcendentals=0),
        name="split",
    )(window[0], queries[0])

    def linked(shard, by, steps):
        pairs = [
            (
                s * seq_count + t,
                (s + by) % section_count * seq_count + (t ^ steps[s % 2]),
            )
            for s in range(section_count)
            for t in range(seq_count)
        ]
        return lax.ppermute(shard, ("section", "seq"), pairs)

    came = [linked(shard, 0, steps) for shard, steps in zip(sent[:-1], zip(*there))]
    came.append(sent[-1])
    def linked(shard, by, steps):
        pairs = [
            (
                s * seq_count + t,
                (s + by) % section_count * seq_count + (t ^ steps[s % 2]),
            )
            for s in range(section_count)
            for t in range(seq_count)
        ]
        return lax.ppermute(shard, ("section", "seq"), pairs)

    came = [linked(shard, 0, steps) for shard, steps in zip(sent[:-1], zip(*there))]
    came.append(sent[-1])
    tails = jnp.stack([keys_new[0, rows - halo :], values_new[0, rows - halo :]])

    def halo_from(parity, after):
        mine = tails if after is None else pl.pallas_call(
            halo_kernel,
            out_shape=jax.ShapeDtypeStruct(tails.shape, bf16),
            in_specs=[whole_vmem, anywhere],
            out_specs=whole_vmem,
            compiler_params=params(queries),
            name="halo",
        )(tails, after)
        pairs = [
            (s * seq_count + t, s * seq_count + t + 1)
            for s in range(parity, section_count, 2)
            for t in range(seq_count - 1)
        ]
        return lax.ppermute(mine, ("section", "seq"), pairs)

    halos = [halo_from(1, None), halo_from(0, came[0])]
    picks = random_blocks[0].reshape(-1)

    def far_call(chosen):
        count = len(chosen)
        return pl.pallas_call(
            functools.partial(far_kernel, there, chosen),
            out_shape=[chunk_shape] * count,
            in_specs=[whole_smem] * 3 + [whole_vmem] * (2 + count),
            out_specs=[whole_vmem] * count,
            compiler_params=params(queries),
            cost_estimate=pl.CostEstimate(
                flops=40 * count * rows * 320 * HD * 4,
                bytes_accessed=2 * 2 * keys_cache.shape[1] * HD + 4 * count * rows * HD,
                transcendentals=count * rows * 320,
            ),
            name="far",
        )(
            window[0],
            global_blocks[0],
            picks,
            keys_cache[0],
            values_cache[0],
            *[came[at] for at in chosen],
        )

    late = list(range(seq_count - 1 - seq_count // 4, seq_count - 1))
    early = [at for at in range(seq_count) if at not in late]
    far = dict(zip(early, far_call(early)))
    if late:
        far.update(zip(late, far_call(late)))
    far = [far[at] for at in range(seq_count)]
    handed = [linked(shard, 1, steps) for shard, steps in zip(far[:-1], zip(*there))]

    def near_call(kernel, name, near_part, out_rows, vmem_count, scratch, *operands):
        return pl.pallas_call(
            functools.partial(kernel, there),
            out_shape=jax.ShapeDtypeStruct((out_rows, wide), bf16),
            in_specs=[
                whole_vmem if index < 3 + vmem_count else anywhere
                for index in range(3 + len(operands))
            ],
            out_specs=whole_vmem,
            scratch_shapes=scratch,
            compiler_params=params(queries),
            cost_estimate=pl.CostEstimate(
                flops=40 * heads * near_part * 256 * HD * 4,
                bytes_accessed=9 * near_part * wide,
                transcendentals=heads * near_part * 256,
            ),
            name=name,
        )(queries[0], keys_new[0], values_new[0], *operands)

    packed_rows = -(-(rows + STAT_ROWS) // (STAT_ROWS * heads)) * STAT_ROWS
    inner_part = near_call(
        near_inner_kernel, "near_inner", rows - halo, rows - halo + STAT_ROWS + packed_rows,
        1 + seq_count, [], far[-1], *came,
    )
    edge_part = near_call(
        near_edge_kernel, "near_edge", halo, halo + STAT_ROWS,
        2 + seq_count, [pltpu.VMEM(tails.shape, bf16)], *halos, *came, *handed[:2],
    )
    handed_inner = linked(inner_part, 1, [0, 0])
    handed_edge = linked(edge_part, 1, [0, 0])

    merged = pl.pallas_call(
        functools.partial(merge_kernel, there),
        out_shape=jax.ShapeDtypeStruct((rows, wide), bf16),
        in_specs=[whole_vmem] * (1 + seq_count),
        out_specs=whole_vmem,
        scratch_shapes=[pltpu.VMEM(chunk_shape.shape, bf16)],
        compiler_params=params(queries),
        cost_estimate=pl.CostEstimate(flops=0, bytes_accessed=6 * rows * wide, transcendentals=0),
        name="merge",
    )(handed_edge, handed_inner, *handed)
    return merged[None]


def solution(mesh):
    placed = (
        P("section", "seq", None),
        P("section", "seq", None),
        P("section", "seq", None),
        P("section", None, "seq"),
        P("section", None, "seq"),
        P("section", "seq"),
        P("section", None),
        P("section", None, None),
    )
    return jax.shard_map(
        per_device, mesh=mesh, in_specs=placed, out_specs=P("section", "seq", None), check_vma=False
    )
```

```python
import functools
import math

import jax
import jax.numpy as jnp
from jax import lax
from jax.experimental import pallas as pl
from jax.experimental.pallas import tpu as pltpu
from jax.sharding import PartitionSpec as P

HD = 128
BLK = 64
WMAX = 3
GLOB = 2
RAND = 3
LANES = 128
STAT_ROWS = 16
MASKED = -1e30
EXPO_SCALE = math.log2(math.e) / math.sqrt(HD)
VMEM_BASE = 12 * 1024 * 1024

whole_vmem = pl.BlockSpec(memory_space=pltpu.VMEM)
anywhere = pl.BlockSpec(memory_space=pl.ANY)
in_hbm = pl.BlockSpec(memory_space=pltpu.HBM)
whole_smem = pl.BlockSpec(memory_space=pltpu.SMEM)


def peers_of(there, by):
    count = lax.axis_size("section")
    other = lax.rem(lax.axis_index("section") + (by + count), count)
    odd = lax.rem(other, 2) == 1
    me = lax.axis_index("seq")
    return [
        jnp.bitwise_xor(me, jnp.where(odd, odd_step, even_step))
        for even_step, odd_step in zip(*there)
    ]


def scores_of(query, keys):
    return lax.dot_general(
        query, keys, (((1,), (1,)), ((), ())), preferred_element_type=jnp.float32
    )


def softmax_parts(scores, values):
    tops = [jnp.max(score, axis=1, keepdims=True) for score in scores]
    expos = [jnp.exp2((score - top) * EXPO_SCALE) for score, top in zip(scores, tops)]
    totals = [jnp.sum(expo, axis=1, keepdims=True) for expo in expos]
    mixed = [
        jnp.dot(expo.astype(jnp.bfloat16), value, preferred_element_type=jnp.float32)
        for expo, value in zip(expos, values)
    ]
    parts = [(mix * (1.0 / total)).astype(jnp.bfloat16) for mix, total in zip(mixed, totals)]
    lses = [top * EXPO_SCALE + jnp.log2(total) for top, total in zip(tops, totals)]
    return parts, lses


def as_row(column, offset):
    shape = (column.shape[0], LANES)
    row_at = lax.broadcasted_iota(jnp.int32, shape, 0)
    lane_at = lax.broadcasted_iota(jnp.int32, shape, 1)
    spread = jnp.where(lane_at == row_at + offset, column, 0.0)
    return jnp.sum(spread, axis=0, keepdims=True)


def stat_tile(rows):
    at = lax.broadcasted_iota(jnp.int32, (STAT_ROWS, LANES), 0)
    tile = jnp.zeros((STAT_ROWS, LANES), jnp.float32)
    count = len(rows)
    for index, row in enumerate(rows):
        high = row.astype(jnp.bfloat16).astype(jnp.float32)
        middle = (row - high).astype(jnp.bfloat16).astype(jnp.float32)
        low = row - high - middle
        for part, value in enumerate((high, middle, low)):
            tile = jnp.where(at == part * count + index, value, tile)
    return tile.astype(jnp.bfloat16)


def stat_rows_of(tile, count):
    wide = tile.astype(jnp.float32)
    return [
        wide[index : index + 1]
        + wide[count + index : count + index + 1]
        + wide[2 * count + index : 2 * count + index + 1]
        for index in range(count)
    ]


def stat_count(rows):
    return -(-rows // LANES)


def split_kernel(there, span_ref, query_ref, *refs):
    out_refs, arrived = refs[:-1], refs[-1]
    rows = query_ref.shape[0]
    copies = []
    for peer, out_ref in zip(peers_of(there, 0), out_refs):
        head = pl.multiple_of(peer * HD, HD)
        copies.append((query_ref.at[:, pl.ds(head, HD)], out_ref.at[:rows]))
    copies = [
        pltpu.make_async_copy(source, target, arrived.at[index])
        for index, (source, target) in enumerate(copies)
    ]
    for copy in copies:
        copy.start()
    width = jnp.full((STAT_ROWS, HD), span_ref[0].astype(jnp.float32)).astype(jnp.bfloat16)
    for out_ref in out_refs:
        out_ref[rows:, :] = width
    for copy in copies:
        copy.wait()


def halo_kernel(rows_ref, _, out_ref):
    out_ref[...] = rows_ref[...]


def far_kernel(
    there, chosen, span_ref, global_ref, random_ref, key_ref, value_ref, *refs
):
    span = span_ref[0]
    last = key_ref.shape[0] // BLK - 1

    def block(ref, at):
        if isinstance(at, int):
            return ref[at * BLK : (at + 1) * BLK, :]
        return ref[pl.ds(pl.multiple_of(at * BLK, BLK), BLK), :]

    glob_keys = [block(key_ref, global_ref[g]) for g in range(GLOB)]
    glob_values = [block(value_ref, global_ref[g]) for g in range(GLOB)]
    peers = [peers_of(there, 0)[at] for at in chosen]
    query_refs, out_refs = refs[: len(peers)], refs[-len(peers) :]
    rows = query_refs[0].shape[0] - STAT_ROWS
    for chunk, query_ref, out_ref in zip(peers, query_refs, out_refs):
        blocks = rows // BLK
        first = chunk == 0
        all_scores, all_picks = [], []
        for b in range(blocks):
            query = query_ref[b * BLK : (b + 1) * BLK, :]
            base = (chunk * blocks + b) * RAND
            picks = [random_ref[base + r] for r in range(RAND)]
            keys = glob_keys + [block(key_ref, pick) for pick in picks]
            known = len(keys) * BLK
            spare = [last + 1 + b - w for w in range(b + 1, WMAX)]
            keys = keys + [block(key_ref, at) for at in spare]
            scores = scores_of(query, jnp.concatenate(keys, axis=0))
            if spare:
                open_slots = jnp.where(first, jnp.clip(span - (b + 1), 0, len(spare)), 0)
                lane_at = lax.broadcasted_iota(jnp.int32, scores.shape, 1)
                scores = jnp.where(lane_at < known + open_slots * BLK, scores, MASKED)
            all_scores.append(scores)
            all_picks.append(picks + spare)
        all_values = [
            jnp.concatenate(glob_values + [block(value_ref, at) for at in picks], axis=0)
            for picks in all_picks
        ]
        parts, lses = softmax_parts(all_scores, all_values)
        stats = []
        for b in range(blocks):
            row = as_row(lses[b], (b * BLK) % LANES)
            if (b * BLK) % LANES:
                stats[-1] = stats[-1] + row
            else:
                stats.append(row)
        tile = stat_tile(stats)
        for b in range(blocks):
            out_ref[b * BLK : (b + 1) * BLK, :] = parts[b]
        out_ref[rows:, :] = tile


def near_rows(
    there, first, last, query_ref, key_ref, value_ref, halo_ref, came_refs, out_ref
):
    rows = query_ref.shape[0]
    halo = (WMAX - 1) * BLK
    starts = list(range(first, last, 2 * BLK))
    sizes = [min(2 * BLK, last - start) for start in starts]
    leads = [
        halo if start < halo else min(-(-(size + halo) // LANES) * LANES - size, start)
        for start, size in zip(starts, sizes)
    ]
    peers = peers_of(there, 0)
    for begin in range(0, len(peers), 2):
        pair = range(begin, min(begin + 2, len(peers)))
        all_lanes = [pl.ds(pl.multiple_of(peers[at] * HD, HD), HD) for at in pair]
        all_scores, all_values = [], []
        for at, lanes in zip(pair, all_lanes):
            width = came_refs[at][rows:, :].astype(jnp.float32)[:1]
            width = jnp.concatenate([width] * ((2 * BLK + halo) // LANES), axis=1)
            for start, size, lead in zip(starts, sizes, leads):
                query = query_ref[start : start + size, lanes]
                if start < lead:
                    keys = [halo_ref[0, start:, lanes], key_ref[: start + size, lanes]]
                    values = [halo_ref[1, start:, lanes], value_ref[: start + size, lanes]]
                    keys, values = jnp.concatenate(keys, axis=0), jnp.concatenate(values, axis=0)
                else:
                    keys = key_ref[start - lead : start + size, lanes]
                    values = value_ref[start - lead : start + size, lanes]
                scores = scores_of(query, keys)
                row_at = lax.broadcasted_iota(jnp.int32, scores.shape, 0)
                lane_at = lax.broadcasted_iota(jnp.int32, scores.shape, 1)
                slot = (lane_at // BLK - row_at // BLK - lead // BLK).astype(jnp.float32)
                allowed = (lane_at <= row_at + lead) & (slot + width[:, : size + lead] >= 1.0)
                if start < lead:
                    closed = jnp.where(lax.axis_index("seq") == 0, lead - start, 0)
                    allowed = allowed & (lane_at >= closed)
                all_scores.append(jnp.where(allowed, scores, MASKED))
                all_values.append(values)
        parts, lses = softmax_parts(all_scores, all_values)
        for index, lanes in enumerate(all_lanes):
            own = slice(index * len(starts), (index + 1) * len(starts))
            tile = stat_tile([as_row(lse, 0) for lse in lses[own]])
            for start, size, part in zip(starts, sizes, parts[own]):
                out_ref[start - first : start - first + size, lanes] = part
            out_ref[last - first : last - first + STAT_ROWS, lanes] = tile


def packed_at(index, first, wide):
    across = wide // HD
    row, lane = first + index // across * STAT_ROWS, index % across * HD
    return slice(row, row + STAT_ROWS), slice(lane, lane + HD)


def near_inner_kernel(there, query_ref, key_ref, value_ref, own_ref, *refs):
    rows, wide = query_ref.shape
    halo = (WMAX - 1) * BLK
    came_refs, out_ref = refs[:-1], refs[-1]
    near_rows(there, halo, rows, query_ref, key_ref, value_ref, None, came_refs, out_ref)
    for index in range(own_ref.shape[0] // STAT_ROWS):
        at = packed_at(index, rows - halo + STAT_ROWS, wide)
        out_ref[at] = own_ref[index * STAT_ROWS : (index + 1) * STAT_ROWS, :]


def near_edge_kernel(there, query_ref, key_ref, value_ref, odd_ref, even_ref, *refs):
    halo = (WMAX - 1) * BLK
    came_refs, out_ref, halo_ref = refs[: len(there[0])], refs[-2], refs[-1]
    halo_ref[...] = odd_ref[...] + even_ref[...]
    near_rows(there, 0, halo, query_ref, key_ref, value_ref, halo_ref, came_refs, out_ref)


def merge_kernel(there, edge_ref, inner_ref, *refs):
    far_refs, out_ref, own_ref = refs[:-2], refs[-2], refs[-1]
    rows, wide = out_ref.shape
    halo = (WMAX - 1) * BLK
    for index in range(own_ref.shape[0] // STAT_ROWS):
        at = packed_at(index, rows - halo + STAT_ROWS, wide)
        own_ref[index * STAT_ROWS : (index + 1) * STAT_ROWS, :] = inner_ref[at]
    count = stat_count(rows)
    for peer, far_ref in zip(peers_of(there, -1), (*far_refs, own_ref)):
        lanes = pl.ds(pl.multiple_of(peer * HD, HD), HD)
        far_stats = stat_rows_of(far_ref[rows:, :], count)
        near_stats = stat_rows_of(edge_ref[halo:, lanes], 1) + stat_rows_of(
            inner_ref[rows - halo : rows - halo + STAT_ROWS, lanes], count - 1
        )
        for group in range(count):
            start = group * LANES
            size = min(LANES, rows - start)
            share = 1.0 / (1.0 + jnp.exp2(near_stats[group] - far_stats[group]))
            row_at = lax.broadcasted_iota(jnp.int32, (size, LANES), 0)
            lane_at = lax.broadcasted_iota(jnp.int32, (size, LANES), 1)
            column = jnp.sum(
                jnp.where(row_at == lane_at, share, 0.0), axis=1, keepdims=True
            )
            far = far_ref[start : start + size, :].astype(jnp.float32)
            if start < halo:
                near = edge_ref[start : start + size, lanes].astype(jnp.float32)
            else:
                near = inner_ref[start - halo : start - halo + size, lanes].astype(jnp.float32)
            out_ref[start : start + size, lanes] = (
                far * column + near * (1.0 - column)
            ).astype(jnp.bfloat16)


def params(shard):
    return pltpu.CompilerParams(vmem_limit_bytes=VMEM_BASE + 14 * 2 * math.prod(shard.shape))


def per_device(
    queries, keys_new, values_new, keys_cache, values_cache, window, global_blocks, random_blocks
):
    section_count = lax.axis_size("section")
    seq_count = lax.axis_size("seq")
    rows, wide = queries.shape[1], queries.shape[2]
    halo = (WMAX - 1) * BLK
    heads = wide // HD
    bf16 = jnp.bfloat16
    half = max(seq_count // 2, 1)
    inner, outer = list(range(1, half)), list(range(seq_count - 1, half - 1, -1))
    there = [outer + inner + [0], inner + outer + [0]]

    chunk_shape = jax.ShapeDtypeStruct((rows + STAT_ROWS, HD), bf16)
    chunk_shape = jax.ShapeDtypeStruct((rows + STAT_ROWS, HD), bf16)
    sent = pl.pallas_call(
        functools.partial(split_kernel, there),
        out_shape=[chunk_shape] * seq_count,
        in_specs=[whole_smem, in_hbm],
        out_specs=[whole_vmem] * seq_count,
        scratch_shapes=[pltpu.SemaphoreType.DMA((seq_count,))],
        compiler_params=params(queries),
        cost_estimate=pl.CostEstimate(flops=0, bytes_accessed=5 * rows * wide, transcendentals=0),
        name="split",
    )(window[0], queries[0])

    def linked(shard, by, steps):
        pairs = [
            (
                s * seq_count + t,
                (s + by) % section_count * seq_count + (t ^ steps[s % 2]),
            )
            for s in range(section_count)
            for t in range(seq_count)
        ]
        return lax.ppermute(shard, ("section", "seq"), pairs)

    came = [linked(shard, 0, steps) for shard, steps in zip(sent[:-1], zip(*there))]
    came.append(sent[-1])
    def linked(shard, by, steps):
        pairs = [
            (
                s * seq_count + t,
                (s + by) % section_count * seq_count + (t ^ steps[s % 2]),
            )
            for s in range(section_count)
            for t in range(seq_count)
        ]
        return lax.ppermute(shard, ("section", "seq"), pairs)

    came = [linked(shard, 0, steps) for shard, steps in zip(sent[:-1], zip(*there))]
    came.append(sent[-1])
    tails = jnp.stack([keys_new[0, rows - halo :], values_new[0, rows - halo :]])

    def halo_from(parity, after):
        mine = tails if after is None else pl.pallas_call(
            halo_kernel,
            out_shape=jax.ShapeDtypeStruct(tails.shape, bf16),
            in_specs=[whole_vmem, anywhere],
            out_specs=whole_vmem,
            compiler_params=params(queries),
            name="halo",
        )(tails, after)
        pairs = [
            (s * seq_count + t, s * seq_count + t + 1)
            for s in range(parity, section_count, 2)
            for t in range(seq_count - 1)
        ]
        return lax.ppermute(mine, ("section", "seq"), pairs)

    halos = [halo_from(1, None), halo_from(0, came[0])]
    picks = random_blocks[0].reshape(-1)

    def far_call(chosen, *after):
        count = len(chosen)
        return pl.pallas_call(
            functools.partial(far_kernel, there, chosen),
            out_shape=[chunk_shape] * count,
            in_specs=[whole_smem] * 3 + [whole_vmem] * (2 + count) + [anywhere] * len(after),
            out_specs=[whole_vmem] * count,
            compiler_params=params(queries),
            cost_estimate=pl.CostEstimate(
                flops=40 * count * rows * 320 * HD * 4,
                bytes_accessed=2 * 2 * keys_cache.shape[1] * HD + 4 * count * rows * HD,
                transcendentals=count * rows * 320,
            ),
            name="far",
        )(
            window[0],
            global_blocks[0],
            picks,
            keys_cache[0],
            values_cache[0],
            *[came[at] for at in chosen],
            *after,
        )

    late = list(range(seq_count - 1 - seq_count // 4, seq_count - 1))
    early = [at for at in range(seq_count) if at not in late]
    far = dict(zip(early, far_call(early, halos[0])))
    if late:
        far.update(zip(late, far_call(late, far[early[0]])))
    far = [far[at] for at in range(seq_count)]
    handed = [linked(shard, 1, steps) for shard, steps in zip(far[:-1], zip(*there))]

    def near_call(kernel, name, near_part, out_rows, vmem_count, scratch, *operands):
        return pl.pallas_call(
            functools.partial(kernel, there),
            out_shape=jax.ShapeDtypeStruct((out_rows, wide), bf16),
            in_specs=[
                whole_vmem if index < 3 + vmem_count else anywhere
                for index in range(3 + len(operands))
            ],
            out_specs=whole_vmem,
            scratch_shapes=scratch,
            compiler_params=params(queries),
            cost_estimate=pl.CostEstimate(
                flops=40 * heads * near_part * 256 * HD * 4,
                bytes_accessed=9 * near_part * wide,
                transcendentals=heads * near_part * 256,
            ),
            name=name,
        )(queries[0], keys_new[0], values_new[0], *operands)

    packed_rows = -(-(rows + STAT_ROWS) // (STAT_ROWS * heads)) * STAT_ROWS
    inner_part = near_call(
        near_inner_kernel, "near_inner", rows - halo, rows - halo + STAT_ROWS + packed_rows,
        1 + seq_count, [], far[-1], *came,
    )
    edge_part = near_call(
        near_edge_kernel, "near_edge", halo, halo + STAT_ROWS,
        2 + seq_count, [pltpu.VMEM(tails.shape, bf16)], *halos, *came, *handed[:2],
    )
    handed_inner = linked(inner_part, 1, [0, 0])
    handed_edge = linked(edge_part, 1, [0, 0])

    merged = pl.pallas_call(
        functools.partial(merge_kernel, there),
        out_shape=jax.ShapeDtypeStruct((rows, wide), bf16),
        in_specs=[whole_vmem] * (1 + seq_count),
        out_specs=whole_vmem,
        scratch_shapes=[pltpu.VMEM(chunk_shape.shape, bf16)],
        compiler_params=params(queries),
        cost_estimate=pl.CostEstimate(flops=0, bytes_accessed=6 * rows * wide, transcendentals=0),
        name="merge",
    )(handed_edge, handed_inner, *handed)
    return merged[None]


def solution(mesh):
    placed = (
        P("section", "seq", None),
        P("section", "seq", None),
        P("section", "seq", None),
        P("section", None, "seq"),
        P("section", None, "seq"),
        P("section", "seq"),
        P("section", None),
        P("section", None, None),
    )
    return jax.shard_map(
        per_device, mesh=mesh, in_specs=placed, out_specs=P("section", "seq", None), check_vma=False
    )
```

```python
import functools
import math

import jax
import jax.numpy as jnp
from jax import lax
from jax.experimental import pallas as pl
from jax.experimental.pallas import tpu as pltpu
from jax.sharding import PartitionSpec as P

HD = 128
BLK = 64
WMAX = 3
GLOB = 2
RAND = 3
LANES = 128
STAT_ROWS = 16
MASKED = -1e30
EXPO_SCALE = math.log2(math.e) / math.sqrt(HD)
VMEM_BASE = 12 * 1024 * 1024

whole_vmem = pl.BlockSpec(memory_space=pltpu.VMEM)
anywhere = pl.BlockSpec(memory_space=pl.ANY)
in_hbm = pl.BlockSpec(memory_space=pltpu.HBM)
whole_smem = pl.BlockSpec(memory_space=pltpu.SMEM)


def peers_of(there, by):
    count = lax.axis_size("section")
    other = lax.rem(lax.axis_index("section") + (by + count), count)
    odd = lax.rem(other, 2) == 1
    me = lax.axis_index("seq")
    return [
        jnp.bitwise_xor(me, jnp.where(odd, odd_step, even_step))
        for even_step, odd_step in zip(*there)
    ]


def scores_of(query, keys):
    return lax.dot_general(
        query, keys, (((1,), (1,)), ((), ())), preferred_element_type=jnp.float32
    )


def softmax_parts(scores, values):
    tops = [jnp.max(score, axis=1, keepdims=True) for score in scores]
    expos = [jnp.exp2((score - top) * EXPO_SCALE) for score, top in zip(scores, tops)]
    totals = [jnp.sum(expo, axis=1, keepdims=True) for expo in expos]
    mixed = [
        jnp.dot(expo.astype(jnp.bfloat16), value, preferred_element_type=jnp.float32)
        for expo, value in zip(expos, values)
    ]
    parts = [(mix * (1.0 / total)).astype(jnp.bfloat16) for mix, total in zip(mixed, totals)]
    lses = [top * EXPO_SCALE + jnp.log2(total) for top, total in zip(tops, totals)]
    return parts, lses


def as_row(column, offset):
    shape = (column.shape[0], LANES)
    row_at = lax.broadcasted_iota(jnp.int32, shape, 0)
    lane_at = lax.broadcasted_iota(jnp.int32, shape, 1)
    spread = jnp.where(lane_at == row_at + offset, column, 0.0)
    return jnp.sum(spread, axis=0, keepdims=True)


def stat_tile(rows):
    at = lax.broadcasted_iota(jnp.int32, (STAT_ROWS, LANES), 0)
    tile = jnp.zeros((STAT_ROWS, LANES), jnp.float32)
    count = len(rows)
    for index, row in enumerate(rows):
        high = row.astype(jnp.bfloat16).astype(jnp.float32)
        middle = (row - high).astype(jnp.bfloat16).astype(jnp.float32)
        low = row - high - middle
        for part, value in enumerate((high, middle, low)):
            tile = jnp.where(at == part * count + index, value, tile)
    return tile.astype(jnp.bfloat16)


def stat_rows_of(tile, count):
    wide = tile.astype(jnp.float32)
    return [
        wide[index : index + 1]
        + wide[count + index : count + index + 1]
        + wide[2 * count + index : 2 * count + index + 1]
        for index in range(count)
    ]


def stat_count(rows):
    return -(-rows // LANES)


def split_kernel(there, span_ref, query_ref, *refs):
    out_refs, arrived = refs[:-1], refs[-1]
    rows = query_ref.shape[0]
    copies = []
    for peer, out_ref in zip(peers_of(there, 0), out_refs):
        head = pl.multiple_of(peer * HD, HD)
        copies.append((query_ref.at[:, pl.ds(head, HD)], out_ref.at[:rows]))
    copies = [
        pltpu.make_async_copy(source, target, arrived.at[index])
        for index, (source, target) in enumerate(copies)
    ]
    for copy in copies:
        copy.start()
    width = jnp.full((STAT_ROWS, HD), span_ref[0].astype(jnp.float32)).astype(jnp.bfloat16)
    for out_ref in out_refs:
        out_ref[rows:, :] = width
    for copy in copies:
        copy.wait()


def halo_kernel(rows_ref, _, out_ref):
    out_ref[...] = rows_ref[...]


def far_kernel(
    there, chosen, span_ref, global_ref, random_ref, key_ref, value_ref, *refs
):
    span = span_ref[0]
    last = key_ref.shape[0] // BLK - 1

    def block(ref, at):
        if isinstance(at, int):
            return ref[at * BLK : (at + 1) * BLK, :]
        return ref[pl.ds(pl.multiple_of(at * BLK, BLK), BLK), :]

    glob_keys = [block(key_ref, global_ref[g]) for g in range(GLOB)]
    glob_values = [block(value_ref, global_ref[g]) for g in range(GLOB)]
    peers = [peers_of(there, 0)[at] for at in chosen]
    query_refs, out_refs = refs[: len(peers)], refs[len(peers) :]
    rows = query_refs[0].shape[0] - STAT_ROWS
    for chunk, query_ref, out_ref in zip(peers, query_refs, out_refs):
        blocks = rows // BLK
        first = chunk == 0
        all_scores, all_picks = [], []
        for b in range(blocks):
            query = query_ref[b * BLK : (b + 1) * BLK, :]
            base = (chunk * blocks + b) * RAND
            picks = [random_ref[base + r] for r in range(RAND)]
            keys = glob_keys + [block(key_ref, pick) for pick in picks]
            known = len(keys) * BLK
            spare = [last + 1 + b - w for w in range(b + 1, WMAX)]
            keys = keys + [block(key_ref, at) for at in spare]
            scores = scores_of(query, jnp.concatenate(keys, axis=0))
            if spare:
                open_slots = jnp.where(first, jnp.clip(span - (b + 1), 0, len(spare)), 0)
                lane_at = lax.broadcasted_iota(jnp.int32, scores.shape, 1)
                scores = jnp.where(lane_at < known + open_slots * BLK, scores, MASKED)
            all_scores.append(scores)
            all_picks.append(picks + spare)
        all_values = [
            jnp.concatenate(glob_values + [block(value_ref, at) for at in picks], axis=0)
            for picks in all_picks
        ]
        parts, lses = softmax_parts(all_scores, all_values)
        stats = []
        for b in range(blocks):
            row = as_row(lses[b], (b * BLK) % LANES)
            if (b * BLK) % LANES:
                stats[-1] = stats[-1] + row
            else:
                stats.append(row)
        tile = stat_tile(stats)
        for b in range(blocks):
            out_ref[b * BLK : (b + 1) * BLK, :] = parts[b]
        out_ref[rows:, :] = tile


def near_rows(
    there, first, last, query_ref, key_ref, value_ref, halo_ref, came_refs, out_ref
):
    rows = query_ref.shape[0]
    halo = (WMAX - 1) * BLK
    starts = list(range(first, last, 2 * BLK))
    sizes = [min(2 * BLK, last - start) for start in starts]
    leads = [
        halo if start < halo else min(-(-(size + halo) // LANES) * LANES - size, start)
        for start, size in zip(starts, sizes)
    ]
    peers = peers_of(there, 0)
    for peer, came_ref in zip(peers, came_refs):
        all_lanes = [pl.ds(pl.multiple_of(peer * HD, HD), HD)]
        all_scores, all_values = [], []
        for lanes in all_lanes:
            width = came_ref[rows:, :].astype(jnp.float32)[:1]
            width = jnp.concatenate([width] * ((2 * BLK + halo) // LANES), axis=1)
            for start, size, lead in zip(starts, sizes, leads):
                query = query_ref[start : start + size, lanes]
                if start < lead:
                    keys = [halo_ref[0, start:, lanes], key_ref[: start + size, lanes]]
                    values = [halo_ref[1, start:, lanes], value_ref[: start + size, lanes]]
                    keys, values = jnp.concatenate(keys, axis=0), jnp.concatenate(values, axis=0)
                else:
                    keys = key_ref[start - lead : start + size, lanes]
                    values = value_ref[start - lead : start + size, lanes]
                scores = scores_of(query, keys)
                row_at = lax.broadcasted_iota(jnp.int32, scores.shape, 0)
                lane_at = lax.broadcasted_iota(jnp.int32, scores.shape, 1)
                slot = (lane_at // BLK - row_at // BLK - lead // BLK).astype(jnp.float32)
                allowed = (lane_at <= row_at + lead) & (slot + width[:, : size + lead] >= 1.0)
                if start < lead:
                    closed = jnp.where(lax.axis_index("seq") == 0, lead - start, 0)
                    allowed = allowed & (lane_at >= closed)
                all_scores.append(jnp.where(allowed, scores, MASKED))
                all_values.append(values)
        parts, lses = softmax_parts(all_scores, all_values)
        for index, lanes in enumerate(all_lanes):
            own = slice(index * len(starts), (index + 1) * len(starts))
            tile = stat_tile([as_row(lse, 0) for lse in lses[own]])
            for start, size, part in zip(starts, sizes, parts[own]):
                out_ref[start - first : start - first + size, lanes] = part
            out_ref[last - first : last - first + STAT_ROWS, lanes] = tile


def packed_at(index, first, wide):
    across = wide // HD
    row, lane = first + index // across * STAT_ROWS, index % across * HD
    return slice(row, row + STAT_ROWS), slice(lane, lane + HD)


def near_inner_kernel(there, query_ref, key_ref, value_ref, own_ref, *refs):
    rows, wide = query_ref.shape
    halo = (WMAX - 1) * BLK
    came_refs, out_ref = refs[:-1], refs[-1]
    near_rows(there, halo, rows, query_ref, key_ref, value_ref, None, came_refs, out_ref)
    for index in range(own_ref.shape[0] // STAT_ROWS):
        at = packed_at(index, rows - halo + STAT_ROWS, wide)
        out_ref[at] = own_ref[index * STAT_ROWS : (index + 1) * STAT_ROWS, :]


def near_edge_kernel(there, query_ref, key_ref, value_ref, odd_ref, even_ref, *refs):
    halo = (WMAX - 1) * BLK
    came_refs, out_ref, halo_ref = refs[: len(there[0])], refs[-2], refs[-1]
    halo_ref[...] = odd_ref[...] + even_ref[...]
    near_rows(there, 0, halo, query_ref, key_ref, value_ref, halo_ref, came_refs, out_ref)


def merge_kernel(there, edge_ref, inner_ref, *refs):
    far_refs, out_ref, own_ref = refs[:-2], refs[-2], refs[-1]
    rows, wide = out_ref.shape
    halo = (WMAX - 1) * BLK
    for index in range(own_ref.shape[0] // STAT_ROWS):
        at = packed_at(index, rows - halo + STAT_ROWS, wide)
        own_ref[index * STAT_ROWS : (index + 1) * STAT_ROWS, :] = inner_ref[at]
    count = stat_count(rows)
    for peer, far_ref in zip(peers_of(there, -1), (*far_refs, own_ref)):
        lanes = pl.ds(pl.multiple_of(peer * HD, HD), HD)
        far_stats = stat_rows_of(far_ref[rows:, :], count)
        near_stats = stat_rows_of(edge_ref[halo:, lanes], 1) + stat_rows_of(
            inner_ref[rows - halo : rows - halo + STAT_ROWS, lanes], count - 1
        )
        for group in range(count):
            start = group * LANES
            size = min(LANES, rows - start)
            share = 1.0 / (1.0 + jnp.exp2(near_stats[group] - far_stats[group]))
            row_at = lax.broadcasted_iota(jnp.int32, (size, LANES), 0)
            lane_at = lax.broadcasted_iota(jnp.int32, (size, LANES), 1)
            column = jnp.sum(
                jnp.where(row_at == lane_at, share, 0.0), axis=1, keepdims=True
            )
            far = far_ref[start : start + size, :].astype(jnp.float32)
            if start < halo:
                near = edge_ref[start : start + size, lanes].astype(jnp.float32)
            else:
                near = inner_ref[start - halo : start - halo + size, lanes].astype(jnp.float32)
            out_ref[start : start + size, lanes] = (
                far * column + near * (1.0 - column)
            ).astype(jnp.bfloat16)


def params(shard):
    return pltpu.CompilerParams(vmem_limit_bytes=VMEM_BASE + 14 * 2 * math.prod(shard.shape))


def per_device(
    queries, keys_new, values_new, keys_cache, values_cache, window, global_blocks, random_blocks
):
    section_count = lax.axis_size("section")
    seq_count = lax.axis_size("seq")
    rows, wide = queries.shape[1], queries.shape[2]
    halo = (WMAX - 1) * BLK
    heads = wide // HD
    bf16 = jnp.bfloat16
    half = max(seq_count // 2, 1)
    inner, outer = list(range(1, half)), list(range(seq_count - 1, half - 1, -1))
    there = [outer + inner + [0], inner + outer + [0]]

    chunk_shape = jax.ShapeDtypeStruct((rows + STAT_ROWS, HD), bf16)
    chunk_shape = jax.ShapeDtypeStruct((rows + STAT_ROWS, HD), bf16)
    sent = pl.pallas_call(
        functools.partial(split_kernel, there),
        out_shape=[chunk_shape] * seq_count,
        in_specs=[whole_smem, in_hbm],
        out_specs=[whole_vmem] * seq_count,
        scratch_shapes=[pltpu.SemaphoreType.DMA((seq_count,))],
        compiler_params=params(queries),
        cost_estimate=pl.CostEstimate(flops=0, bytes_accessed=5 * rows * wide, transcendentals=0),
        name="split",
    )(window[0], queries[0])

    def linked(shard, by, steps):
        pairs = [
            (
                s * seq_count + t,
                (s + by) % section_count * seq_count + (t ^ steps[s % 2]),
            )
            for s in range(section_count)
            for t in range(seq_count)
        ]
        return lax.ppermute(shard, ("section", "seq"), pairs)

    came = [linked(shard, 0, steps) for shard, steps in zip(sent[:-1], zip(*there))]
    came.append(sent[-1])
    def linked(shard, by, steps):
        pairs = [
            (
                s * seq_count + t,
                (s + by) % section_count * seq_count + (t ^ steps[s % 2]),
            )
            for s in range(section_count)
            for t in range(seq_count)
        ]
        return lax.ppermute(shard, ("section", "seq"), pairs)

    came = [linked(shard, 0, steps) for shard, steps in zip(sent[:-1], zip(*there))]
    came.append(sent[-1])
    tails = jnp.stack([keys_new[0, rows - halo :], values_new[0, rows - halo :]])

    def halo_from(parity, after):
        mine = tails if after is None else pl.pallas_call(
            halo_kernel,
            out_shape=jax.ShapeDtypeStruct(tails.shape, bf16),
            in_specs=[whole_vmem, anywhere],
            out_specs=whole_vmem,
            compiler_params=params(queries),
            name="halo",
        )(tails, after)
        pairs = [
            (s * seq_count + t, s * seq_count + t + 1)
            for s in range(parity, section_count, 2)
            for t in range(seq_count - 1)
        ]
        return lax.ppermute(mine, ("section", "seq"), pairs)

    halos = [halo_from(0, None), halo_from(1, came[0])]
    picks = random_blocks[0].reshape(-1)

    def far_call(chosen):
        count = len(chosen)
        return pl.pallas_call(
            functools.partial(far_kernel, there, chosen),
            out_shape=[chunk_shape] * count,
            in_specs=[whole_smem] * 3 + [whole_vmem] * (2 + count),
            out_specs=[whole_vmem] * count,
            compiler_params=params(queries),
            cost_estimate=pl.CostEstimate(
                flops=40 * count * rows * 320 * HD * 4,
                bytes_accessed=2 * 2 * keys_cache.shape[1] * HD + 4 * count * rows * HD,
                transcendentals=count * rows * 320,
            ),
            name="far",
        )(
            window[0],
            global_blocks[0],
            picks,
            keys_cache[0],
            values_cache[0],
            *[came[at] for at in chosen],
        )

    late = list(range(seq_count - 1 - seq_count // 4, seq_count - 1))
    early = [at for at in range(seq_count) if at not in late]
    far = dict(zip(early, far_call(early)))
    if late:
        far.update(zip(late, far_call(late)))
    far = [far[at] for at in range(seq_count)]
    handed = [linked(shard, 1, steps) for shard, steps in zip(far[:-1], zip(*there))]

    def near_call(kernel, name, near_part, out_rows, vmem_count, scratch, *operands):
        return pl.pallas_call(
            functools.partial(kernel, there),
            out_shape=jax.ShapeDtypeStruct((out_rows, wide), bf16),
            in_specs=[
                whole_vmem if index < 3 + vmem_count else anywhere
                for index in range(3 + len(operands))
            ],
            out_specs=whole_vmem,
            scratch_shapes=scratch,
            compiler_params=params(queries),
            cost_estimate=pl.CostEstimate(
                flops=40 * heads * near_part * 256 * HD * 4,
                bytes_accessed=9 * near_part * wide,
                transcendentals=heads * near_part * 256,
            ),
            name=name,
        )(queries[0], keys_new[0], values_new[0], *operands)

    packed_rows = -(-(rows + STAT_ROWS) // (STAT_ROWS * heads)) * STAT_ROWS
    inner_part = near_call(
        near_inner_kernel, "near_inner", rows - halo, rows - halo + STAT_ROWS + packed_rows,
        1 + seq_count, [], far[-1], *came,
    )
    edge_part = near_call(
        near_edge_kernel, "near_edge", halo, halo + STAT_ROWS,
        2 + seq_count, [pltpu.VMEM(tails.shape, bf16)], *halos, *came, *handed[:2],
    )
    handed_inner = linked(inner_part, 1, [0, 0])
    handed_edge = linked(edge_part, 1, [0, 0])

    merged = pl.pallas_call(
        functools.partial(merge_kernel, there),
        out_shape=jax.ShapeDtypeStruct((rows, wide), bf16),
        in_specs=[whole_vmem] * (1 + seq_count),
        out_specs=whole_vmem,
        scratch_shapes=[pltpu.VMEM(chunk_shape.shape, bf16)],
        compiler_params=params(queries),
        cost_estimate=pl.CostEstimate(flops=0, bytes_accessed=6 * rows * wide, transcendentals=0),
        name="merge",
    )(handed_edge, handed_inner, *handed)
    return merged[None]


def solution(mesh):
    placed = (
        P("section", "seq", None),
        P("section", "seq", None),
        P("section", "seq", None),
        P("section", None, "seq"),
        P("section", None, "seq"),
        P("section", "seq"),
        P("section", None),
        P("section", None, None),
    )
    return jax.shard_map(
        per_device, mesh=mesh, in_specs=placed, out_specs=P("section", "seq", None), check_vma=False
    )
```

```python
import functools
import math

import jax
import jax.numpy as jnp
from jax import lax
from jax.experimental import pallas as pl
from jax.experimental.pallas import tpu as pltpu
from jax.sharding import PartitionSpec as P

HD = 128
BLK = 64
WMAX = 3
GLOB = 2
RAND = 3
LANES = 128
STAT_ROWS = 16
MASKED = -1e30
EXPO_SCALE = math.log2(math.e) / math.sqrt(HD)
VMEM_BASE = 12 * 1024 * 1024

whole_vmem = pl.BlockSpec(memory_space=pltpu.VMEM)
anywhere = pl.BlockSpec(memory_space=pl.ANY)
in_hbm = pl.BlockSpec(memory_space=pltpu.HBM)
whole_smem = pl.BlockSpec(memory_space=pltpu.SMEM)


def peers_of(there, by):
    count = lax.axis_size("section")
    other = lax.rem(lax.axis_index("section") + (by + count), count)
    odd = lax.rem(other, 2) == 1
    me = lax.axis_index("seq")
    return [
        jnp.bitwise_xor(me, jnp.where(odd, odd_step, even_step))
        for even_step, odd_step in zip(*there)
    ]


def scores_of(query, keys):
    return lax.dot_general(
        query, keys, (((1,), (1,)), ((), ())), preferred_element_type=jnp.float32
    )


def softmax_parts(scores, values):
    tops = [jnp.max(score, axis=1, keepdims=True) for score in scores]
    expos = [jnp.exp2((score - top) * EXPO_SCALE) for score, top in zip(scores, tops)]
    totals = [jnp.sum(expo, axis=1, keepdims=True) for expo in expos]
    mixed = [
        jnp.dot(expo.astype(jnp.bfloat16), value, preferred_element_type=jnp.float32)
        for expo, value in zip(expos, values)
    ]
    parts = [(mix * (1.0 / total)).astype(jnp.bfloat16) for mix, total in zip(mixed, totals)]
    lses = [top * EXPO_SCALE + jnp.log2(total) for top, total in zip(tops, totals)]
    return parts, lses


def as_row(column, offset):
    shape = (column.shape[0], LANES)
    row_at = lax.broadcasted_iota(jnp.int32, shape, 0)
    lane_at = lax.broadcasted_iota(jnp.int32, shape, 1)
    spread = jnp.where(lane_at == row_at + offset, column, 0.0)
    return jnp.sum(spread, axis=0, keepdims=True)


def stat_tile(rows):
    at = lax.broadcasted_iota(jnp.int32, (STAT_ROWS, LANES), 0)
    tile = jnp.zeros((STAT_ROWS, LANES), jnp.float32)
    count = len(rows)
    for index, row in enumerate(rows):
        high = row.astype(jnp.bfloat16).astype(jnp.float32)
        middle = (row - high).astype(jnp.bfloat16).astype(jnp.float32)
        low = row - high - middle
        for part, value in enumerate((high, middle, low)):
            tile = jnp.where(at == part * count + index, value, tile)
    return tile.astype(jnp.bfloat16)


def stat_rows_of(tile, count):
    wide = tile.astype(jnp.float32)
    return [
        wide[index : index + 1]
        + wide[count + index : count + index + 1]
        + wide[2 * count + index : 2 * count + index + 1]
        for index in range(count)
    ]


def stat_count(rows):
    return -(-rows // LANES)


def split_kernel(there, span_ref, query_ref, *refs):
    out_refs, arrived = refs[:-1], refs[-1]
    rows = query_ref.shape[0]
    copies = []
    for peer, out_ref in zip(peers_of(there, 0), out_refs):
        head = pl.multiple_of(peer * HD, HD)
        copies.append((query_ref.at[:, pl.ds(head, HD)], out_ref.at[:rows]))
    copies = [
        pltpu.make_async_copy(source, target, arrived.at[index])
        for index, (source, target) in enumerate(copies)
    ]
    for copy in copies:
        copy.start()
    width = jnp.full((STAT_ROWS, HD), span_ref[0].astype(jnp.float32)).astype(jnp.bfloat16)
    for out_ref in out_refs:
        out_ref[rows:, :] = width
    for copy in copies:
        copy.wait()


def halo_kernel(rows_ref, _, out_ref):
    out_ref[...] = rows_ref[...]


def far_kernel(
    there, chosen, span_ref, global_ref, random_ref, key_ref, value_ref, *refs
):
    span = span_ref[0]
    last = key_ref.shape[0] // BLK - 1

    def block(ref, at):
        if isinstance(at, int):
            return ref[at * BLK : (at + 1) * BLK, :]
        return ref[pl.ds(pl.multiple_of(at * BLK, BLK), BLK), :]

    glob_keys = [block(key_ref, global_ref[g]) for g in range(GLOB)]
    glob_values = [block(value_ref, global_ref[g]) for g in range(GLOB)]
    peers = [peers_of(there, 0)[at] for at in chosen]
    query_refs, out_refs = refs[: len(peers)], refs[len(peers) :]
    rows = query_refs[0].shape[0] - STAT_ROWS
    for chunk, query_ref, out_ref in zip(peers, query_refs, out_refs):
        blocks = rows // BLK
        first = chunk == 0
        all_scores, all_picks = [], []
        for b in range(blocks):
            query = query_ref[b * BLK : (b + 1) * BLK, :]
            base = (chunk * blocks + b) * RAND
            picks = [random_ref[base + r] for r in range(RAND)]
            keys = glob_keys + [block(key_ref, pick) for pick in picks]
            known = len(keys) * BLK
            spare = [last + 1 + b - w for w in range(b + 1, WMAX)]
            keys = keys + [block(key_ref, at) for at in spare]
            scores = scores_of(query, jnp.concatenate(keys, axis=0))
            if spare:
                open_slots = jnp.where(first, jnp.clip(span - (b + 1), 0, len(spare)), 0)
                lane_at = lax.broadcasted_iota(jnp.int32, scores.shape, 1)
                scores = jnp.where(lane_at < known + open_slots * BLK, scores, MASKED)
            all_scores.append(scores)
            all_picks.append(picks + spare)
        all_values = [
            jnp.concatenate(glob_values + [block(value_ref, at) for at in picks], axis=0)
            for picks in all_picks
        ]
        parts, lses = softmax_parts(all_scores, all_values)
        stats = []
        for b in range(blocks):
            row = as_row(lses[b], (b * BLK) % LANES)
            if (b * BLK) % LANES:
                stats[-1] = stats[-1] + row
            else:
                stats.append(row)
        tile = stat_tile(stats)
        for b in range(blocks):
            out_ref[b * BLK : (b + 1) * BLK, :] = parts[b]
        out_ref[rows:, :] = tile


def near_rows(
    there, first, last, query_ref, key_ref, value_ref, halo_ref, came_refs, out_ref
):
    rows = query_ref.shape[0]
    halo = (WMAX - 1) * BLK
    starts = list(range(first, last, 2 * BLK))
    sizes = [min(2 * BLK, last - start) for start in starts]
    leads = [
        halo if start < halo else min(-(-(size + halo) // LANES) * LANES - size, start)
        for start, size in zip(starts, sizes)
    ]
    peers = peers_of(there, 0)
    together = min(len(starts), 2)
    for begin in range(0, len(peers), together):
        pair = range(begin, min(begin + together, len(peers)))
        all_lanes = [pl.ds(pl.multiple_of(peers[at] * HD, HD), HD) for at in pair]
        all_scores, all_values = [], []
        for at, lanes in zip(pair, all_lanes):
            width = came_refs[at][rows:, :].astype(jnp.float32)[:1]
            width = jnp.concatenate([width] * ((2 * BLK + halo) // LANES), axis=1)
            for start, size, lead in zip(starts, sizes, leads):
                query = query_ref[start : start + size, lanes]
                if start < lead:
                    keys = [halo_ref[0, start:, lanes], key_ref[: start + size, lanes]]
                    values = [halo_ref[1, start:, lanes], value_ref[: start + size, lanes]]
                    keys, values = jnp.concatenate(keys, axis=0), jnp.concatenate(values, axis=0)
                else:
                    keys = key_ref[start - lead : start + size, lanes]
                    values = value_ref[start - lead : start + size, lanes]
                scores = scores_of(query, keys)
                row_at = lax.broadcasted_iota(jnp.int32, scores.shape, 0)
                lane_at = lax.broadcasted_iota(jnp.int32, scores.shape, 1)
                slot = (lane_at // BLK - row_at // BLK - lead // BLK).astype(jnp.float32)
                allowed = (lane_at <= row_at + lead) & (slot + width[:, : size + lead] >= 1.0)
                if start < lead:
                    closed = jnp.where(lax.axis_index("seq") == 0, lead - start, 0)
                    allowed = allowed & (lane_at >= closed)
                all_scores.append(jnp.where(allowed, scores, MASKED))
                all_values.append(values)
        parts, lses = softmax_parts(all_scores, all_values)
        for index, lanes in enumerate(all_lanes):
            own = slice(index * len(starts), (index + 1) * len(starts))
            tile = stat_tile([as_row(lse, 0) for lse in lses[own]])
            for start, size, part in zip(starts, sizes, parts[own]):
                out_ref[start - first : start - first + size, lanes] = part
            out_ref[last - first : last - first + STAT_ROWS, lanes] = tile


def packed_at(index, first, wide):
    across = wide // HD
    row, lane = first + index // across * STAT_ROWS, index % across * HD
    return slice(row, row + STAT_ROWS), slice(lane, lane + HD)


def near_inner_kernel(there, query_ref, key_ref, value_ref, own_ref, *refs):
    rows, wide = query_ref.shape
    halo = (WMAX - 1) * BLK
    came_refs, out_ref = refs[:-1], refs[-1]
    near_rows(there, halo, rows, query_ref, key_ref, value_ref, None, came_refs, out_ref)
    for index in range(own_ref.shape[0] // STAT_ROWS):
        at = packed_at(index, rows - halo + STAT_ROWS, wide)
        out_ref[at] = own_ref[index * STAT_ROWS : (index + 1) * STAT_ROWS, :]


def near_edge_kernel(there, query_ref, key_ref, value_ref, odd_ref, even_ref, *refs):
    halo = (WMAX - 1) * BLK
    came_refs, out_ref, halo_ref = refs[: len(there[0])], refs[-2], refs[-1]
    halo_ref[...] = odd_ref[...] + even_ref[...]
    near_rows(there, 0, halo, query_ref, key_ref, value_ref, halo_ref, came_refs, out_ref)


def merge_kernel(there, edge_ref, inner_ref, *refs):
    far_refs, out_ref, own_ref = refs[:-2], refs[-2], refs[-1]
    rows, wide = out_ref.shape
    halo = (WMAX - 1) * BLK
    for index in range(own_ref.shape[0] // STAT_ROWS):
        at = packed_at(index, rows - halo + STAT_ROWS, wide)
        own_ref[index * STAT_ROWS : (index + 1) * STAT_ROWS, :] = inner_ref[at]
    count = stat_count(rows)
    for peer, far_ref in zip(peers_of(there, -1), (*far_refs, own_ref)):
        lanes = pl.ds(pl.multiple_of(peer * HD, HD), HD)
        far_stats = stat_rows_of(far_ref[rows:, :], count)
        near_stats = stat_rows_of(edge_ref[halo:, lanes], 1) + stat_rows_of(
            inner_ref[rows - halo : rows - halo + STAT_ROWS, lanes], count - 1
        )
        for group in range(count):
            start = group * LANES
            size = min(LANES, rows - start)
            share = 1.0 / (1.0 + jnp.exp2(near_stats[group] - far_stats[group]))
            row_at = lax.broadcasted_iota(jnp.int32, (size, LANES), 0)
            lane_at = lax.broadcasted_iota(jnp.int32, (size, LANES), 1)
            column = jnp.sum(
                jnp.where(row_at == lane_at, share, 0.0), axis=1, keepdims=True
            )
            far = far_ref[start : start + size, :].astype(jnp.float32)
            if start < halo:
                near = edge_ref[start : start + size, lanes].astype(jnp.float32)
            else:
                near = inner_ref[start - halo : start - halo + size, lanes].astype(jnp.float32)
            out_ref[start : start + size, lanes] = (
                far * column + near * (1.0 - column)
            ).astype(jnp.bfloat16)


def params(shard):
    return pltpu.CompilerParams(vmem_limit_bytes=VMEM_BASE + 14 * 2 * math.prod(shard.shape))


def per_device(
    queries, keys_new, values_new, keys_cache, values_cache, window, global_blocks, random_blocks
):
    section_count = lax.axis_size("section")
    seq_count = lax.axis_size("seq")
    rows, wide = queries.shape[1], queries.shape[2]
    halo = (WMAX - 1) * BLK
    heads = wide // HD
    bf16 = jnp.bfloat16
    half = max(seq_count // 2, 1)
    inner, outer = list(range(1, half)), list(range(seq_count - 1, half - 1, -1))
    there = [outer[:1] + inner[:1] + outer[1:] + inner[1:] + [0], inner + outer + [0]]

    chunk_shape = jax.ShapeDtypeStruct((rows + STAT_ROWS, HD), bf16)
    chunk_shape = jax.ShapeDtypeStruct((rows + STAT_ROWS, HD), bf16)
    sent = pl.pallas_call(
        functools.partial(split_kernel, there),
        out_shape=[chunk_shape] * seq_count,
        in_specs=[whole_smem, in_hbm],
        out_specs=[whole_vmem] * seq_count,
        scratch_shapes=[pltpu.SemaphoreType.DMA((seq_count,))],
        compiler_params=params(queries),
        cost_estimate=pl.CostEstimate(flops=0, bytes_accessed=5 * rows * wide, transcendentals=0),
        name="split",
    )(window[0], queries[0])

    def linked(shard, by, steps):
        pairs = [
            (
                s * seq_count + t,
                (s + by) % section_count * seq_count + (t ^ steps[s % 2]),
            )
            for s in range(section_count)
            for t in range(seq_count)
        ]
        return lax.ppermute(shard, ("section", "seq"), pairs)

    came = [linked(shard, 0, steps) for shard, steps in zip(sent[:-1], zip(*there))]
    came.append(sent[-1])
    def linked(shard, by, steps):
        pairs = [
            (
                s * seq_count + t,
                (s + by) % section_count * seq_count + (t ^ steps[s % 2]),
            )
            for s in range(section_count)
            for t in range(seq_count)
        ]
        return lax.ppermute(shard, ("section", "seq"), pairs)

    came = [linked(shard, 0, steps) for shard, steps in zip(sent[:-1], zip(*there))]
    came.append(sent[-1])
    tails = jnp.stack([keys_new[0, rows - halo :], values_new[0, rows - halo :]])

    def halo_from(parity, after):
        mine = tails if after is None else pl.pallas_call(
            halo_kernel,
            out_shape=jax.ShapeDtypeStruct(tails.shape, bf16),
            in_specs=[whole_vmem, anywhere],
            out_specs=whole_vmem,
            compiler_params=params(queries),
            name="halo",
        )(tails, after)
        pairs = [
            (s * seq_count + t, s * seq_count + t + 1)
            for s in range(parity, section_count, 2)
            for t in range(seq_count - 1)
        ]
        return lax.ppermute(mine, ("section", "seq"), pairs)

    halos = [halo_from(1, None), halo_from(0, came[0])]
    picks = random_blocks[0].reshape(-1)

    def far_call(chosen):
        count = len(chosen)
        return pl.pallas_call(
            functools.partial(far_kernel, there, chosen),
            out_shape=[chunk_shape] * count,
            in_specs=[whole_smem] * 3 + [whole_vmem] * (2 + count),
            out_specs=[whole_vmem] * count,
            compiler_params=params(queries),
            cost_estimate=pl.CostEstimate(
                flops=40 * count * rows * 320 * HD * 4,
                bytes_accessed=2 * 2 * keys_cache.shape[1] * HD + 4 * count * rows * HD,
                transcendentals=count * rows * 320,
            ),
            name="far",
        )(
            window[0],
            global_blocks[0],
            picks,
            keys_cache[0],
            values_cache[0],
            *[came[at] for at in chosen],
        )

    late = list(range(seq_count - 1 - seq_count // 4, seq_count - 1))
    early = [at for at in range(seq_count) if at not in late]
    far = dict(zip(early, far_call(early)))
    if late:
        far.update(zip(late, far_call(late)))
    far = [far[at] for at in range(seq_count)]
    handed = [linked(shard, 1, steps) for shard, steps in zip(far[:-1], zip(*there))]

    def near_call(kernel, name, near_part, out_rows, vmem_count, scratch, *operands):
        return pl.pallas_call(
            functools.partial(kernel, there),
            out_shape=jax.ShapeDtypeStruct((out_rows, wide), bf16),
            in_specs=[
                whole_vmem if index < 3 + vmem_count else anywhere
                for index in range(3 + len(operands))
            ],
            out_specs=whole_vmem,
            scratch_shapes=scratch,
            compiler_params=params(queries),
            cost_estimate=pl.CostEstimate(
                flops=40 * heads * near_part * 256 * HD * 4,
                bytes_accessed=9 * near_part * wide,
                transcendentals=heads * near_part * 256,
            ),
            name=name,
        )(queries[0], keys_new[0], values_new[0], *operands)

    packed_rows = -(-(rows + STAT_ROWS) // (STAT_ROWS * heads)) * STAT_ROWS
    inner_part = near_call(
        near_inner_kernel, "near_inner", rows - halo, rows - halo + STAT_ROWS + packed_rows,
        1 + seq_count, [], far[-1], *came,
    )
    edge_part = near_call(
        near_edge_kernel, "near_edge", halo, halo + STAT_ROWS,
        2 + seq_count, [pltpu.VMEM(tails.shape, bf16)], *halos, *came, *handed[:2],
    )
    handed_inner = linked(inner_part, 1, [0, 0])
    handed_edge = linked(edge_part, 1, [0, 0])

    merged = pl.pallas_call(
        functools.partial(merge_kernel, there),
        out_shape=jax.ShapeDtypeStruct((rows, wide), bf16),
        in_specs=[whole_vmem] * (1 + seq_count),
        out_specs=whole_vmem,
        scratch_shapes=[pltpu.VMEM(chunk_shape.shape, bf16)],
        compiler_params=params(queries),
        cost_estimate=pl.CostEstimate(flops=0, bytes_accessed=6 * rows * wide, transcendentals=0),
        name="merge",
    )(handed_edge, handed_inner, *handed)
    return merged[None]


def solution(mesh):
    placed = (
        P("section", "seq", None),
        P("section", "seq", None),
        P("section", "seq", None),
        P("section", None, "seq"),
        P("section", None, "seq"),
        P("section", "seq"),
        P("section", None),
        P("section", None, None),
    )
    return jax.shard_map(
        per_device, mesh=mesh, in_specs=placed, out_specs=P("section", "seq", None), check_vma=False
    )
```

```python
import functools
import math

import jax
import jax.numpy as jnp
from jax import lax
from jax.experimental import pallas as pl
from jax.experimental.pallas import tpu as pltpu
from jax.sharding import PartitionSpec as P

HD = 128
BLK = 64
WMAX = 3
GLOB = 2
RAND = 3
LANES = 128
STAT_ROWS = 16
MASKED = -1e30
EXPO_SCALE = math.log2(math.e) / math.sqrt(HD)
VMEM_BASE = 12 * 1024 * 1024

whole_vmem = pl.BlockSpec(memory_space=pltpu.VMEM)
anywhere = pl.BlockSpec(memory_space=pl.ANY)
in_hbm = pl.BlockSpec(memory_space=pltpu.HBM)
whole_smem = pl.BlockSpec(memory_space=pltpu.SMEM)


def peers_of(there, by):
    count = lax.axis_size("section")
    other = lax.rem(lax.axis_index("section") + (by + count), count)
    odd = lax.rem(other, 2) == 1
    me = lax.axis_index("seq")
    return [
        jnp.bitwise_xor(me, jnp.where(odd, odd_step, even_step))
        for even_step, odd_step in zip(*there)
    ]


def scores_of(query, keys):
    return lax.dot_general(
        query, keys, (((1,), (1,)), ((), ())), preferred_element_type=jnp.float32
    )


def softmax_parts(scores, values):
    tops = [jnp.max(score, axis=1, keepdims=True) for score in scores]
    expos = [jnp.exp2((score - top) * EXPO_SCALE) for score, top in zip(scores, tops)]
    totals = [jnp.sum(expo, axis=1, keepdims=True) for expo in expos]
    mixed = [
        jnp.dot(expo.astype(jnp.bfloat16), value, preferred_element_type=jnp.float32)
        for expo, value in zip(expos, values)
    ]
    parts = [(mix * (1.0 / total)).astype(jnp.bfloat16) for mix, total in zip(mixed, totals)]
    lses = [top * EXPO_SCALE + jnp.log2(total) for top, total in zip(tops, totals)]
    return parts, lses


def as_row(column, offset):
    shape = (column.shape[0], LANES)
    row_at = lax.broadcasted_iota(jnp.int32, shape, 0)
    lane_at = lax.broadcasted_iota(jnp.int32, shape, 1)
    spread = jnp.where(lane_at == row_at + offset, column, 0.0)
    return jnp.sum(spread, axis=0, keepdims=True)


def stat_tile(rows):
    at = lax.broadcasted_iota(jnp.int32, (STAT_ROWS, LANES), 0)
    tile = jnp.zeros((STAT_ROWS, LANES), jnp.float32)
    count = len(rows)
    for index, row in enumerate(rows):
        high = row.astype(jnp.bfloat16).astype(jnp.float32)
        middle = (row - high).astype(jnp.bfloat16).astype(jnp.float32)
        low = row - high - middle
        for part, value in enumerate((high, middle, low)):
            tile = jnp.where(at == part * count + index, value, tile)
    return tile.astype(jnp.bfloat16)


def stat_rows_of(tile, count):
    wide = tile.astype(jnp.float32)
    return [
        wide[index : index + 1]
        + wide[count + index : count + index + 1]
        + wide[2 * count + index : 2 * count + index + 1]
        for index in range(count)
    ]


def stat_count(rows):
    return -(-rows // LANES)


def split_kernel(there, span_ref, query_ref, *refs):
    out_refs, arrived = refs[:-1], refs[-1]
    rows = query_ref.shape[0]
    copies = []
    for peer, out_ref in zip(peers_of(there, 0), out_refs):
        head = pl.multiple_of(peer * HD, HD)
        copies.append((query_ref.at[:, pl.ds(head, HD)], out_ref.at[:rows]))
    copies = [
        pltpu.make_async_copy(source, target, arrived.at[index])
        for index, (source, target) in enumerate(copies)
    ]
    for copy in copies:
        copy.start()
    width = jnp.full((STAT_ROWS, HD), span_ref[0].astype(jnp.float32)).astype(jnp.bfloat16)
    for out_ref in out_refs:
        out_ref[rows:, :] = width
    for copy in copies:
        copy.wait()


def halo_kernel(rows_ref, _, out_ref):
    out_ref[...] = rows_ref[...]


def far_kernel(
    there, chosen, span_ref, global_ref, random_ref, key_ref, value_ref, *refs
):
    span = span_ref[0]
    last = key_ref.shape[0] // BLK - 1

    def block(ref, at):
        if isinstance(at, int):
            return ref[at * BLK : (at + 1) * BLK, :]
        return ref[pl.ds(pl.multiple_of(at * BLK, BLK), BLK), :]

    glob_keys = jnp.concatenate([block(key_ref, global_ref[g]) for g in range(GLOB)], axis=0)
    glob_values = jnp.concatenate([block(value_ref, global_ref[g]) for g in range(GLOB)], axis=0)
    peers = [peers_of(there, 0)[at] for at in chosen]
    query_refs, out_refs = refs[: len(peers)], refs[len(peers) :]
    rows = query_refs[0].shape[0] - STAT_ROWS
    for chunk, query_ref, out_ref in zip(peers, query_refs, out_refs):
        blocks = rows // BLK
        first = chunk == 0
        glob_scores = scores_of(query_ref[:rows, :], glob_keys)
        all_scores, all_values = [], []
        for b in range(blocks):
            base = (chunk * blocks + b) * RAND
            spare = [last + 1 + b - w for w in range(b + 1, WMAX)]
            picks = [random_ref[base + r] for r in range(RAND)] + spare
            keys = jnp.concatenate([block(key_ref, pick) for pick in picks], axis=0)
            scores = scores_of(query_ref[b * BLK : (b + 1) * BLK, :], keys)
            if spare:
                open_slots = jnp.where(first, jnp.clip(span - (b + 1), 0, len(spare)), 0)
                lane_at = lax.broadcasted_iota(jnp.int32, scores.shape, 1)
                scores = jnp.where(lane_at < (RAND + open_slots) * BLK, scores, MASKED)
            glob = glob_scores[b * BLK : (b + 1) * BLK, :]
            all_scores.append(jnp.concatenate([glob, scores], axis=1))
            all_values.append(
                jnp.concatenate([block(value_ref, pick) for pick in picks], axis=0)
            )
        tops = [jnp.max(scores, axis=1, keepdims=True) for scores in all_scores]
        expos = [
            jnp.exp2((scores - top) * EXPO_SCALE) for scores, top in zip(all_scores, tops)
        ]
        totals = [jnp.sum(expo, axis=1, keepdims=True) for expo in expos]
        weights = [expo.astype(jnp.bfloat16) for expo in expos]
        shared = GLOB * BLK
        glob_mixed = jnp.dot(
            jnp.concatenate([weight[:, :shared] for weight in weights], axis=0),
            glob_values,
            preferred_element_type=jnp.float32,
        )
        mixed = [
            glob_mixed[b * BLK : (b + 1) * BLK, :]
            + jnp.dot(weight[:, shared:], value, preferred_element_type=jnp.float32)
            for b, (weight, value) in enumerate(zip(weights, all_values))
        ]
        parts = [(mix * (1.0 / total)).astype(jnp.bfloat16) for mix, total in zip(mixed, totals)]
        lses = [top * EXPO_SCALE + jnp.log2(total) for top, total in zip(tops, totals)]
        stats = []
        for b in range(blocks):
            row = as_row(lses[b], (b * BLK) % LANES)
            if (b * BLK) % LANES:
                stats[-1] = stats[-1] + row
            else:
                stats.append(row)
        tile = stat_tile(stats)
        for b in range(blocks):
            out_ref[b * BLK : (b + 1) * BLK, :] = parts[b]
        out_ref[rows:, :] = tile


def near_rows(
    there, first, last, query_ref, key_ref, value_ref, halo_ref, came_refs, out_ref
):
    rows = query_ref.shape[0]
    halo = (WMAX - 1) * BLK
    starts = list(range(first, last, 2 * BLK))
    sizes = [min(2 * BLK, last - start) for start in starts]
    leads = [
        halo if start < halo else min(-(-(size + halo) // LANES) * LANES - size, start)
        for start, size in zip(starts, sizes)
    ]
    peers = peers_of(there, 0)
    together = min(len(starts), 2)
    for begin in range(0, len(peers), together):
        pair = range(begin, min(begin + together, len(peers)))
        all_lanes = [pl.ds(pl.multiple_of(peers[at] * HD, HD), HD) for at in pair]
        all_scores, all_values = [], []
        for at, lanes in zip(pair, all_lanes):
            width = came_refs[at][rows:, :].astype(jnp.float32)[:1]
            width = jnp.concatenate([width] * ((2 * BLK + halo) // LANES), axis=1)
            for start, size, lead in zip(starts, sizes, leads):
                query = query_ref[start : start + size, lanes]
                if start < lead:
                    keys = [halo_ref[0, start:, lanes], key_ref[: start + size, lanes]]
                    values = [halo_ref[1, start:, lanes], value_ref[: start + size, lanes]]
                    keys, values = jnp.concatenate(keys, axis=0), jnp.concatenate(values, axis=0)
                else:
                    keys = key_ref[start - lead : start + size, lanes]
                    values = value_ref[start - lead : start + size, lanes]
                scores = scores_of(query, keys)
                row_at = lax.broadcasted_iota(jnp.int32, scores.shape, 0)
                lane_at = lax.broadcasted_iota(jnp.int32, scores.shape, 1)
                slot = (lane_at // BLK - row_at // BLK - lead // BLK).astype(jnp.float32)
                allowed = (lane_at <= row_at + lead) & (slot + width[:, : size + lead] >= 1.0)
                if start < lead:
                    closed = jnp.where(lax.axis_index("seq") == 0, lead - start, 0)
                    allowed = allowed & (lane_at >= closed)
                all_scores.append(jnp.where(allowed, scores, MASKED))
                all_values.append(values)
        parts, lses = softmax_parts(all_scores, all_values)
        for index, lanes in enumerate(all_lanes):
            own = slice(index * len(starts), (index + 1) * len(starts))
            tile = stat_tile([as_row(lse, 0) for lse in lses[own]])
            for start, size, part in zip(starts, sizes, parts[own]):
                out_ref[start - first : start - first + size, lanes] = part
            out_ref[last - first : last - first + STAT_ROWS, lanes] = tile


def packed_at(index, first, wide):
    across = wide // HD
    row, lane = first + index // across * STAT_ROWS, index % across * HD
    return slice(row, row + STAT_ROWS), slice(lane, lane + HD)


def near_inner_kernel(there, query_ref, key_ref, value_ref, own_ref, *refs):
    rows, wide = query_ref.shape
    halo = (WMAX - 1) * BLK
    came_refs, out_ref = refs[:-1], refs[-1]
    near_rows(there, halo, rows, query_ref, key_ref, value_ref, None, came_refs, out_ref)
    for index in range(own_ref.shape[0] // STAT_ROWS):
        at = packed_at(index, rows - halo + STAT_ROWS, wide)
        out_ref[at] = own_ref[index * STAT_ROWS : (index + 1) * STAT_ROWS, :]


def near_edge_kernel(there, query_ref, key_ref, value_ref, odd_ref, even_ref, *refs):
    halo = (WMAX - 1) * BLK
    came_refs, out_ref, halo_ref = refs[: len(there[0])], refs[-2], refs[-1]
    halo_ref[...] = odd_ref[...] + even_ref[...]
    near_rows(there, 0, halo, query_ref, key_ref, value_ref, halo_ref, came_refs, out_ref)


def merge_kernel(there, edge_ref, inner_ref, *refs):
    far_refs, out_ref, own_ref = refs[:-2], refs[-2], refs[-1]
    rows, wide = out_ref.shape
    halo = (WMAX - 1) * BLK
    for index in range(own_ref.shape[0] // STAT_ROWS):
        at = packed_at(index, rows - halo + STAT_ROWS, wide)
        own_ref[index * STAT_ROWS : (index + 1) * STAT_ROWS, :] = inner_ref[at]
    count = stat_count(rows)
    for peer, far_ref in zip(peers_of(there, -1), (*far_refs, own_ref)):
        lanes = pl.ds(pl.multiple_of(peer * HD, HD), HD)
        far_stats = stat_rows_of(far_ref[rows:, :], count)
        near_stats = stat_rows_of(edge_ref[halo:, lanes], 1) + stat_rows_of(
            inner_ref[rows - halo : rows - halo + STAT_ROWS, lanes], count - 1
        )
        for group in range(count):
            start = group * LANES
            size = min(LANES, rows - start)
            share = 1.0 / (1.0 + jnp.exp2(near_stats[group] - far_stats[group]))
            row_at = lax.broadcasted_iota(jnp.int32, (size, LANES), 0)
            lane_at = lax.broadcasted_iota(jnp.int32, (size, LANES), 1)
            column = jnp.sum(
                jnp.where(row_at == lane_at, share, 0.0), axis=1, keepdims=True
            )
            far = far_ref[start : start + size, :].astype(jnp.float32)
            if start < halo:
                near = edge_ref[start : start + size, lanes].astype(jnp.float32)
            else:
                near = inner_ref[start - halo : start - halo + size, lanes].astype(jnp.float32)
            out_ref[start : start + size, lanes] = (
                far * column + near * (1.0 - column)
            ).astype(jnp.bfloat16)


def params(shard):
    return pltpu.CompilerParams(vmem_limit_bytes=VMEM_BASE + 14 * 2 * math.prod(shard.shape))


def per_device(
    queries, keys_new, values_new, keys_cache, values_cache, window, global_blocks, random_blocks
):
    section_count = lax.axis_size("section")
    seq_count = lax.axis_size("seq")
    rows, wide = queries.shape[1], queries.shape[2]
    halo = (WMAX - 1) * BLK
    heads = wide // HD
    bf16 = jnp.bfloat16
    half = max(seq_count // 2, 1)
    inner, outer = list(range(1, half)), list(range(seq_count - 1, half - 1, -1))
    there = [outer + inner + [0], inner + outer + [0]]

    chunk_shape = jax.ShapeDtypeStruct((rows + STAT_ROWS, HD), bf16)
    chunk_shape = jax.ShapeDtypeStruct((rows + STAT_ROWS, HD), bf16)
    sent = pl.pallas_call(
        functools.partial(split_kernel, there),
        out_shape=[chunk_shape] * seq_count,
        in_specs=[whole_smem, in_hbm],
        out_specs=[whole_vmem] * seq_count,
        scratch_shapes=[pltpu.SemaphoreType.DMA((seq_count,))],
        compiler_params=params(queries),
        cost_estimate=pl.CostEstimate(flops=0, bytes_accessed=5 * rows * wide, transcendentals=0),
        name="split",
    )(window[0], queries[0])

    def linked(shard, by, steps):
        pairs = [
            (
                s * seq_count + t,
                (s + by) % section_count * seq_count + (t ^ steps[s % 2]),
            )
            for s in range(section_count)
            for t in range(seq_count)
        ]
        return lax.ppermute(shard, ("section", "seq"), pairs)

    came = [linked(shard, 0, steps) for shard, steps in zip(sent[:-1], zip(*there))]
    came.append(sent[-1])
    def linked(shard, by, steps):
        pairs = [
            (
                s * seq_count + t,
                (s + by) % section_count * seq_count + (t ^ steps[s % 2]),
            )
            for s in range(section_count)
            for t in range(seq_count)
        ]
        return lax.ppermute(shard, ("section", "seq"), pairs)

    came = [linked(shard, 0, steps) for shard, steps in zip(sent[:-1], zip(*there))]
    came.append(sent[-1])
    tails = jnp.stack([keys_new[0, rows - halo :], values_new[0, rows - halo :]])

    def halo_from(parity, after):
        mine = tails if after is None else pl.pallas_call(
            halo_kernel,
            out_shape=jax.ShapeDtypeStruct(tails.shape, bf16),
            in_specs=[whole_vmem, anywhere],
            out_specs=whole_vmem,
            compiler_params=params(queries),
            name="halo",
        )(tails, after)
        pairs = [
            (s * seq_count + t, s * seq_count + t + 1)
            for s in range(parity, section_count, 2)
            for t in range(seq_count - 1)
        ]
        return lax.ppermute(mine, ("section", "seq"), pairs)

    halos = [halo_from(1, None), halo_from(0, came[0])]
    picks = random_blocks[0].reshape(-1)

    def far_call(chosen):
        count = len(chosen)
        return pl.pallas_call(
            functools.partial(far_kernel, there, chosen),
            out_shape=[chunk_shape] * count,
            in_specs=[whole_smem] * 3 + [whole_vmem] * (2 + count),
            out_specs=[whole_vmem] * count,
            compiler_params=params(queries),
            cost_estimate=pl.CostEstimate(
                flops=40 * count * rows * 320 * HD * 4,
                bytes_accessed=2 * 2 * keys_cache.shape[1] * HD + 4 * count * rows * HD,
                transcendentals=count * rows * 320,
            ),
            name="far",
        )(
            window[0],
            global_blocks[0],
            picks,
            keys_cache[0],
            values_cache[0],
            *[came[at] for at in chosen],
        )

    late = list(range(seq_count - 1 - seq_count // 4, seq_count - 1))
    early = [at for at in range(seq_count) if at not in late]
    far = dict(zip(early, far_call(early)))
    if late:
        far.update(zip(late, far_call(late)))
    far = [far[at] for at in range(seq_count)]
    handed = [linked(shard, 1, steps) for shard, steps in zip(far[:-1], zip(*there))]

    def near_call(kernel, name, near_part, out_rows, vmem_count, scratch, *operands):
        return pl.pallas_call(
            functools.partial(kernel, there),
            out_shape=jax.ShapeDtypeStruct((out_rows, wide), bf16),
            in_specs=[
                whole_vmem if index < 3 + vmem_count else anywhere
                for index in range(3 + len(operands))
            ],
            out_specs=whole_vmem,
            scratch_shapes=scratch,
            compiler_params=params(queries),
            cost_estimate=pl.CostEstimate(
                flops=40 * heads * near_part * 256 * HD * 4,
                bytes_accessed=9 * near_part * wide,
                transcendentals=heads * near_part * 256,
            ),
            name=name,
        )(queries[0], keys_new[0], values_new[0], *operands)

    packed_rows = -(-(rows + STAT_ROWS) // (STAT_ROWS * heads)) * STAT_ROWS
    inner_part = near_call(
        near_inner_kernel, "near_inner", rows - halo, rows - halo + STAT_ROWS + packed_rows,
        1 + seq_count, [], far[-1], *came,
    )
    edge_part = near_call(
        near_edge_kernel, "near_edge", halo, halo + STAT_ROWS,
        2 + seq_count, [pltpu.VMEM(tails.shape, bf16)], *halos, *came, *handed[:2],
    )
    handed_inner = linked(inner_part, 1, [0, 0])
    handed_edge = linked(edge_part, 1, [0, 0])

    merged = pl.pallas_call(
        functools.partial(merge_kernel, there),
        out_shape=jax.ShapeDtypeStruct((rows, wide), bf16),
        in_specs=[whole_vmem] * (1 + seq_count),
        out_specs=whole_vmem,
        scratch_shapes=[pltpu.VMEM(chunk_shape.shape, bf16)],
        compiler_params=params(queries),
        cost_estimate=pl.CostEstimate(flops=0, bytes_accessed=6 * rows * wide, transcendentals=0),
        name="merge",
    )(handed_edge, handed_inner, *handed)
    return merged[None]


def solution(mesh):
    placed = (
        P("section", "seq", None),
        P("section", "seq", None),
        P("section", "seq", None),
        P("section", None, "seq"),
        P("section", None, "seq"),
        P("section", "seq"),
        P("section", None),
        P("section", None, None),
    )
    return jax.shard_map(
        per_device, mesh=mesh, in_specs=placed, out_specs=P("section", "seq", None), check_vma=False
    )
```

```python
import functools
import math

import jax
import jax.numpy as jnp
from jax import lax
from jax.experimental import pallas as pl
from jax.experimental.pallas import tpu as pltpu
from jax.sharding import PartitionSpec as P

HD = 128
BLK = 64
WMAX = 3
GLOB = 2
RAND = 3
LANES = 128
STAT_ROWS = 16
MASKED = -1e30
EXPO_SCALE = math.log2(math.e) / math.sqrt(HD)
VMEM_BASE = 12 * 1024 * 1024

whole_vmem = pl.BlockSpec(memory_space=pltpu.VMEM)
anywhere = pl.BlockSpec(memory_space=pl.ANY)
in_hbm = pl.BlockSpec(memory_space=pltpu.HBM)
whole_smem = pl.BlockSpec(memory_space=pltpu.SMEM)


def peers_of(there, by):
    count = lax.axis_size("section")
    other = lax.rem(lax.axis_index("section") + (by + count), count)
    odd = lax.rem(other, 2) == 1
    me = lax.axis_index("seq")
    return [
        jnp.bitwise_xor(me, jnp.where(odd, odd_step, even_step))
        for even_step, odd_step in zip(*there)
    ]


def scores_of(query, keys):
    return lax.dot_general(
        query, keys, (((1,), (1,)), ((), ())), preferred_element_type=jnp.float32
    )


def softmax_parts(scores, values):
    tops = [jnp.max(score, axis=1, keepdims=True) for score in scores]
    expos = [jnp.exp2((score - top) * EXPO_SCALE) for score, top in zip(scores, tops)]
    totals = [jnp.sum(expo, axis=1, keepdims=True) for expo in expos]
    mixed = [
        jnp.dot(expo.astype(jnp.bfloat16), value, preferred_element_type=jnp.float32)
        for expo, value in zip(expos, values)
    ]
    parts = [(mix * (1.0 / total)).astype(jnp.bfloat16) for mix, total in zip(mixed, totals)]
    lses = [top * EXPO_SCALE + jnp.log2(total) for top, total in zip(tops, totals)]
    return parts, lses


def as_row(column, offset):
    shape = (column.shape[0], LANES)
    row_at = lax.broadcasted_iota(jnp.int32, shape, 0)
    lane_at = lax.broadcasted_iota(jnp.int32, shape, 1)
    spread = jnp.where(lane_at == row_at + offset, column, 0.0)
    return jnp.sum(spread, axis=0, keepdims=True)


def stat_tile(rows):
    at = lax.broadcasted_iota(jnp.int32, (STAT_ROWS, LANES), 0)
    tile = jnp.zeros((STAT_ROWS, LANES), jnp.float32)
    count = len(rows)
    for index, row in enumerate(rows):
        high = row.astype(jnp.bfloat16).astype(jnp.float32)
        middle = (row - high).astype(jnp.bfloat16).astype(jnp.float32)
        low = row - high - middle
        for part, value in enumerate((high, middle, low)):
            tile = jnp.where(at == part * count + index, value, tile)
    return tile.astype(jnp.bfloat16)


def stat_rows_of(tile, count):
    wide = tile.astype(jnp.float32)
    return [
        wide[index : index + 1]
        + wide[count + index : count + index + 1]
        + wide[2 * count + index : 2 * count + index + 1]
        for index in range(count)
    ]


def stat_count(rows):
    return -(-rows // LANES)


def split_kernel(there, span_ref, query_ref, *refs):
    out_refs, arrived = refs[:-1], refs[-1]
    rows = query_ref.shape[0]
    copies = []
    for peer, out_ref in zip(peers_of(there, 0), out_refs):
        head = pl.multiple_of(peer * HD, HD)
        copies.append((query_ref.at[:, pl.ds(head, HD)], out_ref.at[:rows]))
    copies = [
        pltpu.make_async_copy(source, target, arrived.at[index])
        for index, (source, target) in enumerate(copies)
    ]
    for copy in copies:
        copy.start()
    width = jnp.full((STAT_ROWS, HD), span_ref[0].astype(jnp.float32)).astype(jnp.bfloat16)
    for out_ref in out_refs:
        out_ref[rows:, :] = width
    for copy in copies:
        copy.wait()


def halo_kernel(rows_ref, _, out_ref):
    out_ref[...] = rows_ref[...]


def far_kernel(
    there, back, chosen, span_ref, global_ref, random_ref, key_ref, value_ref, *refs
):
    span = span_ref[0]
    last = key_ref.shape[0] // BLK - 1

    def block(ref, at):
        if isinstance(at, int):
            return ref[at * BLK : (at + 1) * BLK, :]
        return ref[pl.ds(pl.multiple_of(at * BLK, BLK), BLK), :]

    glob_keys = [block(key_ref, global_ref[g]) for g in range(GLOB)]
    glob_values = [block(value_ref, global_ref[g]) for g in range(GLOB)]
    count = len(chosen)
    query_refs, out_refs, held_ref = refs[:count], refs[count:-1], refs[-1]
    rows = query_refs[0].shape[0] - STAT_ROWS
    odd = lax.rem(lax.axis_index("section"), 2) == 1
    moved = any(steps != others for steps, others in zip(there, back))
    if moved:
        for index, query_ref in enumerate(query_refs):
            held_ref[index] = query_ref[:rows, :]
    for index, (at, out_ref) in enumerate(zip(chosen, out_refs)):
        chunk = peers_of(back, 0)[at]
        if moved:
            even_at, odd_at = (
                chosen.index(steps.index(others[at])) for steps, others in zip(there, back)
            )
            query_ref = held_ref.at[jnp.where(odd, odd_at, even_at)]
        else:
            query_ref = query_refs[index]
        blocks = rows // BLK
        first = chunk == 0
        all_scores, all_picks = [], []
        for b in range(blocks):
            query = query_ref[b * BLK : (b + 1) * BLK, :]
            base = (chunk * blocks + b) * RAND
            picks = [random_ref[base + r] for r in range(RAND)]
            keys = glob_keys + [block(key_ref, pick) for pick in picks]
            known = len(keys) * BLK
            spare = [last + 1 + b - w for w in range(b + 1, WMAX)]
            keys = keys + [block(key_ref, at) for at in spare]
            scores = scores_of(query, jnp.concatenate(keys, axis=0))
            if spare:
                open_slots = jnp.where(first, jnp.clip(span - (b + 1), 0, len(spare)), 0)
                lane_at = lax.broadcasted_iota(jnp.int32, scores.shape, 1)
                scores = jnp.where(lane_at < known + open_slots * BLK, scores, MASKED)
            all_scores.append(scores)
            all_picks.append(picks + spare)
        all_values = [
            jnp.concatenate(glob_values + [block(value_ref, at) for at in picks], axis=0)
            for picks in all_picks
        ]
        parts, lses = softmax_parts(all_scores, all_values)
        stats = []
        for b in range(blocks):
            row = as_row(lses[b], (b * BLK) % LANES)
            if (b * BLK) % LANES:
                stats[-1] = stats[-1] + row
            else:
                stats.append(row)
        tile = stat_tile(stats)
        for b in range(blocks):
            out_ref[b * BLK : (b + 1) * BLK, :] = parts[b]
        out_ref[rows:, :] = tile


def near_rows(
    there, first, last, query_ref, key_ref, value_ref, halo_ref, came_refs, out_ref
):
    rows = query_ref.shape[0]
    halo = (WMAX - 1) * BLK
    starts = list(range(first, last, 2 * BLK))
    sizes = [min(2 * BLK, last - start) for start in starts]
    leads = [
        halo if start < halo else min(-(-(size + halo) // LANES) * LANES - size, start)
        for start, size in zip(starts, sizes)
    ]
    peers = peers_of(there, 0)
    together = min(len(starts), 2)
    for begin in range(0, len(peers), together):
        pair = range(begin, min(begin + together, len(peers)))
        all_lanes = [pl.ds(pl.multiple_of(peers[at] * HD, HD), HD) for at in pair]
        all_scores, all_values = [], []
        for at, lanes in zip(pair, all_lanes):
            width = came_refs[at][rows:, :].astype(jnp.float32)[:1]
            width = jnp.concatenate([width] * ((2 * BLK + halo) // LANES), axis=1)
            for start, size, lead in zip(starts, sizes, leads):
                query = query_ref[start : start + size, lanes]
                if start < lead:
                    keys = [halo_ref[0, start:, lanes], key_ref[: start + size, lanes]]
                    values = [halo_ref[1, start:, lanes], value_ref[: start + size, lanes]]
                    keys, values = jnp.concatenate(keys, axis=0), jnp.concatenate(values, axis=0)
                else:
                    keys = key_ref[start - lead : start + size, lanes]
                    values = value_ref[start - lead : start + size, lanes]
                scores = scores_of(query, keys)
                row_at = lax.broadcasted_iota(jnp.int32, scores.shape, 0)
                lane_at = lax.broadcasted_iota(jnp.int32, scores.shape, 1)
                slot = (lane_at // BLK - row_at // BLK - lead // BLK).astype(jnp.float32)
                allowed = (lane_at <= row_at + lead) & (slot + width[:, : size + lead] >= 1.0)
                if start < lead:
                    closed = jnp.where(lax.axis_index("seq") == 0, lead - start, 0)
                    allowed = allowed & (lane_at >= closed)
                all_scores.append(jnp.where(allowed, scores, MASKED))
                all_values.append(values)
        parts, lses = softmax_parts(all_scores, all_values)
        for index, lanes in enumerate(all_lanes):
            own = slice(index * len(starts), (index + 1) * len(starts))
            tile = stat_tile([as_row(lse, 0) for lse in lses[own]])
            for start, size, part in zip(starts, sizes, parts[own]):
                out_ref[start - first : start - first + size, lanes] = part
            out_ref[last - first : last - first + STAT_ROWS, lanes] = tile


def packed_at(index, first, wide):
    across = wide // HD
    row, lane = first + index // across * STAT_ROWS, index % across * HD
    return slice(row, row + STAT_ROWS), slice(lane, lane + HD)


def near_inner_kernel(there, query_ref, key_ref, value_ref, own_ref, *refs):
    rows, wide = query_ref.shape
    halo = (WMAX - 1) * BLK
    came_refs, out_ref = refs[:-1], refs[-1]
    near_rows(there, halo, rows, query_ref, key_ref, value_ref, None, came_refs, out_ref)
    for index in range(own_ref.shape[0] // STAT_ROWS):
        at = packed_at(index, rows - halo + STAT_ROWS, wide)
        out_ref[at] = own_ref[index * STAT_ROWS : (index + 1) * STAT_ROWS, :]


def near_edge_kernel(there, query_ref, key_ref, value_ref, odd_ref, even_ref, *refs):
    halo = (WMAX - 1) * BLK
    came_refs, out_ref, halo_ref = refs[: len(there[0])], refs[-2], refs[-1]
    halo_ref[...] = odd_ref[...] + even_ref[...]
    near_rows(there, 0, halo, query_ref, key_ref, value_ref, halo_ref, came_refs, out_ref)


def merge_kernel(there, edge_ref, inner_ref, *refs):
    far_refs, out_ref, own_ref = refs[:-2], refs[-2], refs[-1]
    rows, wide = out_ref.shape
    halo = (WMAX - 1) * BLK
    for index in range(own_ref.shape[0] // STAT_ROWS):
        at = packed_at(index, rows - halo + STAT_ROWS, wide)
        own_ref[index * STAT_ROWS : (index + 1) * STAT_ROWS, :] = inner_ref[at]
    count = stat_count(rows)
    for peer, far_ref in zip(peers_of(there, -1), (*far_refs, own_ref)):
        lanes = pl.ds(pl.multiple_of(peer * HD, HD), HD)
        far_stats = stat_rows_of(far_ref[rows:, :], count)
        near_stats = stat_rows_of(edge_ref[halo:, lanes], 1) + stat_rows_of(
            inner_ref[rows - halo : rows - halo + STAT_ROWS, lanes], count - 1
        )
        for group in range(count):
            start = group * LANES
            size = min(LANES, rows - start)
            share = 1.0 / (1.0 + jnp.exp2(near_stats[group] - far_stats[group]))
            row_at = lax.broadcasted_iota(jnp.int32, (size, LANES), 0)
            lane_at = lax.broadcasted_iota(jnp.int32, (size, LANES), 1)
            column = jnp.sum(
                jnp.where(row_at == lane_at, share, 0.0), axis=1, keepdims=True
            )
            far = far_ref[start : start + size, :].astype(jnp.float32)
            if start < halo:
                near = edge_ref[start : start + size, lanes].astype(jnp.float32)
            else:
                near = inner_ref[start - halo : start - halo + size, lanes].astype(jnp.float32)
            out_ref[start : start + size, lanes] = (
                far * column + near * (1.0 - column)
            ).astype(jnp.bfloat16)


def params(shard):
    return pltpu.CompilerParams(vmem_limit_bytes=VMEM_BASE + 14 * 2 * math.prod(shard.shape))


def per_device(
    queries, keys_new, values_new, keys_cache, values_cache, window, global_blocks, random_blocks
):
    section_count = lax.axis_size("section")
    seq_count = lax.axis_size("seq")
    rows, wide = queries.shape[1], queries.shape[2]
    halo = (WMAX - 1) * BLK
    heads = wide // HD
    bf16 = jnp.bfloat16
    half = max(seq_count // 2, 1)
    inner, outer = list(range(1, half)), list(range(seq_count - 1, half - 1, -1))
    there = [outer[:1] + inner[:1] + outer[1:] + inner[1:] + [0], inner + outer + [0]]
    back = [outer + inner + [0], inner + outer + [0]]

    chunk_shape = jax.ShapeDtypeStruct((rows + STAT_ROWS, HD), bf16)
    chunk_shape = jax.ShapeDtypeStruct((rows + STAT_ROWS, HD), bf16)
    sent = pl.pallas_call(
        functools.partial(split_kernel, there),
        out_shape=[chunk_shape] * seq_count,
        in_specs=[whole_smem, in_hbm],
        out_specs=[whole_vmem] * seq_count,
        scratch_shapes=[pltpu.SemaphoreType.DMA((seq_count,))],
        compiler_params=params(queries),
        cost_estimate=pl.CostEstimate(flops=0, bytes_accessed=5 * rows * wide, transcendentals=0),
        name="split",
    )(window[0], queries[0])

    def linked(shard, by, steps):
        pairs = [
            (
                s * seq_count + t,
                (s + by) % section_count * seq_count + (t ^ steps[s % 2]),
            )
            for s in range(section_count)
            for t in range(seq_count)
        ]
        return lax.ppermute(shard, ("section", "seq"), pairs)

    came = [linked(shard, 0, steps) for shard, steps in zip(sent[:-1], zip(*there))]
    came.append(sent[-1])
    def linked(shard, by, steps):
        pairs = [
            (
                s * seq_count + t,
                (s + by) % section_count * seq_count + (t ^ steps[s % 2]),
            )
            for s in range(section_count)
            for t in range(seq_count)
        ]
        return lax.ppermute(shard, ("section", "seq"), pairs)

    tails = jnp.stack([keys_new[0, rows - halo :], values_new[0, rows - halo :]])

    def halo_from(parity, after):
        mine = tails if after is None else pl.pallas_call(
            halo_kernel,
            out_shape=jax.ShapeDtypeStruct(tails.shape, bf16),
            in_specs=[whole_vmem, anywhere],
            out_specs=whole_vmem,
            compiler_params=params(queries),
            name="halo",
        )(tails, after)
        pairs = [
            (s * seq_count + t, s * seq_count + t + 1)
            for s in range(parity, section_count, 2)
            for t in range(seq_count - 1)
        ]
        return lax.ppermute(mine, ("section", "seq"), pairs)

    halos = [halo_from(1, None), halo_from(0, came[0])]
    picks = random_blocks[0].reshape(-1)

    def far_call(chosen):
        count = len(chosen)
        moved = any(steps[at] != others[at] for steps, others in zip(there, back) for at in chosen)
        return pl.pallas_call(
            functools.partial(far_kernel, there, back if moved else there, chosen),
            out_shape=[chunk_shape] * count,
            in_specs=[whole_smem] * 3 + [whole_vmem] * (2 + count),
            out_specs=[whole_vmem] * count,
            scratch_shapes=[pltpu.VMEM((count, rows, HD), bf16)],
            compiler_params=params(queries),
            cost_estimate=pl.CostEstimate(
                flops=40 * count * rows * 320 * HD * 4,
                bytes_accessed=2 * 2 * keys_cache.shape[1] * HD + 4 * count * rows * HD,
                transcendentals=count * rows * 320,
            ),
            name="far",
        )(
            window[0],
            global_blocks[0],
            picks,
            keys_cache[0],
            values_cache[0],
            *[came[at] for at in chosen],
        )

    late = list(range(seq_count - 1 - seq_count // 4, seq_count - 1))
    early = [at for at in range(seq_count) if at not in late]
    far = dict(zip(early, far_call(early)))
    if late:
        far.update(zip(late, far_call(late)))
    far = [far[at] for at in range(seq_count)]
    handed = [linked(shard, 1, steps) for shard, steps in zip(far[:-1], zip(*back))]

    def near_call(kernel, name, near_part, out_rows, vmem_count, scratch, *operands):
        return pl.pallas_call(
            functools.partial(kernel, there),
            out_shape=jax.ShapeDtypeStruct((out_rows, wide), bf16),
            in_specs=[
                whole_vmem if index < 3 + vmem_count else anywhere
                for index in range(3 + len(operands))
            ],
            out_specs=whole_vmem,
            scratch_shapes=scratch,
            compiler_params=params(queries),
            cost_estimate=pl.CostEstimate(
                flops=40 * heads * near_part * 256 * HD * 4,
                bytes_accessed=9 * near_part * wide,
                transcendentals=heads * near_part * 256,
            ),
            name=name,
        )(queries[0], keys_new[0], values_new[0], *operands)

    packed_rows = -(-(rows + STAT_ROWS) // (STAT_ROWS * heads)) * STAT_ROWS
    inner_part = near_call(
        near_inner_kernel, "near_inner", rows - halo, rows - halo + STAT_ROWS + packed_rows,
        1 + seq_count, [], far[-1], *came,
    )
    edge_part = near_call(
        near_edge_kernel, "near_edge", halo, halo + STAT_ROWS,
        2 + seq_count, [pltpu.VMEM(tails.shape, bf16)], *halos, *came, *handed[:2],
    )
    handed_inner = linked(inner_part, 1, [0, 0])
    handed_edge = linked(edge_part, 1, [0, 0])

    merged = pl.pallas_call(
        functools.partial(merge_kernel, back),
        out_shape=jax.ShapeDtypeStruct((rows, wide), bf16),
        in_specs=[whole_vmem] * (1 + seq_count),
        out_specs=whole_vmem,
        scratch_shapes=[pltpu.VMEM(chunk_shape.shape, bf16)],
        compiler_params=params(queries),
        cost_estimate=pl.CostEstimate(flops=0, bytes_accessed=6 * rows * wide, transcendentals=0),
        name="merge",
    )(handed_edge, handed_inner, *handed)
    return merged[None]


def solution(mesh):
    placed = (
        P("section", "seq", None),
        P("section", "seq", None),
        P("section", "seq", None),
        P("section", None, "seq"),
        P("section", None, "seq"),
        P("section", "seq"),
        P("section", None),
        P("section", None, None),
    )
    return jax.shard_map(
        per_device, mesh=mesh, in_specs=placed, out_specs=P("section", "seq", None), check_vma=False
    )
```

```python
import functools
import math

import jax
import jax.numpy as jnp
from jax import lax
from jax.experimental import pallas as pl
from jax.experimental.pallas import tpu as pltpu
from jax.sharding import PartitionSpec as P

HD = 128
BLK = 64
WMAX = 3
GLOB = 2
RAND = 3
LANES = 128
STAT_ROWS = 16
MASKED = -1e30
EXPO_SCALE = math.log2(math.e) / math.sqrt(HD)
VMEM_BASE = 12 * 1024 * 1024

whole_vmem = pl.BlockSpec(memory_space=pltpu.VMEM)
anywhere = pl.BlockSpec(memory_space=pl.ANY)
in_hbm = pl.BlockSpec(memory_space=pltpu.HBM)
whole_smem = pl.BlockSpec(memory_space=pltpu.SMEM)


def peers_of(there, by):
    count = lax.axis_size("section")
    other = lax.rem(lax.axis_index("section") + (by + count), count)
    odd = lax.rem(other, 2) == 1
    me = lax.axis_index("seq")
    return [
        jnp.bitwise_xor(me, jnp.where(odd, odd_step, even_step))
        for even_step, odd_step in zip(*there)
    ]


def scores_of(query, keys):
    return lax.dot_general(
        query, keys, (((1,), (1,)), ((), ())), preferred_element_type=jnp.float32
    )


def softmax_parts(scores, values):
    tops = [jnp.max(score, axis=1, keepdims=True) for score in scores]
    expos = [jnp.exp2((score - top) * EXPO_SCALE) for score, top in zip(scores, tops)]
    totals = [jnp.sum(expo, axis=1, keepdims=True) for expo in expos]
    mixed = [
        jnp.dot(expo.astype(jnp.bfloat16), value, preferred_element_type=jnp.float32)
        for expo, value in zip(expos, values)
    ]
    parts = [(mix * (1.0 / total)).astype(jnp.bfloat16) for mix, total in zip(mixed, totals)]
    lses = [top * EXPO_SCALE + jnp.log2(total) for top, total in zip(tops, totals)]
    return parts, lses


def as_row(column, offset):
    shape = (column.shape[0], LANES)
    row_at = lax.broadcasted_iota(jnp.int32, shape, 0)
    lane_at = lax.broadcasted_iota(jnp.int32, shape, 1)
    spread = jnp.where(lane_at == row_at + offset, column, 0.0)
    return jnp.sum(spread, axis=0, keepdims=True)


def stat_tile(rows):
    at = lax.broadcasted_iota(jnp.int32, (STAT_ROWS, LANES), 0)
    tile = jnp.zeros((STAT_ROWS, LANES), jnp.float32)
    count = len(rows)
    for index, row in enumerate(rows):
        high = row.astype(jnp.bfloat16).astype(jnp.float32)
        middle = (row - high).astype(jnp.bfloat16).astype(jnp.float32)
        low = row - high - middle
        for part, value in enumerate((high, middle, low)):
            tile = jnp.where(at == part * count + index, value, tile)
    return tile.astype(jnp.bfloat16)


def stat_rows_of(tile, count):
    wide = tile.astype(jnp.float32)
    return [
        wide[index : index + 1]
        + wide[count + index : count + index + 1]
        + wide[2 * count + index : 2 * count + index + 1]
        for index in range(count)
    ]


def stat_count(rows):
    return -(-rows // LANES)


def split_kernel(there, span_ref, query_ref, *refs):
    out_refs, arrived = refs[:-1], refs[-1]
    rows = query_ref.shape[0]
    copies = []
    for peer, out_ref in zip(peers_of(there, 0), out_refs):
        head = pl.multiple_of(peer * HD, HD)
        copies.append((query_ref.at[:, pl.ds(head, HD)], out_ref.at[:rows]))
    copies = [
        pltpu.make_async_copy(source, target, arrived.at[index])
        for index, (source, target) in enumerate(copies)
    ]
    for copy in copies:
        copy.start()
    width = jnp.full((STAT_ROWS, HD), span_ref[0].astype(jnp.float32)).astype(jnp.bfloat16)
    for out_ref in out_refs:
        out_ref[rows:, :] = width
    for copy in copies:
        copy.wait()


def halo_kernel(rows_ref, _, out_ref):
    out_ref[...] = rows_ref[...]


def far_kernel(
    there, chosen, span_ref, global_ref, random_ref, key_ref, value_ref, *refs
):
    span = span_ref[0]
    last = key_ref.shape[0] // BLK - 1

    def block(ref, at):
        if isinstance(at, int):
            return ref[at * BLK : (at + 1) * BLK, :]
        return ref[pl.ds(pl.multiple_of(at * BLK, BLK), BLK), :]

    glob_keys = [block(key_ref, global_ref[g]) for g in range(GLOB)]
    glob_values = [block(value_ref, global_ref[g]) for g in range(GLOB)]
    peers = [peers_of(there, 0)[at] for at in chosen]
    query_refs, out_refs = refs[: len(peers)], refs[len(peers) :]
    rows = query_refs[0].shape[0] - STAT_ROWS
    for chunk, query_ref, out_ref in zip(peers, query_refs, out_refs):
        blocks = rows // BLK
        first = chunk == 0
        all_scores, all_picks = [], []
        for b in range(blocks):
            query = query_ref[b * BLK : (b + 1) * BLK, :]
            base = (chunk * blocks + b) * RAND
            picks = [random_ref[base + r] for r in range(RAND)]
            keys = glob_keys + [block(key_ref, pick) for pick in picks]
            known = len(keys) * BLK
            spare = [last + 1 + b - w for w in range(b + 1, WMAX)]
            keys = keys + [block(key_ref, at) for at in spare]
            scores = scores_of(query, jnp.concatenate(keys, axis=0))
            if spare:
                open_slots = jnp.where(first, jnp.clip(span - (b + 1), 0, len(spare)), 0)
                lane_at = lax.broadcasted_iota(jnp.int32, scores.shape, 1)
                scores = jnp.where(lane_at < known + open_slots * BLK, scores, MASKED)
            all_scores.append(scores)
            all_picks.append(picks + spare)
        all_values = [
            jnp.concatenate(glob_values + [block(value_ref, at) for at in picks], axis=0)
            for picks in all_picks
        ]
        parts, lses = softmax_parts(all_scores, all_values)
        stats = []
        for b in range(blocks):
            row = as_row(lses[b], (b * BLK) % LANES)
            if (b * BLK) % LANES:
                stats[-1] = stats[-1] + row
            else:
                stats.append(row)
        tile = stat_tile(stats)
        for b in range(blocks):
            out_ref[b * BLK : (b + 1) * BLK, :] = parts[b]
        out_ref[rows:, :] = tile


def near_rows(
    there, first, last, query_ref, key_ref, value_ref, halo_ref, came_refs, out_ref
):
    rows = query_ref.shape[0]
    halo = (WMAX - 1) * BLK
    starts = list(range(first, last, 2 * BLK))
    sizes = [min(2 * BLK, last - start) for start in starts]
    leads = [
        halo if start < halo else min(-(-(size + halo) // LANES) * LANES - size, start)
        for start, size in zip(starts, sizes)
    ]
    peers = peers_of(there, 0)
    together = min(len(starts), 2)
    for begin in range(0, len(peers), together):
        pair = range(begin, min(begin + together, len(peers)))
        all_lanes = [pl.ds(pl.multiple_of(peers[at] * HD, HD), HD) for at in pair]
        all_scores, all_values = [], []
        for at, lanes in zip(pair, all_lanes):
            width = came_refs[at][rows:, :].astype(jnp.float32)[:1]
            width = jnp.concatenate([width] * ((2 * BLK + halo) // LANES), axis=1)
            for start, size, lead in zip(starts, sizes, leads):
                query = query_ref[start : start + size, lanes]
                if start < lead:
                    keys = [halo_ref[0, start:, lanes], key_ref[: start + size, lanes]]
                    values = [halo_ref[1, start:, lanes], value_ref[: start + size, lanes]]
                    keys, values = jnp.concatenate(keys, axis=0), jnp.concatenate(values, axis=0)
                else:
                    keys = key_ref[start - lead : start + size, lanes]
                    values = value_ref[start - lead : start + size, lanes]
                scores = scores_of(query, keys)
                row_at = lax.broadcasted_iota(jnp.int32, scores.shape, 0)
                lane_at = lax.broadcasted_iota(jnp.int32, scores.shape, 1)
                slot = (lane_at // BLK - row_at // BLK - lead // BLK).astype(jnp.float32)
                allowed = (lane_at <= row_at + lead) & (slot + width[:, : size + lead] >= 1.0)
                if start < lead:
                    closed = jnp.where(lax.axis_index("seq") == 0, lead - start, 0)
                    allowed = allowed & (lane_at >= closed)
                all_scores.append(jnp.where(allowed, scores, MASKED))
                all_values.append(values)
        parts, lses = softmax_parts(all_scores, all_values)
        for index, lanes in enumerate(all_lanes):
            own = slice(index * len(starts), (index + 1) * len(starts))
            tile = stat_tile([as_row(lse, 0) for lse in lses[own]])
            for start, size, part in zip(starts, sizes, parts[own]):
                out_ref[start - first : start - first + size, lanes] = part
            out_ref[last - first : last - first + STAT_ROWS, lanes] = tile


def packed_at(index, first, wide):
    across = wide // HD
    row, lane = first + index // across * STAT_ROWS, index % across * HD
    return slice(row, row + STAT_ROWS), slice(lane, lane + HD)


def near_inner_kernel(there, query_ref, key_ref, value_ref, own_ref, *refs):
    rows, wide = query_ref.shape
    halo = (WMAX - 1) * BLK
    came_refs, out_ref = refs[:-1], refs[-1]
    near_rows(there, halo, rows, query_ref, key_ref, value_ref, None, came_refs, out_ref)
    for index in range(own_ref.shape[0] // STAT_ROWS):
        at = packed_at(index, rows - halo + STAT_ROWS, wide)
        out_ref[at] = own_ref[index * STAT_ROWS : (index + 1) * STAT_ROWS, :]


def near_edge_kernel(there, query_ref, key_ref, value_ref, odd_ref, even_ref, *refs):
    halo = (WMAX - 1) * BLK
    came_refs, out_ref, halo_ref = refs[: len(there[0])], refs[-2], refs[-1]
    halo_ref[...] = odd_ref[...] + even_ref[...]
    near_rows(there, 0, halo, query_ref, key_ref, value_ref, halo_ref, came_refs, out_ref)


def merge_kernel(there, edge_ref, inner_ref, *refs):
    far_refs, out_ref, own_ref = refs[:-2], refs[-2], refs[-1]
    rows, wide = out_ref.shape
    halo = (WMAX - 1) * BLK
    for index in range(own_ref.shape[0] // STAT_ROWS):
        at = packed_at(index, rows - halo + STAT_ROWS, wide)
        own_ref[index * STAT_ROWS : (index + 1) * STAT_ROWS, :] = inner_ref[at]
    count = stat_count(rows)
    for peer, far_ref in zip(peers_of(there, -1), (*far_refs, own_ref)):
        lanes = pl.ds(pl.multiple_of(peer * HD, HD), HD)
        far_stats = stat_rows_of(far_ref[rows:, :], count)
        near_stats = stat_rows_of(edge_ref[halo:, lanes], 1) + stat_rows_of(
            inner_ref[rows - halo : rows - halo + STAT_ROWS, lanes], count - 1
        )
        for group in range(count):
            start = group * LANES
            size = min(LANES, rows - start)
            share = 1.0 / (1.0 + jnp.exp2(near_stats[group] - far_stats[group]))
            row_at = lax.broadcasted_iota(jnp.int32, (size, LANES), 0)
            lane_at = lax.broadcasted_iota(jnp.int32, (size, LANES), 1)
            column = jnp.sum(
                jnp.where(row_at == lane_at, share, 0.0), axis=1, keepdims=True
            )
            far = far_ref[start : start + size, :].astype(jnp.float32)
            if start < halo:
                near = edge_ref[start : start + size, lanes].astype(jnp.float32)
            else:
                near = inner_ref[start - halo : start - halo + size, lanes].astype(jnp.float32)
            out_ref[start : start + size, lanes] = (
                far * column + near * (1.0 - column)
            ).astype(jnp.bfloat16)


def params(shard):
    return pltpu.CompilerParams(vmem_limit_bytes=VMEM_BASE + 14 * 2 * math.prod(shard.shape))


def per_device(
    queries, keys_new, values_new, keys_cache, values_cache, window, global_blocks, random_blocks
):
    section_count = lax.axis_size("section")
    seq_count = lax.axis_size("seq")
    rows, wide = queries.shape[1], queries.shape[2]
    halo = (WMAX - 1) * BLK
    heads = wide // HD
    bf16 = jnp.bfloat16
    half = max(seq_count // 2, 1)
    inner, outer = list(range(1, half)), list(range(seq_count - 1, half - 1, -1))
    there = [outer + inner + [0], inner + outer + [0]]

    chunk_shape = jax.ShapeDtypeStruct((rows + STAT_ROWS, HD), bf16)
    chunk_shape = jax.ShapeDtypeStruct((rows + STAT_ROWS, HD), bf16)
    sent = pl.pallas_call(
        functools.partial(split_kernel, there),
        out_shape=[chunk_shape] * seq_count,
        in_specs=[whole_smem, in_hbm],
        out_specs=[whole_vmem] * seq_count,
        scratch_shapes=[pltpu.SemaphoreType.DMA((seq_count,))],
        compiler_params=params(queries),
        cost_estimate=pl.CostEstimate(flops=0, bytes_accessed=5 * rows * wide, transcendentals=0),
        name="split",
    )(window[0], queries[0])

    def linked(shard, by, steps):
        pairs = [
            (
                s * seq_count + t,
                (s + by) % section_count * seq_count + (t ^ steps[s % 2]),
            )
            for s in range(section_count)
            for t in range(seq_count)
        ]
        return lax.ppermute(shard, ("section", "seq"), pairs)

    came = [linked(shard, 0, steps) for shard, steps in zip(sent[:-1], zip(*there))]
    came.append(sent[-1])
    tails = jnp.stack([keys_new[0, rows - halo :], values_new[0, rows - halo :]])

    def halo_from(parity, after):
        mine = tails if after is None else pl.pallas_call(
            halo_kernel,
            out_shape=jax.ShapeDtypeStruct(tails.shape, bf16),
            in_specs=[whole_vmem, anywhere],
            out_specs=whole_vmem,
            compiler_params=params(queries),
            name="halo",
        )(tails, after)
        pairs = [
            (s * seq_count + t, s * seq_count + t + 1)
            for s in range(parity, section_count, 2)
            for t in range(seq_count - 1)
        ]
        return lax.ppermute(mine, ("section", "seq"), pairs)

    halos = [halo_from(1, None), halo_from(0, came[0])]
    picks = random_blocks[0].reshape(-1)

    def far_call(chosen):
        count = len(chosen)
        return pl.pallas_call(
            functools.partial(far_kernel, there, chosen),
            out_shape=[chunk_shape] * count,
            in_specs=[whole_smem] * 3 + [whole_vmem] * (2 + count),
            out_specs=[whole_vmem] * count,
            compiler_params=params(queries),
            cost_estimate=pl.CostEstimate(
                flops=40 * count * rows * 320 * HD * 4,
                bytes_accessed=2 * 2 * keys_cache.shape[1] * HD + 4 * count * rows * HD,
                transcendentals=count * rows * 320,
            ),
            name="far",
        )(
            window[0],
            global_blocks[0],
            picks,
            keys_cache[0],
            values_cache[0],
            *[came[at] for at in chosen],
        )

    late = list(range(seq_count - 1 - seq_count // 4, seq_count - 1))
    early = [at for at in range(seq_count) if at not in late]
    far = dict(zip(early, far_call(early)))
    if late:
        far.update(zip(late, far_call(late)))
    far = [far[at] for at in range(seq_count)]
    handed = [linked(shard, 1, steps) for shard, steps in zip(far[:-1], zip(*there))]

    def near_call(kernel, name, near_part, out_rows, vmem_count, scratch, *operands):
        return pl.pallas_call(
            functools.partial(kernel, there),
            out_shape=jax.ShapeDtypeStruct((out_rows, wide), bf16),
            in_specs=[
                whole_vmem if index < 3 + vmem_count else anywhere
                for index in range(3 + len(operands))
            ],
            out_specs=whole_vmem,
            scratch_shapes=scratch,
            compiler_params=params(queries),
            cost_estimate=pl.CostEstimate(
                flops=40 * heads * near_part * 256 * HD * 4,
                bytes_accessed=9 * near_part * wide,
                transcendentals=heads * near_part * 256,
            ),
            name=name,
        )(queries[0], keys_new[0], values_new[0], *operands)

    packed_rows = -(-(rows + STAT_ROWS) // (STAT_ROWS * heads)) * STAT_ROWS
    inner_part = near_call(
        near_inner_kernel, "near_inner", rows - halo, rows - halo + STAT_ROWS + packed_rows,
        1 + seq_count, [], far[-1], *came,
    )
    edge_part = near_call(
        near_edge_kernel, "near_edge", halo, halo + STAT_ROWS,
        2 + seq_count, [pltpu.VMEM(tails.shape, bf16)], *halos, *came, *handed[:1],
    )
    handed_inner = linked(inner_part, 1, [0, 0])
    handed_edge = linked(edge_part, 1, [0, 0])

    merged = pl.pallas_call(
        functools.partial(merge_kernel, there),
        out_shape=jax.ShapeDtypeStruct((rows, wide), bf16),
        in_specs=[whole_vmem] * (1 + seq_count),
        out_specs=whole_vmem,
        scratch_shapes=[pltpu.VMEM(chunk_shape.shape, bf16)],
        compiler_params=params(queries),
        cost_estimate=pl.CostEstimate(flops=0, bytes_accessed=6 * rows * wide, transcendentals=0),
        name="merge",
    )(handed_edge, handed_inner, *handed)
    return merged[None]


def solution(mesh):
    placed = (
        P("section", "seq", None),
        P("section", "seq", None),
        P("section", "seq", None),
        P("section", None, "seq"),
        P("section", None, "seq"),
        P("section", "seq"),
        P("section", None),
        P("section", None, None),
    )
    return jax.shard_map(
        per_device, mesh=mesh, in_specs=placed, out_specs=P("section", "seq", None), check_vma=False
    )
```

```python
import functools
import math

import jax
import jax.numpy as jnp
from jax import lax
from jax.experimental import pallas as pl
from jax.experimental.pallas import tpu as pltpu
from jax.sharding import PartitionSpec as P

HD = 128
BLK = 64
WMAX = 3
GLOB = 2
RAND = 3
LANES = 128
STAT_ROWS = 16
MASKED = -1e30
EXPO_SCALE = math.log2(math.e) / math.sqrt(HD)
VMEM_BASE = 12 * 1024 * 1024

whole_vmem = pl.BlockSpec(memory_space=pltpu.VMEM)
anywhere = pl.BlockSpec(memory_space=pl.ANY)
in_hbm = pl.BlockSpec(memory_space=pltpu.HBM)
whole_smem = pl.BlockSpec(memory_space=pltpu.SMEM)


def peers_of(there, by):
    count = lax.axis_size("section")
    other = lax.rem(lax.axis_index("section") + (by + count), count)
    odd = lax.rem(other, 2) == 1
    me = lax.axis_index("seq")
    return [
        jnp.bitwise_xor(me, jnp.where(odd, odd_step, even_step))
        for even_step, odd_step in zip(*there)
    ]


def scores_of(query, keys):
    return lax.dot_general(
        query, keys, (((1,), (1,)), ((), ())), preferred_element_type=jnp.float32
    )


def softmax_parts(scores, values):
    tops = [jnp.max(score, axis=1, keepdims=True) for score in scores]
    expos = [jnp.exp2((score - top) * EXPO_SCALE) for score, top in zip(scores, tops)]
    totals = [jnp.sum(expo, axis=1, keepdims=True) for expo in expos]
    mixed = [
        jnp.dot(expo.astype(jnp.bfloat16), value, preferred_element_type=jnp.float32)
        for expo, value in zip(expos, values)
    ]
    parts = [(mix * (1.0 / total)).astype(jnp.bfloat16) for mix, total in zip(mixed, totals)]
    lses = [top * EXPO_SCALE + jnp.log2(total) for top, total in zip(tops, totals)]
    return parts, lses


def as_row(column, offset):
    shape = (column.shape[0], LANES)
    row_at = lax.broadcasted_iota(jnp.int32, shape, 0)
    lane_at = lax.broadcasted_iota(jnp.int32, shape, 1)
    spread = jnp.where(lane_at == row_at + offset, column, 0.0)
    return jnp.sum(spread, axis=0, keepdims=True)


def stat_tile(rows):
    at = lax.broadcasted_iota(jnp.int32, (STAT_ROWS, LANES), 0)
    tile = jnp.zeros((STAT_ROWS, LANES), jnp.float32)
    count = len(rows)
    for index, row in enumerate(rows):
        high = row.astype(jnp.bfloat16).astype(jnp.float32)
        middle = (row - high).astype(jnp.bfloat16).astype(jnp.float32)
        low = row - high - middle
        for part, value in enumerate((high, middle, low)):
            tile = jnp.where(at == part * count + index, value, tile)
    return tile.astype(jnp.bfloat16)


def stat_rows_of(tile, count):
    wide = tile.astype(jnp.float32)
    return [
        wide[index : index + 1]
        + wide[count + index : count + index + 1]
        + wide[2 * count + index : 2 * count + index + 1]
        for index in range(count)
    ]


def stat_count(rows):
    return -(-rows // LANES)


def split_kernel(there, span_ref, query_ref, *refs):
    out_refs, arrived = refs[:-1], refs[-1]
    rows = query_ref.shape[0]
    copies = []
    for peer, out_ref in zip(peers_of(there, 0), out_refs):
        head = pl.multiple_of(peer * HD, HD)
        copies.append((query_ref.at[:, pl.ds(head, HD)], out_ref.at[:rows]))
    copies = [
        pltpu.make_async_copy(source, target, arrived.at[index])
        for index, (source, target) in enumerate(copies)
    ]
    for copy in copies:
        copy.start()
    width = jnp.full((STAT_ROWS, HD), span_ref[0].astype(jnp.float32)).astype(jnp.bfloat16)
    for out_ref in out_refs:
        out_ref[rows:, :] = width
    for copy in copies:
        copy.wait()


def halo_kernel(rows_ref, _, out_ref):
    out_ref[...] = rows_ref[...]


def far_kernel(
    there, chosen, span_ref, global_ref, random_ref, key_ref, value_ref, *refs
):
    span = span_ref[0]
    last = key_ref.shape[0] // BLK - 1

    def block(ref, at):
        if isinstance(at, int):
            return ref[at * BLK : (at + 1) * BLK, :]
        return ref[pl.ds(pl.multiple_of(at * BLK, BLK), BLK), :]

    glob_keys = [block(key_ref, global_ref[g]) for g in range(GLOB)]
    glob_values = [block(value_ref, global_ref[g]) for g in range(GLOB)]
    peers = [peers_of(there, 0)[at] for at in chosen]
    query_refs, out_refs = refs[: len(peers)], refs[len(peers) :]
    rows = query_refs[0].shape[0] - STAT_ROWS
    for chunk, query_ref, out_ref in zip(peers, query_refs, out_refs):
        blocks = rows // BLK
        first = chunk == 0
        all_scores, all_picks = [], []
        for b in range(blocks):
            query = query_ref[b * BLK : (b + 1) * BLK, :]
            base = (chunk * blocks + b) * RAND
            picks = [random_ref[base + r] for r in range(RAND)]
            keys = glob_keys + [block(key_ref, pick) for pick in picks]
            known = len(keys) * BLK
            spare = [last + 1 + b - w for w in range(b + 1, WMAX)]
            keys = keys + [block(key_ref, at) for at in spare]
            scores = scores_of(query, jnp.concatenate(keys, axis=0))
            if spare:
                open_slots = jnp.where(first, jnp.clip(span - (b + 1), 0, len(spare)), 0)
                lane_at = lax.broadcasted_iota(jnp.int32, scores.shape, 1)
                scores = jnp.where(lane_at < known + open_slots * BLK, scores, MASKED)
            all_scores.append(scores)
            all_picks.append(picks + spare)
        all_values = [
            jnp.concatenate(glob_values + [block(value_ref, at) for at in picks], axis=0)
            for picks in all_picks
        ]
        parts, lses = softmax_parts(all_scores, all_values)
        stats = []
        for b in range(blocks):
            row = as_row(lses[b], (b * BLK) % LANES)
            if (b * BLK) % LANES:
                stats[-1] = stats[-1] + row
            else:
                stats.append(row)
        tile = stat_tile(stats)
        for b in range(blocks):
            out_ref[b * BLK : (b + 1) * BLK, :] = parts[b]
        out_ref[rows:, :] = tile


def near_rows(
    there, first, last, query_ref, key_ref, value_ref, halo_ref, came_refs, out_ref
):
    rows = query_ref.shape[0]
    halo = (WMAX - 1) * BLK
    starts = list(range(first, last, 2 * BLK))
    sizes = [min(2 * BLK, last - start) for start in starts]
    leads = [
        halo if start < halo else min(-(-(size + halo) // LANES) * LANES - size, start)
        for start, size in zip(starts, sizes)
    ]
    peers = peers_of(there, 0)
    together = min(len(starts), 2)
    for begin in range(0, len(peers), together):
        pair = range(begin, min(begin + together, len(peers)))
        all_lanes = [pl.ds(pl.multiple_of(peers[at] * HD, HD), HD) for at in pair]
        all_scores, all_values = [], []
        for at, lanes in zip(pair, all_lanes):
            width = came_refs[at][rows:, :].astype(jnp.float32)[:1]
            width = jnp.concatenate([width] * ((2 * BLK + halo) // LANES), axis=1)
            for start, size, lead in zip(starts, sizes, leads):
                query = query_ref[start : start + size, lanes]
                if start < lead:
                    keys = [halo_ref[0, start:, lanes], key_ref[: start + size, lanes]]
                    values = [halo_ref[1, start:, lanes], value_ref[: start + size, lanes]]
                    keys, values = jnp.concatenate(keys, axis=0), jnp.concatenate(values, axis=0)
                else:
                    keys = key_ref[start - lead : start + size, lanes]
                    values = value_ref[start - lead : start + size, lanes]
                scores = scores_of(query, keys)
                row_at = lax.broadcasted_iota(jnp.int32, scores.shape, 0)
                lane_at = lax.broadcasted_iota(jnp.int32, scores.shape, 1)
                slot = (lane_at // BLK - row_at // BLK - lead // BLK).astype(jnp.float32)
                allowed = (lane_at <= row_at + lead) & (slot + width[:, : size + lead] >= 1.0)
                if start < lead:
                    closed = jnp.where(lax.axis_index("seq") == 0, lead - start, 0)
                    allowed = allowed & (lane_at >= closed)
                all_scores.append(jnp.where(allowed, scores, MASKED))
                all_values.append(values)
        parts, lses = softmax_parts(all_scores, all_values)
        for index, lanes in enumerate(all_lanes):
            own = slice(index * len(starts), (index + 1) * len(starts))
            tile = stat_tile([as_row(lse, 0) for lse in lses[own]])
            for start, size, part in zip(starts, sizes, parts[own]):
                out_ref[start - first : start - first + size, lanes] = part
            out_ref[last - first : last - first + STAT_ROWS, lanes] = tile


def packed_at(index, first, wide):
    across = wide // HD
    row, lane = first + index // across * STAT_ROWS, index % across * HD
    return slice(row, row + STAT_ROWS), slice(lane, lane + HD)


def near_inner_kernel(there, query_ref, key_ref, value_ref, own_ref, *refs):
    rows, wide = query_ref.shape
    halo = (WMAX - 1) * BLK
    came_refs, out_ref = refs[:-1], refs[-1]
    near_rows(there, halo, rows, query_ref, key_ref, value_ref, None, came_refs, out_ref)
    for index in range(own_ref.shape[0] // STAT_ROWS):
        at = packed_at(index, rows - halo + STAT_ROWS, wide)
        out_ref[at] = own_ref[index * STAT_ROWS : (index + 1) * STAT_ROWS, :]


def near_edge_kernel(there, query_ref, key_ref, value_ref, odd_ref, even_ref, *refs):
    halo = (WMAX - 1) * BLK
    came_refs, out_ref, halo_ref = refs[: len(there[0])], refs[-2], refs[-1]
    halo_ref[...] = odd_ref[...] + even_ref[...]
    near_rows(there, 0, halo, query_ref, key_ref, value_ref, halo_ref, came_refs, out_ref)


def merge_kernel(there, edge_ref, inner_ref, *refs):
    far_refs, out_ref, own_ref = refs[:-2], refs[-2], refs[-1]
    rows, wide = out_ref.shape
    halo = (WMAX - 1) * BLK
    for index in range(own_ref.shape[0] // STAT_ROWS):
        at = packed_at(index, rows - halo + STAT_ROWS, wide)
        own_ref[index * STAT_ROWS : (index + 1) * STAT_ROWS, :] = inner_ref[at]
    count = stat_count(rows)
    for peer, far_ref in zip(peers_of(there, -1), (*far_refs, own_ref)):
        lanes = pl.ds(pl.multiple_of(peer * HD, HD), HD)
        far_stats = stat_rows_of(far_ref[rows:, :], count)
        near_stats = stat_rows_of(edge_ref[halo:, lanes], 1) + stat_rows_of(
            inner_ref[rows - halo : rows - halo + STAT_ROWS, lanes], count - 1
        )
        for group in range(count):
            start = group * LANES
            size = min(LANES, rows - start)
            share = 1.0 / (1.0 + jnp.exp2(near_stats[group] - far_stats[group]))
            row_at = lax.broadcasted_iota(jnp.int32, (size, LANES), 0)
            lane_at = lax.broadcasted_iota(jnp.int32, (size, LANES), 1)
            column = jnp.sum(
                jnp.where(row_at == lane_at, share, 0.0), axis=1, keepdims=True
            )
            far = far_ref[start : start + size, :].astype(jnp.float32)
            if start < halo:
                near = edge_ref[start : start + size, lanes].astype(jnp.float32)
            else:
                near = inner_ref[start - halo : start - halo + size, lanes].astype(jnp.float32)
            out_ref[start : start + size, lanes] = (
                far * column + near * (1.0 - column)
            ).astype(jnp.bfloat16)


def params(shard):
    return pltpu.CompilerParams(vmem_limit_bytes=VMEM_BASE + 14 * 2 * math.prod(shard.shape))


def per_device(
    queries, keys_new, values_new, keys_cache, values_cache, window, global_blocks, random_blocks
):
    section_count = lax.axis_size("section")
    seq_count = lax.axis_size("seq")
    rows, wide = queries.shape[1], queries.shape[2]
    halo = (WMAX - 1) * BLK
    heads = wide // HD
    bf16 = jnp.bfloat16
    half = max(seq_count // 2, 1)
    inner, outer = list(range(1, half)), list(range(seq_count - 1, half - 1, -1))
    there = [outer + inner + [0], inner + outer + [0]]

    chunk_shape = jax.ShapeDtypeStruct((rows + STAT_ROWS, HD), bf16)
    chunk_shape = jax.ShapeDtypeStruct((rows + STAT_ROWS, HD), bf16)
    sent = pl.pallas_call(
        functools.partial(split_kernel, there),
        out_shape=[chunk_shape] * seq_count,
        in_specs=[whole_smem, in_hbm],
        out_specs=[whole_vmem] * seq_count,
        scratch_shapes=[pltpu.SemaphoreType.DMA((seq_count,))],
        compiler_params=params(queries),
        cost_estimate=pl.CostEstimate(flops=0, bytes_accessed=5 * rows * wide, transcendentals=0),
        name="split",
    )(window[0], queries[0])

    def linked(shard, by, steps):
        pairs = [
            (
                s * seq_count + t,
                (s + by) % section_count * seq_count + (t ^ steps[s % 2]),
            )
            for s in range(section_count)
            for t in range(seq_count)
        ]
        return lax.ppermute(shard, ("section", "seq"), pairs)

    came = [linked(shard, 0, steps) for shard, steps in zip(sent[:-1], zip(*there))]
    came.append(sent[-1])
    tails = jnp.stack([keys_new[0, rows - halo :], values_new[0, rows - halo :]])

    def halo_from(parity, after):
        mine = tails if after is None else pl.pallas_call(
            halo_kernel,
            out_shape=jax.ShapeDtypeStruct(tails.shape, bf16),
            in_specs=[whole_vmem, anywhere],
            out_specs=whole_vmem,
            compiler_params=params(queries),
            name="halo",
        )(tails, after)
        pairs = [
            (s * seq_count + t, s * seq_count + t + 1)
            for s in range(parity, section_count, 2)
            for t in range(seq_count - 1)
        ]
        return lax.ppermute(mine, ("section", "seq"), pairs)

    halos = [halo_from(1, None), halo_from(0, came[0])]
    picks = random_blocks[0].reshape(-1)

    def far_call(chosen):
        count = len(chosen)
        return pl.pallas_call(
            functools.partial(far_kernel, there, chosen),
            out_shape=[chunk_shape] * count,
            in_specs=[whole_smem] * 3 + [whole_vmem] * (2 + count),
            out_specs=[whole_vmem] * count,
            compiler_params=params(queries),
            cost_estimate=pl.CostEstimate(
                flops=40 * count * rows * 320 * HD * 4,
                bytes_accessed=2 * 2 * keys_cache.shape[1] * HD + 4 * count * rows * HD,
                transcendentals=count * rows * 320,
            ),
            name="far",
        )(
            window[0],
            global_blocks[0],
            picks,
            keys_cache[0],
            values_cache[0],
            *[came[at] for at in chosen],
        )

    late = list(range(seq_count - 1 - seq_count // 4, seq_count - 1))
    early = [at for at in range(seq_count) if at not in late]
    far = dict(zip(early, far_call(early)))
    if late:
        far.update(zip(late, far_call(late)))
    far = [far[at] for at in range(seq_count)]
    handed = [linked(shard, 1, steps) for shard, steps in zip(far[:-1], zip(*there))]

    def near_call(kernel, name, near_part, out_rows, vmem_count, scratch, *operands):
        return pl.pallas_call(
            functools.partial(kernel, there),
            out_shape=jax.ShapeDtypeStruct((out_rows, wide), bf16),
            in_specs=[
                whole_vmem if index < 3 + vmem_count else anywhere
                for index in range(3 + len(operands))
            ],
            out_specs=whole_vmem,
            scratch_shapes=scratch,
            compiler_params=params(queries),
            cost_estimate=pl.CostEstimate(
                flops=40 * heads * near_part * 256 * HD * 4,
                bytes_accessed=9 * near_part * wide,
                transcendentals=heads * near_part * 256,
            ),
            name=name,
        )(queries[0], keys_new[0], values_new[0], *operands)

    packed_rows = -(-(rows + STAT_ROWS) // (STAT_ROWS * heads)) * STAT_ROWS
    inner_part = near_call(
        near_inner_kernel, "near_inner", rows - halo, rows - halo + STAT_ROWS + packed_rows,
        1 + seq_count, [], far[-1], *came,
    )
    edge_part = near_call(
        near_edge_kernel, "near_edge", halo, halo + STAT_ROWS,
        2 + seq_count, [pltpu.VMEM(tails.shape, bf16)], *halos, *came, *handed[:2],
    )
    handed_inner = linked(inner_part, 1, [0, 0])
    handed_edge = linked(edge_part, 1, [0, 0])

    merged = pl.pallas_call(
        functools.partial(merge_kernel, there),
        out_shape=jax.ShapeDtypeStruct((rows, wide), bf16),
        in_specs=[whole_vmem] * (1 + seq_count),
        out_specs=whole_vmem,
        scratch_shapes=[pltpu.VMEM(chunk_shape.shape, bf16)],
        compiler_params=params(queries),
        cost_estimate=pl.CostEstimate(flops=0, bytes_accessed=6 * rows * wide, transcendentals=0),
        name="merge",
    )(handed_edge, handed_inner, *handed)
    return merged[None]


def solution(mesh):
    placed = (
        P("section", "seq", None),
        P("section", "seq", None),
        P("section", "seq", None),
        P("section", None, "seq"),
        P("section", None, "seq"),
        P("section", "seq"),
        P("section", None),
        P("section", None, None),
    )
    return jax.shard_map(
        per_device, mesh=mesh, in_specs=placed, out_specs=P("section", "seq", None), check_vma=False
    )
```

```python
import functools
import math

import jax
import jax.numpy as jnp
from jax import lax
from jax.experimental import pallas as pl
from jax.experimental.pallas import tpu as pltpu
from jax.sharding import PartitionSpec as P

HD = 128
BLK = 64
WMAX = 3
GLOB = 2
RAND = 3
LANES = 128
STAT_ROWS = 16
MASKED = -1e30
EXPO_SCALE = math.log2(math.e) / math.sqrt(HD)
VMEM_BASE = 12 * 1024 * 1024

whole_vmem = pl.BlockSpec(memory_space=pltpu.VMEM)
anywhere = pl.BlockSpec(memory_space=pl.ANY)
in_hbm = pl.BlockSpec(memory_space=pltpu.HBM)
whole_smem = pl.BlockSpec(memory_space=pltpu.SMEM)


def peers_of(there, by):
    count = lax.axis_size("section")
    other = lax.rem(lax.axis_index("section") + (by + count), count)
    odd = lax.rem(other, 2) == 1
    me = lax.axis_index("seq")
    return [
        jnp.bitwise_xor(me, jnp.where(odd, odd_step, even_step))
        for even_step, odd_step in zip(*there)
    ]


def scores_of(query, keys):
    return lax.dot_general(
        query, keys, (((1,), (1,)), ((), ())), preferred_element_type=jnp.float32
    )


def softmax_parts(scores, values):
    tops = [jnp.max(score, axis=1, keepdims=True) for score in scores]
    expos = [jnp.exp2((score - top) * EXPO_SCALE) for score, top in zip(scores, tops)]
    totals = [jnp.sum(expo, axis=1, keepdims=True) for expo in expos]
    mixed = [
        jnp.dot(expo.astype(jnp.bfloat16), value, preferred_element_type=jnp.float32)
        for expo, value in zip(expos, values)
    ]
    parts = [(mix * (1.0 / total)).astype(jnp.bfloat16) for mix, total in zip(mixed, totals)]
    lses = [top * EXPO_SCALE + jnp.log2(total) for top, total in zip(tops, totals)]
    return parts, lses


def as_row(column, offset):
    shape = (column.shape[0], LANES)
    row_at = lax.broadcasted_iota(jnp.int32, shape, 0)
    lane_at = lax.broadcasted_iota(jnp.int32, shape, 1)
    spread = jnp.where(lane_at == row_at + offset, column, 0.0)
    return jnp.sum(spread, axis=0, keepdims=True)


def stat_tile(rows):
    at = lax.broadcasted_iota(jnp.int32, (STAT_ROWS, LANES), 0)
    tile = jnp.zeros((STAT_ROWS, LANES), jnp.float32)
    count = len(rows)
    for index, row in enumerate(rows):
        high = row.astype(jnp.bfloat16).astype(jnp.float32)
        middle = (row - high).astype(jnp.bfloat16).astype(jnp.float32)
        low = row - high - middle
        for part, value in enumerate((high, middle, low)):
            tile = jnp.where(at == part * count + index, value, tile)
    return tile.astype(jnp.bfloat16)


def stat_rows_of(tile, count):
    wide = tile.astype(jnp.float32)
    return [
        wide[index : index + 1]
        + wide[count + index : count + index + 1]
        + wide[2 * count + index : 2 * count + index + 1]
        for index in range(count)
    ]


def stat_count(rows):
    return -(-rows // LANES)


def split_kernel(there, span_ref, query_ref, *refs):
    out_refs, arrived = refs[:-1], refs[-1]
    rows = query_ref.shape[0]
    copies = []
    for peer, out_ref in zip(peers_of(there, 0), out_refs):
        head = pl.multiple_of(peer * HD, HD)
        copies.append((query_ref.at[:, pl.ds(head, HD)], out_ref.at[:rows]))
    copies = [
        pltpu.make_async_copy(source, target, arrived.at[index])
        for index, (source, target) in enumerate(copies)
    ]
    for copy in copies:
        copy.start()
    width = jnp.full((STAT_ROWS, HD), span_ref[0].astype(jnp.float32)).astype(jnp.bfloat16)
    for out_ref in out_refs:
        out_ref[rows:, :] = width
    for copy in copies:
        copy.wait()


def halo_kernel(rows_ref, _, out_ref):
    out_ref[...] = rows_ref[...]


def far_kernel(
    there, chosen, span_ref, global_ref, random_ref, key_ref, value_ref, *refs
):
    span = span_ref[0]
    last = key_ref.shape[0] // BLK - 1

    def block(ref, at):
        if isinstance(at, int):
            return ref[at * BLK : (at + 1) * BLK, :]
        return ref[pl.ds(pl.multiple_of(at * BLK, BLK), BLK), :]

    glob_keys = [block(key_ref, global_ref[g]) for g in range(GLOB)]
    glob_values = [block(value_ref, global_ref[g]) for g in range(GLOB)]
    peers = [peers_of(there, 0)[at] for at in chosen]
    query_refs, out_refs = refs[: len(peers)], refs[len(peers) :]
    rows = query_refs[0].shape[0] - STAT_ROWS
    for chunk, query_ref, out_ref in zip(peers, query_refs, out_refs):
        blocks = rows // BLK
        first = chunk == 0
        all_scores, all_picks = [], []
        for b in range(blocks):
            query = query_ref[b * BLK : (b + 1) * BLK, :]
            base = (chunk * blocks + b) * RAND
            picks = [random_ref[base + r] for r in range(RAND)]
            keys = glob_keys + [block(key_ref, pick) for pick in picks]
            known = len(keys) * BLK
            spare = [last + 1 + b - w for w in range(b + 1, WMAX)]
            keys = keys + [block(key_ref, at) for at in spare]
            scores = scores_of(query, jnp.concatenate(keys, axis=0))
            if spare:
                open_slots = jnp.where(first, jnp.clip(span - (b + 1), 0, len(spare)), 0)
                lane_at = lax.broadcasted_iota(jnp.int32, scores.shape, 1)
                scores = jnp.where(lane_at < known + open_slots * BLK, scores, MASKED)
            all_scores.append(scores)
            all_picks.append(picks + spare)
        all_values = [
            jnp.concatenate(glob_values + [block(value_ref, at) for at in picks], axis=0)
            for picks in all_picks
        ]
        parts, lses = softmax_parts(all_scores, all_values)
        stats = []
        for b in range(blocks):
            row = as_row(lses[b], (b * BLK) % LANES)
            if (b * BLK) % LANES:
                stats[-1] = stats[-1] + row
            else:
                stats.append(row)
        tile = stat_tile(stats)
        for b in range(blocks):
            out_ref[b * BLK : (b + 1) * BLK, :] = parts[b]
        out_ref[rows:, :] = tile


def near_rows(
    there, first, last, query_ref, key_ref, value_ref, halo_ref, came_refs, out_ref
):
    rows = query_ref.shape[0]
    halo = (WMAX - 1) * BLK
    starts = list(range(first, last, 2 * BLK))
    sizes = [min(2 * BLK, last - start) for start in starts]
    leads = [
        halo if start < halo else min(-(-(size + halo) // LANES) * LANES - size, start)
        for start, size in zip(starts, sizes)
    ]
    peers = peers_of(there, 0)
    together = 4 if len(starts) > 1 else 1
    for begin in range(0, len(peers), together):
        pair = range(begin, min(begin + together, len(peers)))
        all_lanes = [pl.ds(pl.multiple_of(peers[at] * HD, HD), HD) for at in pair]
        all_scores, all_values = [], []
        for at, lanes in zip(pair, all_lanes):
            width = came_refs[at][rows:, :].astype(jnp.float32)[:1]
            width = jnp.concatenate([width] * ((2 * BLK + halo) // LANES), axis=1)
            for start, size, lead in zip(starts, sizes, leads):
                query = query_ref[start : start + size, lanes]
                if start < lead:
                    keys = [halo_ref[0, start:, lanes], key_ref[: start + size, lanes]]
                    values = [halo_ref[1, start:, lanes], value_ref[: start + size, lanes]]
                    keys, values = jnp.concatenate(keys, axis=0), jnp.concatenate(values, axis=0)
                else:
                    keys = key_ref[start - lead : start + size, lanes]
                    values = value_ref[start - lead : start + size, lanes]
                scores = scores_of(query, keys)
                row_at = lax.broadcasted_iota(jnp.int32, scores.shape, 0)
                lane_at = lax.broadcasted_iota(jnp.int32, scores.shape, 1)
                slot = (lane_at // BLK - row_at // BLK - lead // BLK).astype(jnp.float32)
                allowed = (lane_at <= row_at + lead) & (slot + width[:, : size + lead] >= 1.0)
                if start < lead:
                    closed = jnp.where(lax.axis_index("seq") == 0, lead - start, 0)
                    allowed = allowed & (lane_at >= closed)
                all_scores.append(jnp.where(allowed, scores, MASKED))
                all_values.append(values)
        parts, lses = softmax_parts(all_scores, all_values)
        for index, lanes in enumerate(all_lanes):
            own = slice(index * len(starts), (index + 1) * len(starts))
            tile = stat_tile([as_row(lse, 0) for lse in lses[own]])
            for start, size, part in zip(starts, sizes, parts[own]):
                out_ref[start - first : start - first + size, lanes] = part
            out_ref[last - first : last - first + STAT_ROWS, lanes] = tile


def packed_at(index, first, wide):
    across = wide // HD
    row, lane = first + index // across * STAT_ROWS, index % across * HD
    return slice(row, row + STAT_ROWS), slice(lane, lane + HD)


def near_inner_kernel(there, query_ref, key_ref, value_ref, own_ref, *refs):
    rows, wide = query_ref.shape
    halo = (WMAX - 1) * BLK
    came_refs, out_ref = refs[:-1], refs[-1]
    near_rows(there, halo, rows, query_ref, key_ref, value_ref, None, came_refs, out_ref)
    for index in range(own_ref.shape[0] // STAT_ROWS):
        at = packed_at(index, rows - halo + STAT_ROWS, wide)
        out_ref[at] = own_ref[index * STAT_ROWS : (index + 1) * STAT_ROWS, :]


def near_edge_kernel(there, query_ref, key_ref, value_ref, odd_ref, even_ref, *refs):
    halo = (WMAX - 1) * BLK
    came_refs, out_ref, halo_ref = refs[: len(there[0])], refs[-2], refs[-1]
    halo_ref[...] = odd_ref[...] + even_ref[...]
    near_rows(there, 0, halo, query_ref, key_ref, value_ref, halo_ref, came_refs, out_ref)


def merge_kernel(there, edge_ref, inner_ref, *refs):
    far_refs, out_ref, own_ref = refs[:-2], refs[-2], refs[-1]
    rows, wide = out_ref.shape
    halo = (WMAX - 1) * BLK
    for index in range(own_ref.shape[0] // STAT_ROWS):
        at = packed_at(index, rows - halo + STAT_ROWS, wide)
        own_ref[index * STAT_ROWS : (index + 1) * STAT_ROWS, :] = inner_ref[at]
    count = stat_count(rows)
    for peer, far_ref in zip(peers_of(there, -1), (*far_refs, own_ref)):
        lanes = pl.ds(pl.multiple_of(peer * HD, HD), HD)
        far_stats = stat_rows_of(far_ref[rows:, :], count)
        near_stats = stat_rows_of(edge_ref[halo:, lanes], 1) + stat_rows_of(
            inner_ref[rows - halo : rows - halo + STAT_ROWS, lanes], count - 1
        )
        for group in range(count):
            start = group * LANES
            size = min(LANES, rows - start)
            share = 1.0 / (1.0 + jnp.exp2(near_stats[group] - far_stats[group]))
            row_at = lax.broadcasted_iota(jnp.int32, (size, LANES), 0)
            lane_at = lax.broadcasted_iota(jnp.int32, (size, LANES), 1)
            column = jnp.sum(
                jnp.where(row_at == lane_at, share, 0.0), axis=1, keepdims=True
            )
            far = far_ref[start : start + size, :].astype(jnp.float32)
            if start < halo:
                near = edge_ref[start : start + size, lanes].astype(jnp.float32)
            else:
                near = inner_ref[start - halo : start - halo + size, lanes].astype(jnp.float32)
            out_ref[start : start + size, lanes] = (
                far * column + near * (1.0 - column)
            ).astype(jnp.bfloat16)


def params(shard):
    return pltpu.CompilerParams(vmem_limit_bytes=VMEM_BASE + 14 * 2 * math.prod(shard.shape))


def per_device(
    queries, keys_new, values_new, keys_cache, values_cache, window, global_blocks, random_blocks
):
    section_count = lax.axis_size("section")
    seq_count = lax.axis_size("seq")
    rows, wide = queries.shape[1], queries.shape[2]
    halo = (WMAX - 1) * BLK
    heads = wide // HD
    bf16 = jnp.bfloat16
    half = max(seq_count // 2, 1)
    inner, outer = list(range(1, half)), list(range(seq_count - 1, half - 1, -1))
    there = [outer + inner + [0], inner + outer + [0]]

    chunk_shape = jax.ShapeDtypeStruct((rows + STAT_ROWS, HD), bf16)
    chunk_shape = jax.ShapeDtypeStruct((rows + STAT_ROWS, HD), bf16)
    sent = pl.pallas_call(
        functools.partial(split_kernel, there),
        out_shape=[chunk_shape] * seq_count,
        in_specs=[whole_smem, in_hbm],
        out_specs=[whole_vmem] * seq_count,
        scratch_shapes=[pltpu.SemaphoreType.DMA((seq_count,))],
        compiler_params=params(queries),
        cost_estimate=pl.CostEstimate(flops=0, bytes_accessed=5 * rows * wide, transcendentals=0),
        name="split",
    )(window[0], queries[0])

    def linked(shard, by, steps):
        pairs = [
            (
                s * seq_count + t,
                (s + by) % section_count * seq_count + (t ^ steps[s % 2]),
            )
            for s in range(section_count)
            for t in range(seq_count)
        ]
        return lax.ppermute(shard, ("section", "seq"), pairs)

    came = [linked(shard, 0, steps) for shard, steps in zip(sent[:-1], zip(*there))]
    came.append(sent[-1])
    tails = jnp.stack([keys_new[0, rows - halo :], values_new[0, rows - halo :]])

    def halo_from(parity, after):
        mine = tails if after is None else pl.pallas_call(
            halo_kernel,
            out_shape=jax.ShapeDtypeStruct(tails.shape, bf16),
            in_specs=[whole_vmem, anywhere],
            out_specs=whole_vmem,
            compiler_params=params(queries),
            name="halo",
        )(tails, after)
        pairs = [
            (s * seq_count + t, s * seq_count + t + 1)
            for s in range(parity, section_count, 2)
            for t in range(seq_count - 1)
        ]
        return lax.ppermute(mine, ("section", "seq"), pairs)

    halos = [halo_from(1, None), halo_from(0, came[0])]
    picks = random_blocks[0].reshape(-1)

    def far_call(chosen):
        count = len(chosen)
        return pl.pallas_call(
            functools.partial(far_kernel, there, chosen),
            out_shape=[chunk_shape] * count,
            in_specs=[whole_smem] * 3 + [whole_vmem] * (2 + count),
            out_specs=[whole_vmem] * count,
            compiler_params=params(queries),
            cost_estimate=pl.CostEstimate(
                flops=40 * count * rows * 320 * HD * 4,
                bytes_accessed=2 * 2 * keys_cache.shape[1] * HD + 4 * count * rows * HD,
                transcendentals=count * rows * 320,
            ),
            name="far",
        )(
            window[0],
            global_blocks[0],
            picks,
            keys_cache[0],
            values_cache[0],
            *[came[at] for at in chosen],
        )

    late = list(range(seq_count - 1 - seq_count // 4, seq_count - 1))
    early = [at for at in range(seq_count) if at not in late]
    far = dict(zip(early, far_call(early)))
    if late:
        far.update(zip(late, far_call(late)))
    far = [far[at] for at in range(seq_count)]
    handed = [linked(shard, 1, steps) for shard, steps in zip(far[:-1], zip(*there))]

    def near_call(kernel, name, near_part, out_rows, vmem_count, scratch, *operands):
        return pl.pallas_call(
            functools.partial(kernel, there),
            out_shape=jax.ShapeDtypeStruct((out_rows, wide), bf16),
            in_specs=[
                whole_vmem if index < 3 + vmem_count else anywhere
                for index in range(3 + len(operands))
            ],
            out_specs=whole_vmem,
            scratch_shapes=scratch,
            compiler_params=params(queries),
            cost_estimate=pl.CostEstimate(
                flops=40 * heads * near_part * 256 * HD * 4,
                bytes_accessed=9 * near_part * wide,
                transcendentals=heads * near_part * 256,
            ),
            name=name,
        )(queries[0], keys_new[0], values_new[0], *operands)

    packed_rows = -(-(rows + STAT_ROWS) // (STAT_ROWS * heads)) * STAT_ROWS
    inner_part = near_call(
        near_inner_kernel, "near_inner", rows - halo, rows - halo + STAT_ROWS + packed_rows,
        1 + seq_count, [], far[-1], *came,
    )
    edge_part = near_call(
        near_edge_kernel, "near_edge", halo, halo + STAT_ROWS,
        2 + seq_count, [pltpu.VMEM(tails.shape, bf16)], *halos, *came, *handed[:2],
    )
    handed_inner = linked(inner_part, 1, [0, 0])
    handed_edge = linked(edge_part, 1, [0, 0])

    merged = pl.pallas_call(
        functools.partial(merge_kernel, there),
        out_shape=jax.ShapeDtypeStruct((rows, wide), bf16),
        in_specs=[whole_vmem] * (1 + seq_count),
        out_specs=whole_vmem,
        scratch_shapes=[pltpu.VMEM(chunk_shape.shape, bf16)],
        compiler_params=params(queries),
        cost_estimate=pl.CostEstimate(flops=0, bytes_accessed=6 * rows * wide, transcendentals=0),
        name="merge",
    )(handed_edge, handed_inner, *handed)
    return merged[None]


def solution(mesh):
    placed = (
        P("section", "seq", None),
        P("section", "seq", None),
        P("section", "seq", None),
        P("section", None, "seq"),
        P("section", None, "seq"),
        P("section", "seq"),
        P("section", None),
        P("section", None, None),
    )
    return jax.shard_map(
        per_device, mesh=mesh, in_specs=placed, out_specs=P("section", "seq", None), check_vma=False
    )
```
